128 devices in a mesh: seq: 2 (over x_lo), ctx: 32 (over y, z, core), tp: 2 (over x_hi).
Axes of the slice: x: 4 (x_hi: 2, x_lo: 2; x = x_hi * 2 + x_lo), y: 4, z: 4, core: 2. Of those that a mesh axis runs over, the one named last changes fastest.
Arguments:
- inputs: bfloat16 [2, 8192, 896], P('seq', 'ctx'), may hold values from -6 to 6
- positions: int32 [2, 8192], P('seq', 'ctx'), may hold values from 0 to 8063, as said below
- query_key_value_weight: bfloat16 [896, 2, 576], P(('seq', 'ctx'), 'tp'), may hold values from -0.1875 to 0.1875
- query_key_value_bias: bfloat16 [2, 576], P('tp', ('seq', 'ctx')), may hold values from -3 to 3
- gain_attn: bfloat16 [896], P(('seq', 'ctx')), may hold values from 0.099609375 to 1.8984375
- output_weight: bfloat16 [2, 448, 896], P('tp', None, ('seq', 'ctx')), may hold values from -6 to 6
- gate_weight: bfloat16 [896, 4864], P(('seq', 'ctx'), 'tp'), may hold values from -0.1875 to 0.1875
- up_weight: bfloat16 [896, 4864], P(('seq', 'ctx'), 'tp'), may hold values from -0.1875 to 0.1875
- down_weight: bfloat16 [4864, 896], P('tp', ('seq', 'ctx')), may hold values from -0.078125 to 0.078125
- gain_ffn: bfloat16 [896], P(('seq', 'ctx')), may hold values from 0.099609375 to 1.8984375
- cotangent: bfloat16 [2, 8192, 896], P('seq', 'ctx'), may hold values from -6 to 6
Outputs:
- output: bfloat16 [2, 8192, 896], P('seq', 'ctx')
- grad_inputs: bfloat16 [2, 8192, 896], P('seq', 'ctx')
- grad_w_qkv: float32 [896, 2, 576], P(('seq', 'ctx'), 'tp')
- grad_b_qk: float32 [2, 512], P('tp', ('seq', 'ctx'))
- grad_b_v: float32 [2, 64], P('tp', ('seq', 'ctx'))
- grad_gain_attn: float32 [896], P(('seq', 'ctx'))
- grad_w_out: float32 [2, 448, 896], P('tp', None, ('seq', 'ctx'))
- grad_w_gate: float32 [896, 4864], P(('seq', 'ctx'), 'tp')
- grad_w_up: float32 [896, 4864], P(('seq', 'ctx'), 'tp')
- grad_w_down: float32 [4864, 896], P('tp', ('seq', 'ctx'))
- grad_gain_ffn: float32 [896], P(('seq', 'ctx'))
The draws below stay inside these ranges and needn't reach their ends.
Inputs may be any that keep to these rules, and one draw needn't show every extreme that they name: Each sequence is a pack of three documents: positions count 0, 1, 2, ... along a document and restart at 0 at its first token; the first document ends within the sequence's first 128 tokens, the third begins at token 128 and runs to the sequence's end.
All inputs are finite; a program needn't handle non-finite values.
Results may differ from the reference program's by a relative error of at most 0.035.
Values may be sent and summed in bfloat16 or wider, within the bound.
A program may use at most 128 MiB of HBM per device.

```python
import math
import jax
import jax.numpy as jnp
from jax import lax

D = 896
HEADS = 14
KVH = 2
HD = 64
FF = 4864
TOK_DEV = 256
GROUPQ = 448
GROUP = 576
LENGTH = 8192
SEQS = 2


def draw_positions(key, part):
    key = jax.random.fold_in(key, 7)
    first_cut = jax.random.randint(key, (SEQS, 1), 1, TOK_DEV // 2)
    second_cut = TOK_DEV // 2
    token_index = jnp.arange(LENGTH, dtype=jnp.int32)[None, :]
    doc_begin = jnp.where(token_index >= second_cut, second_cut, jnp.where(token_index >= first_cut, first_cut, 0))
    return (token_index - doc_begin).astype(jnp.int32)


def spiked(array, key, source, target, shards_of, factor):
    def block_of(dim):
        return (jnp.arange(array.shape[dim]) // (array.shape[dim] // shards_of)).reshape((-1,) + (1,) * (array.ndim - 1 - dim))

    first = jax.random.permutation(key, shards_of)[block_of(target)]
    other_side = (block_of(target) + shards_of // 2) % shards_of
    return jnp.where((block_of(source) == first) | (block_of(source) == other_side), factor * array, array)


def level_of(stream_key, shape, shards, least, high):
    loudness = 1.0
    for dim, blocks in shards:
        heights = jax.random.uniform(jax.random.fold_in(jax.random.fold_in(stream_key, 6), dim), (blocks,), jnp.float32, least / len(shards), high / len(shards))
        loudness = loudness * jnp.repeat(jnp.exp(heights), shape[dim] // blocks).reshape((-1,) + (1,) * (len(shape) - 1 - dim))
    return loudness


def normal_values(key, extent, spread, most, pieces=(), kind=jnp.bfloat16):
    drawn = spread * jax.random.normal(key, extent, jnp.float32)
    if pieces:
        drawn = drawn * level_of(key, extent, pieces, -0.22, 0.18)
    return jnp.clip(drawn, -most, most).astype(kind)


def gaussian_with(rng, shape, width, bound, shards, heavy, held_as=jnp.bfloat16):
    entries = width * jax.random.normal(rng, shape, jnp.float32)
    if shards:
        entries = entries * level_of(rng, shape, shards, -0.22, 0.18)
    return jnp.clip(spiked(entries, jax.random.fold_in(rng, 3), *heavy), -bound, bound).astype(held_as)


def setup_inputs(seed: int = 0) -> dict:
    arg_keys = jax.random.split(jax.random.key(seed), 12)
    return {
        "inputs": normal_values(arg_keys[0], (SEQS, LENGTH, D), 1.0, 6.0, ((0, 2), (1, 32))),
        "positions": draw_positions(jax.random.fold_in(arg_keys[11], 71), 0),
        "query_key_value_weight": normal_values(arg_keys[2], (D, KVH, GROUP), D ** -0.5, 0.1875, ((0, 64), (1, 2))),
        "query_key_value_bias": normal_values(arg_keys[3], (KVH, GROUP), 0.5, 3.0, ((0, 2), (1, 64))),
        "gain_attn": jnp.clip(1.0 + 0.18 * jax.random.normal(arg_keys[4], (D,), jnp.float32), 0.099609375, 1.8984375).astype(jnp.bfloat16),
        "output_weight": normal_values(arg_keys[5], (KVH, GROUPQ, D), ((LENGTH // 16) ** 0.5 * (HEADS * HD) ** -0.5), 6.0, ((0, 2), (2, 64))),
        "gate_weight": normal_values(arg_keys[6], (D, FF), D ** -0.5, 0.1875, ((0, 64), (1, 2))),
        "up_weight": normal_values(arg_keys[7], (D, FF), D ** -0.5, 0.1875, ((0, 64), (1, 2))),
        "down_weight": normal_values(arg_keys[8], (FF, D), FF ** -0.5, 0.078125, ((0, 2), (1, 64))),
        "gain_ffn": jnp.clip(1.0 + 0.18 * jax.random.normal(arg_keys[9], (D,), jnp.float32), 0.099609375, 1.8984375).astype(jnp.bfloat16),
        "cotangent": gaussian_with(arg_keys[10], (SEQS, LENGTH, D), 1.0, 6.0, ((0, 2), (1, 32)), (1, 2, 32, 2.75)),
    }


@jax.custom_vjp
def low(v):
    return lax.optimization_barrier(v.astype(jnp.bfloat16)).astype(jnp.float32)

@jax.custom_vjp
def reduced_precision_backward(v):
    return v

def low_keep(v):
    return (low(v), None)

def low_pass(kept, grad):
    return (grad,)

def back_keep(v):
    return (v, None)

def back_low(kept, grad):
    return (low(grad),)
low.defvjp(low_keep, low_pass)
reduced_precision_backward.defvjp(back_keep, back_low)
EPS_VALUE = 1e-06
THETA = 1000000.0
NEGATIVE = -1e+30
HIGH_PRECISION = lax.Precision.HIGHEST

def rope_tables(positions):
    exponents = jnp.arange(HD // 2, dtype=jnp.float32) * (2.0 / HD)
    freqs = THETA ** (-exponents)
    angles = positions.astype(jnp.float32)[..., None] * freqs
    angles = jnp.concatenate([angles, angles], -1)
    return (jnp.cos(angles), jnp.sin(angles))

def rotate(values, cosine, sine_table):
    half_width = values.shape[-1] // 2
    turned = jnp.concatenate([-values[..., half_width:], values[..., :half_width]], -1)
    return values * cosine + turned * sine_table

def rms_norm(values, gain):
    return values * lax.rsqrt(lax.optimization_barrier(jnp.mean(values * values, -1, keepdims=True)) + EPS_VALUE) * gain

def attend_sequence(queries, keys_all, values_all, positions_row):
    length = queries.shape[0]
    block_rows = math.gcd(length, 512)
    blocks = length // block_rows
    row_index = jnp.arange(length, dtype=jnp.int32)
    doc_start = row_index - positions_row.astype(jnp.int32)
    scale = HD ** (-0.5)

    def one_block(items):
        query_block, start_block, index_block = items
        scores = reduced_precision_backward(scale * jnp.einsum('tghd,kgd->ghtk', query_block, keys_all, precision=HIGH_PRECISION))
        visible = (row_index[None, :] >= start_block[:, None]) & (row_index[None, :] <= index_block[:, None])
        scores = jnp.where(visible, scores, NEGATIVE)
        attn_probs = low(jax.nn.softmax(scores, axis=-1))
        return jnp.einsum('ghtk,kgd->tghd', attn_probs, values_all, precision=HIGH_PRECISION)
    outputs = lax.map(jax.checkpoint(one_block), (queries.reshape(blocks, block_rows, KVH, HEADS // KVH, HD), doc_start.reshape(blocks, block_rows), row_index.reshape(blocks, block_rows)))
    return outputs.reshape(length, KVH, HEADS // KVH, HD)

def layer_forward(inputs, positions, query_key_value_weight, query_key_value_bias, gain_attn, output_weight, gate_weight, up_weight, down_weight, gain_ffn):
    seqs = inputs.shape[0]
    length = inputs.shape[1]
    group_q = HEADS // KVH * HD
    normalized_input = low(rms_norm(inputs, gain_attn))
    projected_attention = reduced_precision_backward(jnp.einsum('vfy,yir->vfir', normalized_input, query_key_value_weight, precision=HIGH_PRECISION) + query_key_value_bias)
    cosine, sine_table = rope_tables(positions)
    queries = projected_attention[..., :group_q].reshape(seqs, length, KVH, HEADS // KVH, HD)
    queries = low(rotate(queries, cosine[:, :, None, None, :], sine_table[:, :, None, None, :]))
    keys_all = low(rotate(projected_attention[..., group_q:group_q + HD], cosine[:, :, None, :], sine_table[:, :, None, :]))
    values_all = low(projected_attention[..., group_q + HD:])
    attention_output = jnp.stack([attend_sequence(queries[seq_index], keys_all[seq_index], values_all[seq_index], positions[seq_index]) for seq_index in range(seqs)])
    attention_output = reduced_precision_backward(low(attention_output)).reshape(seqs, length, KVH, group_q)
    residual_branch = reduced_precision_backward(jnp.einsum('uqyo,yot->uqt', attention_output, output_weight, precision=HIGH_PRECISION))
    middle_state = inputs + residual_branch
    normalized_feedforward_input = low(rms_norm(middle_state, gain_ffn))
    gate_activation = reduced_precision_backward(jnp.einsum('grj,je->gre', normalized_feedforward_input, gate_weight, precision=HIGH_PRECISION))
    up_activation = reduced_precision_backward(jnp.einsum('grj,je->gre', normalized_feedforward_input, up_weight, precision=HIGH_PRECISION))
    hidden_state = low(jax.nn.silu(gate_activation) * up_activation)
    return middle_state + jnp.einsum('eoa,ak->eok', hidden_state, down_weight, precision=HIGH_PRECISION)

def reference(inputs, positions, query_key_value_weight, query_key_value_bias, gain_attn, output_weight, gate_weight, up_weight, down_weight, gain_ffn, cotangent):
    floats = [item.astype(jnp.float32) for item in (inputs, query_key_value_weight, query_key_value_bias, gain_attn, output_weight, gate_weight, up_weight, down_weight, gain_ffn)]

    def closed(inputs_f, qkv_f, bias_f, gain_one, out_f, gate_f, up_f, down_f, gain_two):
        return layer_forward(inputs_f, positions, qkv_f, bias_f, gain_one, out_f, gate_f, up_f, down_f, gain_two)
    result, pull = jax.vjp(closed, floats[0], floats[1], floats[2], floats[3], floats[4], floats[5], floats[6], floats[7], floats[8])
    grads = pull(cotangent.astype(jnp.float32))
    split_at = GROUPQ + HD
    return (result.astype(jnp.bfloat16), grads[0].astype(jnp.bfloat16), grads[1], grads[2][:, :split_at], grads[2][:, split_at:], grads[3], grads[4], grads[5], grads[6], grads[7], grads[8])
```

```python
import jax
import jax.numpy as jnp
import numpy as np
from jax import lax
from jax.experimental import pallas as pl
from jax.experimental.pallas import tpu as pltpu
from jax.sharding import PartitionSpec as P

MESH_ID = pl.DeviceIdType.MESH
ANY = pl.ANY
VMEM = pltpu.VMEM


class Place:
    def __init__(self):
        self.seq = lax.axis_index("seq")
        ctx = lax.axis_index("ctx")
        self.ctx = ctx
        self.tp = lax.axis_index("tp")
        self.core = ctx % 2
        core = self.core
        y, z = ctx // 8, (ctx // 2) % 4
        self.a = y * (1 - core) + z * core
        self.b = z * (1 - core) + y * core
        self.stride_a = 8 - 6 * core
        self.stride_b = 2 + 6 * core
        self.a_next = self.peer(1, 0)
        self.a_prev = self.peer(3, 0)
        self.b_next = self.peer(0, 1)
        self.b_prev = self.peer(0, 3)
        self.other_core = {"ctx": ctx + 1 - 2 * core}
        self.other_seq = {"seq": 1 - self.seq}
        self.mirror = {"ctx": 31 - ctx}
        self.other_tp = {"tp": 1 - self.tp}

    def peer(self, da, db):
        a, b = (self.a + da) % 4, (self.b + db) % 4
        return {"ctx": a * self.stride_a + b * self.stride_b + self.core}


def greet(peers):
    barrier = pltpu.get_barrier_semaphore()
    for peer in peers:
        pl.semaphore_signal(barrier, inc=1, device_id=peer, device_id_type=MESH_ID)
    pl.semaphore_wait(barrier, len(peers))


def remote(src, dst, send, recv, index, peer):
    return pltpu.make_async_remote_copy(
        src_ref=src,
        dst_ref=dst,
        send_sem=send.at[index],
        recv_sem=recv.at[index],
        device_id=peer,
        device_id_type=MESH_ID,
    )


GATHER_SEMS = 13


class Gather:
    def __init__(self, place, own, full, send, recv, local):
        self.p, self.own, self.full = place, own, full
        self.send, self.recv, self.local = send, recv, local
        self.pair = full.shape[3] == 2
        self.started = []

    def go(self, src, dst, index, peer):
        copy = remote(src, dst, self.send, self.recv, index, peer)
        copy.start()
        self.started.append(copy)

    def got(self, ref, index):
        remote(ref, ref, self.send, self.recv, index, self.p.a_next).wait_recv()

    def half(self, b, a, which):
        ref = self.full.at[self.p.core, b, a]
        if self.pair:
            return ref.at[which]
        rows = self.full.shape[4] // 2
        return ref.at[0, pl.ds(which * rows, rows)]

    def begin(self):
        p = self.p
        slot = self.full.at[p.core, p.b, p.a, p.seq if self.pair else 0]
        self.mine = pltpu.make_async_copy(self.own, slot, self.local)
        self.mine.start()
        if self.pair:
            self.go(self.own, slot, 0, p.other_seq)

    def first(self):
        p = self.p
        self.mine.wait()
        if self.pair:
            self.got(self.full.at[p.core, p.b, p.a, 1 - p.seq], 0)
        block = self.full.at[p.core, p.b, p.a]
        self.go(block, block, 1, p.a_next)
        self.go(block, block, 2, p.a_prev)

    def second(self):
        p = self.p
        down, up = (p.a + 3) % 4, (p.a + 1) % 4
        self.got(self.full.at[p.core, p.b, down], 1)
        half = self.half(p.b, down, 0)
        self.go(half, half, 3, p.a_next)
        self.got(self.full.at[p.core, p.b, up], 2)
        half = self.half(p.b, up, 1)
        self.go(half, half, 4, p.a_prev)

    def third(self):
        p = self.p
        far = (p.a + 2) % 4
        self.got(self.half(p.b, far, 0), 3)
        self.got(self.half(p.b, far, 1), 4)
        block = self.full.at[p.core, p.b]
        self.go(block, block, 5, p.b_next)
        self.go(block, block, 6, p.b_prev)
        self.go(block, block, 9, p.other_core)

    def fourth(self):
        p = self.p
        down, up = (p.b + 3) % 4, (p.b + 1) % 4
        block = self.full.at[p.core, down]
        self.got(block, 5)
        half = self.full.at[p.core, down, pl.ds(0, 2)]
        self.go(half, half, 7, p.b_next)
        self.go(block, block, 10, p.other_core)
        block = self.full.at[p.core, up]
        self.got(block, 6)
        half = self.full.at[p.core, up, pl.ds(2, 2)]
        self.go(half, half, 8, p.b_prev)
        self.go(block, block, 11, p.other_core)

    def fifth(self):
        p = self.p
        far = (p.b + 2) % 4
        self.got(self.full.at[p.core, far, pl.ds(0, 2)], 7)
        self.got(self.full.at[p.core, far, pl.ds(2, 2)], 8)
        block = self.full.at[p.core, far]
        self.go(block, block, 12, p.other_core)

    def finish(self):
        p = self.p
        for index, step in ((9, 0), (10, 3), (11, 1), (12, 2)):
            self.got(self.full.at[1 - p.core, (p.a + step) % 4], index)
        for copy in self.started:
            copy.wait_send()

    def peers(self):
        p = self.p
        found = [p.a_next, p.a_prev, p.b_next, p.b_prev, p.other_core]
        return found + ([p.other_seq] if self.pair else [])


def add_into(target, extra, count):
    def body(k, carry):
        total = target[k].astype(jnp.float32) + extra[k].astype(jnp.float32)
        target[k] = total.astype(target.dtype)
        return carry

    lax.fori_loop(0, count, body, 0)


SCATTER_SEMS = 13


class Scatter:
    @staticmethod
    def scratch(seqs, rows, width):
        bf16 = jnp.bfloat16
        half = (1, rows, width) if seqs == 2 else (1, rows // 2, width)
        return [
            VMEM((4, 4, seqs, rows, width), bf16),
            VMEM((2, 2, seqs, rows, width), bf16),
            VMEM((2, 4, seqs, rows, width), bf16),
            VMEM((2,) + half, bf16),
            VMEM((2, seqs, rows, width), bf16),
            VMEM((1, rows, width), bf16),
            pltpu.SemaphoreType.DMA((SCATTER_SEMS,)),
            pltpu.SemaphoreType.DMA((SCATTER_SEMS,)),
        ]

    def __init__(self, place, part, scratch):
        self.p, self.part = place, part
        self.sums, self.far_b, self.near_b, self.far_a, self.near_a, self.across, self.send, self.recv = scratch
        self.seqs, self.rows = part.shape[3], part.shape[4]
        self.started = []

    go = Gather.go
    got = Gather.got

    def half(self, b, a, which):
        ref = self.sums.at[b, a]
        if self.seqs == 2:
            return ref.at[pl.ds(which, 1)]
        rows = self.rows // 2
        return ref.at[:, pl.ds(which * rows, rows)]

    def begin(self):
        p = self.p
        for step in (2, 1, 3, 0):
            slot = (p.a + step) % 4
            self.go(self.part.at[1 - p.core, slot], self.sums.at[slot], step, p.other_core)

    def add_core(self, step):
        p = self.p
        slot = (p.b + step) % 4
        self.got(self.sums.at[slot], step)
        for a in range(4):
            add_into(self.sums.at[slot, a], self.part.at[p.core, slot, a], self.seqs)

    def first(self):
        p = self.p
        self.add_core(2)
        far = (p.b + 2) % 4
        self.go(self.sums.at[far, pl.ds(0, 2)], self.far_b.at[0], 4, p.b_next)
        self.go(self.sums.at[far, pl.ds(2, 2)], self.far_b.at[1], 5, p.b_prev)

    def second(self):
        p = self.p
        up, down = (p.b + 1) % 4, (p.b + 3) % 4
        self.add_core(1)
        self.add_core(3)
        self.got(self.far_b.at[0], 4)
        for a in range(2):
            add_into(self.sums.at[up, a], self.far_b.at[0, a], self.seqs)
        self.go(self.sums.at[up], self.near_b.at[0], 6, p.b_next)
        self.got(self.far_b.at[1], 5)
        for a in range(2):
            add_into(self.sums.at[down, a + 2], self.far_b.at[1, a], self.seqs)
        self.go(self.sums.at[down], self.near_b.at[1], 7, p.b_prev)
        self.add_core(0)

    def third(self):
        p = self.p
        for side in range(2):
            self.got(self.near_b.at[side], 6 + side)
            for a in range(4):
                add_into(self.sums.at[p.b, a], self.near_b.at[side, a], self.seqs)
        far = (p.a + 2) % 4
        self.go(self.half(p.b, far, 0), self.far_a.at[0], 8, p.a_next)
        self.go(self.half(p.b, far, 1), self.far_a.at[1], 9, p.a_prev)

    def fourth(self):
        p = self.p
        up, down = (p.a + 1) % 4, (p.a + 3) % 4
        self.got(self.far_a.at[0], 8)
        add_into(self.half(p.b, up, 0), self.far_a.at[0], 1)
        self.go(self.sums.at[p.b, up], self.near_a.at[0], 10, p.a_next)
        self.got(self.far_a.at[1], 9)
        add_into(self.half(p.b, down, 1), self.far_a.at[1], 1)
        self.go(self.sums.at[p.b, down], self.near_a.at[1], 11, p.a_prev)

    def fifth(self):
        p = self.p
        for side in range(2):
            self.got(self.near_a.at[side], 10 + side)
            add_into(self.sums.at[p.b, p.a], self.near_a.at[side], self.seqs)
        if self.seqs == 2:
            self.go(self.sums.at[p.b, p.a, pl.ds(1 - p.seq, 1)], self.across, 12, p.other_seq)

    def finish(self, out):
        p = self.p
        if self.seqs == 2:
            self.got(self.across, 12)
            out[...] = self.sums[p.b, p.a, p.seq].astype(jnp.float32) + self.across[0].astype(jnp.float32)
        else:
            out[...] = self.sums[p.b, p.a, 0].astype(jnp.float32)
        for copy in self.started:
            copy.wait_send()

    def peers(self):
        p = self.p
        found = [p.a_next, p.a_prev, p.b_next, p.b_prev, p.other_core]
        return found + ([p.other_seq] if self.seqs == 2 else [])


def gather_blocks(blocks, seqs, collective_id):
    def kernel(*refs):
        n = len(blocks)
        place = Place()
        gathers = [
            Gather(place, refs[k], refs[n + k], refs[2 * n + 3 * k], refs[2 * n + 3 * k + 1], refs[2 * n + 3 * k + 2])
            for k in range(n)
        ]
        greet(gathers[0].peers())
        for stage in ("begin", "first", "second", "third", "fourth", "fifth", "finish"):
            for gather in gathers:
                getattr(gather, stage)()

    scratch = []
    for block in blocks:
        scratch += [pltpu.SemaphoreType.DMA((GATHER_SEMS,))] * 2 + [pltpu.SemaphoreType.DMA]
    return pl.pallas_call(
        kernel,
        out_shape=[jax.ShapeDtypeStruct((2, 4, 4, seqs) + block.shape, block.dtype) for block in blocks],
        in_specs=[pl.BlockSpec(memory_space=ANY)] * len(blocks),
        out_specs=[pl.BlockSpec(memory_space=ANY)] * len(blocks),
        scratch_shapes=scratch,
        compiler_params=pltpu.CompilerParams(
            collective_id=collective_id, has_side_effects=True, vmem_limit_bytes=60 << 20
        ),
    )(*blocks)


def scatter_sum(part, collective_id):
    seqs, rows, width = part.shape[3:]

    def kernel(part_ref, out_ref, *scratch):
        scatter = Scatter(Place(), part_ref, scratch)
        greet(scatter.peers())
        for stage in ("begin", "first", "second", "third", "fourth", "fifth"):
            getattr(scatter, stage)()
        scatter.finish(out_ref)

    return pl.pallas_call(
        kernel,
        out_shape=jax.ShapeDtypeStruct((rows, width), jnp.float32),
        in_specs=[pl.BlockSpec(memory_space=VMEM)],
        out_specs=pl.BlockSpec(memory_space=VMEM),
        scratch_shapes=Scatter.scratch(seqs, rows, width),
        compiler_params=pltpu.CompilerParams(
            collective_id=collective_id, has_side_effects=True, vmem_limit_bytes=60 << 20
        ),
    )(part)


def swap(arrays, which, collective_id):
    n = len(arrays)

    def kernel(*refs):
        place = Place()
        peer = getattr(place, which)
        greet([peer])
        copies = [remote(refs[k], refs[n + k], refs[2 * n], refs[2 * n + 1], k, peer) for k in range(n)]
        for copy in copies:
            copy.start()
        for copy in copies:
            copy.wait()

    return pl.pallas_call(
        kernel,
        out_shape=[jax.ShapeDtypeStruct(array.shape, array.dtype) for array in arrays],
        in_specs=[pl.BlockSpec(memory_space=ANY)] * n,
        out_specs=[pl.BlockSpec(memory_space=ANY)] * n,
        scratch_shapes=[pltpu.SemaphoreType.DMA((n,))] * 2,
        compiler_params=pltpu.CompilerParams(
            collective_id=collective_id, has_side_effects=True, vmem_limit_bytes=60 << 20
        ),
    )(*arrays)


NEGATIVE = -1e30
HD = 64
ROWS = 896
F32, BF16 = jnp.float32, jnp.bfloat16


def mm(left, right):
    return jnp.dot(left, right, preferred_element_type=F32)


def mm_nt(left, right):
    return lax.dot_general(left, right, (((1,), (1,)), ((), ())), preferred_element_type=F32)


def slot_of(block):
    core, y, z = block % 2, block // 8, (block // 2) % 4
    a = y * (1 - core) + z * core
    b = z * (1 - core) + y * core
    return core, b, a


def for_blocks(count, step):
    step(0, True)

    def body(block, carry):
        step(block, False)
        return carry

    lax.fori_loop(1, count - 1, body, 0)

    @pl.when(count > 1)
    def _():
        step(count - 1, True)


def segment(ctx, index):
    if index == 0:
        return ctx + 1, ctx * 256
    return 32 - ctx, (31 - ctx) * 256 + 128


def visible_of(block, first_row, doc_start, lanes):
    key = lax.broadcasted_iota(jnp.int32, (256, lanes.size), 0) + block * 256
    row = (lax.broadcasted_iota(jnp.int32, (256, lanes.size), 1) + lanes.start) % 128 + first_row
    return (key <= row) & (key >= doc_start)


def attend(ctx, kv_ref, q_ref, doc_ref, out_ref, lse_ref, m_ref, l_ref, acc_ref, chunk):
    for index in range(2):
        count, first_row = segment(ctx, index)
        m_ref[...] = jnp.full(m_ref.shape, NEGATIVE, F32)
        l_ref[...] = jnp.zeros(l_ref.shape, F32)
        acc_ref[...] = jnp.zeros(acc_ref.shape, F32)

        def step(block, masked):
            core, b, a = slot_of(block)
            kv = kv_ref[core, b, a, 0]
            keys, values_t = kv[:, :HD], kv[:, HD:].T
            for start in range(0, ROWS, chunk):
                lanes = pl.ds(start, min(chunk, ROWS - start))
                scores = mm(keys, q_ref[index, :, lanes])
                if masked:
                    doc = doc_ref[:, lanes] if index == 0 else 128
                    scores = jnp.where(visible_of(block, first_row, doc, lanes), scores, NEGATIVE)
                old = m_ref[:, lanes]
                new = jnp.maximum(old, jnp.max(scores, 0, keepdims=True))
                probs = jnp.exp(scores - new)
                keep = jnp.exp(old - new)
                m_ref[:, lanes] = new
                l_ref[:, lanes] = l_ref[:, lanes] * keep + jnp.sum(probs, 0, keepdims=True)
                acc_ref[:, lanes] = acc_ref[:, lanes] * keep + mm(values_t, probs.astype(BF16))

        for_blocks(count, step)
        out_ref[index] = acc_ref[...] / l_ref[...]
        lse_ref[index] = m_ref[...] + jnp.log(l_ref[...])


def attend_back(ctx, kv_ref, q_ref, doc_ref, do_ref, lse_ref, delta_ref, dq_ref, dkv_ref, chunk):
    dq_ref[...] = jnp.zeros(dq_ref.shape, F32)

    def clear(block, carry):
        core, b, a = slot_of(block)
        dkv_ref[core, b, a, 0] = jnp.zeros((256, 128), F32)
        return carry

    lax.fori_loop(0, 32, clear, 0)
    for index in range(2):
        count, first_row = segment(ctx, index)

        def step(block, masked):
            core, b, a = slot_of(block)
            kv = kv_ref[core, b, a, 0]
            keys, values = kv[:, :HD], kv[:, HD:]
            keys_t = keys.T
            dk = dv = jnp.zeros((256, HD), F32)
            for start in range(0, ROWS, chunk):
                lanes = pl.ds(start, min(chunk, ROWS - start))
                q, do = q_ref[index, :, lanes], do_ref[index, :, lanes]
                scores = mm(keys, q)
                if masked:
                    doc = doc_ref[:, lanes] if index == 0 else 128
                    scores = jnp.where(visible_of(block, first_row, doc, lanes), scores, NEGATIVE)
                probs = jnp.exp(scores - lse_ref[index, :, lanes])
                dscores = (probs * (mm(values, do) - delta_ref[index, :, lanes])).astype(BF16)
                dq_ref[index, :, lanes] += mm(keys_t, dscores)
                dk += mm_nt(dscores, q)
                dv += mm_nt(probs.astype(BF16), do)
            dkv_ref[core, b, a, 0] += jnp.concatenate([dk, dv], 1)

        for_blocks(count, step)


D, DPAD, FF_HERE, GROUP, GROUP_Q = 896, 1024, 2432, 576, 448
ATTN_W = GROUP + GROUP_Q + 128
EPS_VALUE = 1e-06
THETA = 1000000.0


def slot_columns():
    index = np.arange(64)
    seq, y, z, core = index // 32, (index // 8) % 4, (index // 2) % 4, index % 2
    a, b = np.where(core == 0, y, z), np.where(core == 0, z, y)
    slot = ((core * 4 + b) * 4 + a) * 2 + seq
    columns = np.full((64, 16), -1)
    columns[slot, :14] = index[:, None] * 14 + np.arange(14)
    return columns.reshape(-1)


def mm_tn(left, right):
    return lax.dot_general(left, right, (((0,), (0,)), ((), ())), preferred_element_type=F32)


def rope_tables(positions):
    exponents = jnp.arange(HD // 2, dtype=F32) * (2.0 / HD)
    freqs = THETA ** (-exponents)
    angles = freqs[:, None] * positions.astype(F32)[None, :]
    angles = jnp.concatenate([angles, angles], 0)
    return jnp.cos(angles), jnp.sin(angles)


def rotate(values, cosine, sine):
    turned = jnp.concatenate([-values[..., 32:, :], values[..., :32, :]], -2)
    return values * cosine + turned * sine


def rotate_back(grads, cosine, sine):
    sined = grads * sine
    return grads * cosine + jnp.concatenate([sined[..., 32:, :], -sined[..., :32, :]], -2)


def norm_back(values, inv_rms, gain, grad_normed):
    scaled = grad_normed * gain
    grad_gain = jnp.sum(grad_normed * values * inv_rms, 1, keepdims=True)
    mean = jnp.sum(scaled * values, 0, keepdims=True) * (1.0 / D)
    return grad_gain, inv_rms * scaled - values * inv_rms**3 * mean


def inv_rms(values):
    return lax.rsqrt(jnp.sum(values * values, 0, keepdims=True) * (1.0 / D) + EPS_VALUE)


def heads_to_lanes(values):
    return values.reshape(7, HD, 128).transpose(1, 0, 2).reshape(HD, ROWS)


def lanes_to_heads(values):
    return values.reshape(HD, 7, 128).transpose(1, 0, 2).reshape(GROUP_Q, 128)


def local_call(kernel, out_shape, inputs, scratch=()):
    return pl.pallas_call(
        kernel,
        out_shape=out_shape,
        in_specs=[pl.BlockSpec(memory_space=VMEM)] * len(inputs),
        out_specs=[pl.BlockSpec(memory_space=VMEM)] * len(out_shape),
        scratch_shapes=list(scratch),
        compiler_params=pltpu.CompilerParams(vmem_limit_bytes=60 << 20),
    )(*inputs)


def shards(
    inputs,
    positions,
    query_key_value_weight,
    query_key_value_bias,
    gain_attn,
    output_weight,
    gate_weight,
    up_weight,
    down_weight,
    gain_ffn,
    cotangent,
):
    me = lax.axis_index("seq") * 32 + lax.axis_index("ctx")
    columns = slot_columns()
    select = jnp.asarray(columns[:, None] == np.arange(D)[None, :], BF16)
    is_bias_row = jnp.asarray((np.arange(DPAD) % 16 == 14)[:, None])

    bias_row = lax.dynamic_update_slice(jnp.zeros((1, GROUP), BF16), query_key_value_bias, (0, 9 * me))
    gains = jnp.stack([gain_attn, gain_ffn], 1)
    attn_row = jnp.concatenate(
        [
            jnp.concatenate([query_key_value_weight[:, 0], bias_row, jnp.zeros((1, GROUP), BF16)], 0),
            jnp.pad(output_weight[0].T, ((0, 2), (0, 0))),
            jnp.pad(gains, ((0, 2), (0, 126))),
        ],
        1,
    )
    ffn_row = jnp.pad(jnp.concatenate([gate_weight, up_weight, down_weight.T], 1), ((0, 2), (0, 0)))
    attn_full, ffn_full = gather_blocks([attn_row, ffn_row], 2, 0)
    attn_full, ffn_full = attn_full.reshape(DPAD, ATTN_W), ffn_full.reshape(DPAD, 3 * FF_HERE)
    w_qkv, w_out = attn_full[:, :GROUP], attn_full[:, GROUP : GROUP + GROUP_Q]
    gain_one = attn_full[:, GROUP + GROUP_Q : GROUP + GROUP_Q + 1].astype(F32)
    gain_two = attn_full[:, GROUP + GROUP_Q + 1 : GROUP + GROUP_Q + 2].astype(F32)
    w_gate, w_up, w_down = (ffn_full[:, k * FF_HERE : (k + 1) * FF_HERE] for k in range(3))

    cosine, sine = rope_tables(positions[0])
    x = mm_nt(select, inputs[0])
    ct_low = mm_nt(select, cotangent[0]).astype(BF16)
    inv_one = inv_rms(x)
    normed = jnp.where(is_bias_row, 1.0, x * inv_one * gain_one).astype(BF16)
    mixed = mm_tn(w_qkv, normed)
    queries = rotate(mixed[:GROUP_Q].reshape(7, HD, 256), cosine, sine).astype(BF16) * BF16(0.125)
    queries = queries.reshape(GROUP_Q, 256)
    keys = rotate(mixed[GROUP_Q : GROUP_Q + HD], cosine, sine).astype(BF16)
    kv = jnp.concatenate([keys, mixed[GROUP_Q + HD :].astype(BF16)], 0).T
    (kv_full,) = gather_blocks([kv], 1, 1)
    (q_far,) = swap([heads_to_lanes(queries[:, 128:])], "mirror", 2)
    q_both = jnp.stack([heads_to_lanes(queries[:, :128]), q_far])
    row = lax.axis_index("ctx") * 256 + jnp.arange(128, dtype=jnp.int32)
    doc_start = jnp.tile((row - positions[0, :128])[None], (1, 7))

    def attend_kernel(*refs):
        attend(lax.axis_index("ctx"), *refs, ROWS)

    attended, lse = local_call(
        attend_kernel,
        [jax.ShapeDtypeStruct((2, HD, ROWS), F32), jax.ShapeDtypeStruct((2, 1, ROWS), F32)],
        [kv_full, q_both, doc_start],
        [VMEM((1, ROWS), F32), VMEM((1, ROWS), F32), VMEM((HD, ROWS), F32)],
    )
    attended_low = attended.astype(BF16)
    (att_far,) = swap([attended_low[1]], "mirror", 3)
    att = jnp.concatenate([lanes_to_heads(attended_low[0]), lanes_to_heads(att_far)], 1)
    branch = mm(w_out, att).astype(BF16)
    (branch_other,) = swap([branch], "other_tp", 4)
    middle = x + (branch.astype(F32) + branch_other.astype(F32))
    inv_two = inv_rms(middle)
    normed_ffn = (middle * inv_two * gain_two).astype(BF16)
    gate, up = mm_tn(normed_ffn, w_gate), mm_tn(normed_ffn, w_up)
    sigmoid = jax.nn.sigmoid(gate)
    hidden = (gate * sigmoid * up).astype(BF16)
    out_part = mm_nt(w_down, hidden).astype(BF16)
    grad_hidden = mm_tn(ct_low, w_down)
    grad_down = mm(ct_low, hidden)
    grad_up_act = (grad_hidden * (gate * sigmoid)).astype(BF16)
    grad_gate_act = (grad_hidden * up * sigmoid * (1.0 + gate * (1.0 - sigmoid))).astype(BF16)
    grad_gate, grad_up = mm(normed_ffn, grad_gate_act), mm(normed_ffn, grad_up_act)
    grad_n = (mm_nt(w_gate, grad_gate_act) + mm_nt(w_up, grad_up_act)).astype(BF16)
    grad_n_other, out_other = swap([grad_n, out_part], "other_tp", 5)
    output = middle + (out_part.astype(F32) + out_other.astype(F32))
    grad_gain_two, grad_norm = norm_back(middle, inv_two, gain_two, grad_n.astype(F32) + grad_n_other.astype(F32))
    grad_middle = ct_low.astype(F32) + grad_norm
    grad_branch = grad_middle.astype(BF16)
    grad_out_w = mm_nt(grad_branch, att)
    grad_att = mm_tn(w_out, grad_branch).astype(BF16)
    (do_far,) = swap([heads_to_lanes(grad_att[:, 128:])], "mirror", 6)
    do_both = jnp.stack([heads_to_lanes(grad_att[:, :128]), do_far])
    delta = jnp.sum(do_both.astype(F32) * attended, 1, keepdims=True)

    def back_kernel(*refs):
        attend_back(lax.axis_index("ctx"), *refs, ROWS)

    grad_q, grad_kv = local_call(
        back_kernel,
        [jax.ShapeDtypeStruct((2, HD, ROWS), F32), jax.ShapeDtypeStruct((2, 4, 4, 1, 256, 128), F32)],
        [kv_full, q_both, doc_start, do_both, lse, delta],
    )
    (dq_far,) = swap([grad_q[1].astype(BF16)], "mirror", 7)
    grad_kv = scatter_sum(grad_kv.astype(BF16), 8).T
    grad_q = jnp.concatenate([lanes_to_heads(grad_q[0]), lanes_to_heads(dq_far).astype(F32)], 1) * 0.125
    grad_q = rotate_back(grad_q.reshape(7, HD, 256), cosine, sine).reshape(GROUP_Q, 256)
    grad_k = rotate_back(grad_kv[:HD], cosine, sine)
    grad_mixed = jnp.concatenate([grad_q, grad_k, grad_kv[HD:]], 0).astype(BF16)
    grad_qkv = mm_nt(normed, grad_mixed)
    grad_normed = mm(w_qkv, grad_mixed).astype(BF16)
    (grad_normed_other,) = swap([grad_normed], "other_tp", 9)
    grad_gain_one, grad_norm = norm_back(
        x, inv_one, gain_one, grad_normed.astype(F32) + grad_normed_other.astype(F32)
    )
    grad_inputs = grad_middle + grad_norm

    part = jnp.concatenate(
        [
            grad_qkv.astype(BF16),
            grad_out_w.astype(BF16),
            jnp.pad(jnp.concatenate([grad_gain_one, grad_gain_two], 1), ((0, 0), (0, 126))).astype(BF16),
            grad_gate.astype(BF16),
            grad_up.astype(BF16),
            grad_down.astype(BF16),
        ],
        1,
    )
    mine = scatter_sum(part.reshape(2, 4, 4, 2, 16, ATTN_W + 3 * FF_HERE), 10)
    ffn = ATTN_W
    return (
        mm_tn(output.astype(BF16), select).astype(BF16)[None],
        mm_tn(grad_inputs.astype(BF16), select).astype(BF16)[None],
        mine[:14, None, :GROUP],
        lax.dynamic_slice(mine, (14, 8 * me), (1, 8)),
        lax.dynamic_slice(mine, (14, 512 + me), (1, 1)),
        mine[:14, GROUP + GROUP_Q],
        mine[:14, GROUP : GROUP + GROUP_Q].T[None],
        mine[:14, ffn : ffn + FF_HERE],
        mine[:14, ffn + FF_HERE : ffn + 2 * FF_HERE],
        mine[:14, ffn + 2 * FF_HERE :].T,
        mine[:14, GROUP + GROUP_Q + 1],
    )


def solution(mesh):
    both = ("seq", "ctx")
    return jax.shard_map(
        shards,
        mesh=mesh,
        in_specs=(
            P("seq", "ctx", None),
            P("seq", "ctx"),
            P(both, "tp", None),
            P("tp", both),
            P(both),
            P("tp", None, both),
            P(both, "tp"),
            P(both, "tp"),
            P("tp", both),
            P(both),
            P("seq", "ctx", None),
        ),
        out_specs=(
            P("seq", "ctx", None),
            P("seq", "ctx", None),
            P(both, "tp", None),
            P("tp", both),
            P("tp", both),
            P(both),
            P("tp", None, both),
            P(both, "tp"),
            P(both, "tp"),
            P("tp", both),
            P(both),
        ),
        check_vma=False,
    )
```

```python
import jax
import jax.numpy as jnp
import numpy as np
from jax import lax
from jax.experimental import pallas as pl
from jax.experimental.pallas import tpu as pltpu
from jax.sharding import PartitionSpec as P

MESH_ID = pl.DeviceIdType.MESH
ANY = pl.ANY
VMEM = pltpu.VMEM


class Place:
    def __init__(self):
        self.seq = lax.axis_index("seq")
        ctx = lax.axis_index("ctx")
        self.ctx = ctx
        self.tp = lax.axis_index("tp")
        self.core = ctx % 2
        core = self.core
        y, z = ctx // 8, (ctx // 2) % 4
        self.a = y * (1 - core) + z * core
        self.b = z * (1 - core) + y * core
        self.stride_a = 8 - 6 * core
        self.stride_b = 2 + 6 * core
        self.a_next = self.peer(1, 0)
        self.a_prev = self.peer(3, 0)
        self.b_next = self.peer(0, 1)
        self.b_prev = self.peer(0, 3)
        self.other_core = {"ctx": ctx + 1 - 2 * core}
        self.other_seq = {"seq": 1 - self.seq}
        self.mirror = {"ctx": 31 - ctx}
        self.other_tp = {"tp": 1 - self.tp}

    def peer(self, da, db):
        a, b = (self.a + da) % 4, (self.b + db) % 4
        return {"ctx": a * self.stride_a + b * self.stride_b + self.core}


def greet(peers):
    barrier = pltpu.get_barrier_semaphore()
    for peer in peers:
        pl.semaphore_signal(barrier, inc=1, device_id=peer, device_id_type=MESH_ID)
    pl.semaphore_wait(barrier, len(peers))


def remote(src, dst, send, recv, index, peer):
    return pltpu.make_async_remote_copy(
        src_ref=src,
        dst_ref=dst,
        send_sem=send.at[index],
        recv_sem=recv.at[index],
        device_id=peer,
        device_id_type=MESH_ID,
    )


GATHER_SEMS = 13


class Gather:
    def __init__(self, place, own, full, send, recv, local):
        self.p, self.own, self.full = place, own, full
        self.send, self.recv, self.local = send, recv, local
        self.pair = full.shape[3] == 2
        self.started = []

    def go(self, src, dst, index, peer):
        copy = remote(src, dst, self.send, self.recv, index, peer)
        copy.start()
        self.started.append(copy)

    def got(self, ref, index):
        remote(ref, ref, self.send, self.recv, index, self.p.a_next).wait_recv()

    def half(self, b, a, which):
        ref = self.full.at[self.p.core, b, a]
        if self.pair:
            return ref.at[which]
        rows = self.full.shape[4] // 2
        return ref.at[0, pl.ds(which * rows, rows)]

    def begin(self):
        p = self.p
        slot = self.full.at[p.core, p.b, p.a, p.seq if self.pair else 0]
        self.mine = pltpu.make_async_copy(self.own, slot, self.local)
        self.mine.start()
        if self.pair:
            self.go(self.own, slot, 0, p.other_seq)

    def first(self):
        p = self.p
        self.mine.wait()
        if self.pair:
            self.got(self.full.at[p.core, p.b, p.a, 1 - p.seq], 0)
        block = self.full.at[p.core, p.b, p.a]
        self.go(block, block, 1, p.a_next)
        self.go(block, block, 2, p.a_prev)

    def second(self):
        p = self.p
        down, up = (p.a + 3) % 4, (p.a + 1) % 4
        self.got(self.full.at[p.core, p.b, down], 1)
        half = self.half(p.b, down, 0)
        self.go(half, half, 3, p.a_next)
        self.got(self.full.at[p.core, p.b, up], 2)
        half = self.half(p.b, up, 1)
        self.go(half, half, 4, p.a_prev)

    def third(self):
        p = self.p
        far = (p.a + 2) % 4
        self.got(self.half(p.b, far, 0), 3)
        self.got(self.half(p.b, far, 1), 4)
        block = self.full.at[p.core, p.b]
        self.go(block, block, 5, p.b_next)
        self.go(block, block, 6, p.b_prev)
        self.go(block, block, 9, p.other_core)

    def fourth(self):
        p = self.p
        down, up = (p.b + 3) % 4, (p.b + 1) % 4
        block = self.full.at[p.core, down]
        self.got(block, 5)
        half = self.full.at[p.core, down, pl.ds(0, 2)]
        self.go(half, half, 7, p.b_next)
        self.go(block, block, 10, p.other_core)
        block = self.full.at[p.core, up]
        self.got(block, 6)
        half = self.full.at[p.core, up, pl.ds(2, 2)]
        self.go(half, half, 8, p.b_prev)
        self.go(block, block, 11, p.other_core)

    def fifth(self):
        p = self.p
        far = (p.b + 2) % 4
        self.got(self.full.at[p.core, far, pl.ds(0, 2)], 7)
        self.got(self.full.at[p.core, far, pl.ds(2, 2)], 8)
        block = self.full.at[p.core, far]
        self.go(block, block, 12, p.other_core)

    def finish(self):
        p = self.p
        for index, step in ((9, 0), (10, 3), (11, 1), (12, 2)):
            self.got(self.full.at[1 - p.core, (p.a + step) % 4], index)
        for copy in self.started:
            copy.wait_send()

    def peers(self):
        p = self.p
        found = [p.a_next, p.a_prev, p.b_next, p.b_prev, p.other_core]
        return found + ([p.other_seq] if self.pair else [])


def add_into(target, extra, count):
    def body(k, carry):
        total = target[k].astype(jnp.float32) + extra[k].astype(jnp.float32)
        target[k] = total.astype(target.dtype)
        return carry

    lax.fori_loop(0, count, body, 0)


SCATTER_SEMS = 13


class Scatter:
    @staticmethod
    def scratch(seqs, rows, width):
        bf16 = jnp.bfloat16
        return [
            VMEM((4, 4, seqs, rows, width), bf16),
            VMEM((2, 2, seqs, rows, width), bf16),
            VMEM((1, rows, width), bf16),
            pltpu.SemaphoreType.DMA((SCATTER_SEMS,)),
            pltpu.SemaphoreType.DMA((SCATTER_SEMS,)),
            pltpu.SemaphoreType.REGULAR,
        ]

    def __init__(self, place, part, scratch):
        self.p, self.part = place, part
        self.sums, self.far_b, self.across, self.send, self.recv, self.free = scratch
        self.seqs, self.rows = part.shape[3], part.shape[4]
        spare = part.at[1 - place.core]
        self.near_b = [spare.at[side] for side in range(2)]
        self.near_a = [spare.at[2, side] for side in range(2)]
        self.far_a = [spare.at[2, 2 + side, pl.ds(0, 1)] for side in range(2)]
        if self.seqs == 1:
            self.far_a = [ref.at[:, pl.ds(0, self.rows // 2)] for ref in self.far_a]
        self.started = []

    go = Gather.go
    got = Gather.got

    def half(self, b, a, which):
        ref = self.sums.at[b, a]
        if self.seqs == 2:
            return ref.at[pl.ds(which, 1)]
        rows = self.rows // 2
        return ref.at[:, pl.ds(which * rows, rows)]

    def begin(self):
        p = self.p
        for step in (2, 1, 3, 0):
            slot = (p.a + step) % 4
            self.go(self.part.at[1 - p.core, slot], self.sums.at[slot], step, p.other_core)

    def add_core(self, step):
        p = self.p
        slot = (p.b + step) % 4
        self.got(self.sums.at[slot], step)
        for a in range(4):
            add_into(self.sums.at[slot, a], self.part.at[p.core, slot, a], self.seqs)

    def first(self):
        p = self.p
        self.add_core(2)
        far = (p.b + 2) % 4
        self.go(self.sums.at[far, pl.ds(0, 2)], self.far_b.at[0], 4, p.b_next)
        self.go(self.sums.at[far, pl.ds(2, 2)], self.far_b.at[1], 5, p.b_prev)

    def second(self):
        p = self.p
        up, down = (p.b + 1) % 4, (p.b + 3) % 4
        for copy in self.started[:4]:
            copy.wait_send()
        self.started = self.started[4:]
        ring = (p.a_next, p.a_prev, p.b_next, p.b_prev)
        for peer in ring:
            pl.semaphore_signal(self.free, inc=1, device_id=peer, device_id_type=MESH_ID)
        self.add_core(1)
        self.add_core(3)
        pl.semaphore_wait(self.free, len(ring))
        self.got(self.far_b.at[0], 4)
        for a in range(2):
            add_into(self.sums.at[up, a], self.far_b.at[0, a], self.seqs)
        self.go(self.sums.at[up], self.near_b[0], 6, p.b_next)
        self.got(self.far_b.at[1], 5)
        for a in range(2):
            add_into(self.sums.at[down, a + 2], self.far_b.at[1, a], self.seqs)
        self.go(self.sums.at[down], self.near_b[1], 7, p.b_prev)
        self.add_core(0)

    def third(self):
        p = self.p
        for side in range(2):
            self.got(self.near_b[side], 6 + side)
            for a in range(4):
                add_into(self.sums.at[p.b, a], self.near_b[side].at[a], self.seqs)
        far = (p.a + 2) % 4
        self.go(self.half(p.b, far, 0), self.far_a[0], 8, p.a_next)
        self.go(self.half(p.b, far, 1), self.far_a[1], 9, p.a_prev)

    def fourth(self):
        p = self.p
        up, down = (p.a + 1) % 4, (p.a + 3) % 4
        self.got(self.far_a[0], 8)
        add_into(self.half(p.b, up, 0), self.far_a[0], 1)
        self.go(self.sums.at[p.b, up], self.near_a[0], 10, p.a_next)
        self.got(self.far_a[1], 9)
        add_into(self.half(p.b, down, 1), self.far_a[1], 1)
        self.go(self.sums.at[p.b, down], self.near_a[1], 11, p.a_prev)

    def fifth(self):
        p = self.p
        for side in range(2):
            self.got(self.near_a[side], 10 + side)
            add_into(self.sums.at[p.b, p.a], self.near_a[side], self.seqs)
        if self.seqs == 2:
            self.go(self.sums.at[p.b, p.a, pl.ds(1 - p.seq, 1)], self.across, 12, p.other_seq)

    def finish(self, out):
        p = self.p
        if self.seqs == 2:
            self.got(self.across, 12)
            out[...] = self.sums[p.b, p.a, p.seq].astype(jnp.float32) + self.across[0].astype(jnp.float32)
        else:
            out[...] = self.sums[p.b, p.a, 0].astype(jnp.float32)
        for copy in self.started:
            copy.wait_send()

    def peers(self):
        p = self.p
        found = [p.a_next, p.a_prev, p.b_next, p.b_prev, p.other_core]
        return found + ([p.other_seq] if self.seqs == 2 else [])


NEGATIVE = -1e30
HD = 64
ROWS = 896
TURNS = 33
F32, BF16 = jnp.float32, jnp.bfloat16


def mm(left, right):
    return jnp.dot(left, right, preferred_element_type=F32)


def mm_nt(left, right):
    return lax.dot_general(left, right, (((1,), (1,)), ((), ())), preferred_element_type=F32)


def slot_of(block):
    core, y, z = block % 2, block // 8, (block // 2) % 4
    a = y * (1 - core) + z * core
    b = z * (1 - core) + y * core
    return core, b, a


class Turn:
    def __init__(self, ctx, t, first):
        counts = (ctx + 1, 32 - ctx)
        inside = (t < counts[first]).astype(jnp.int32)
        self.segment = first * inside + (1 - first) * (1 - inside)
        self.block = t - counts[first] * (1 - inside)
        count = counts[0] * (1 - self.segment) + counts[1] * self.segment
        self.first_row = (count - 1) * 256 + 128 * self.segment
        self.hidden = (self.block == 0) | (self.block == count - 1)
        self.last = self.block == count - 1

    def scores(self, scores, doc_ref, hidden):
        if not hidden:
            return scores
        key = lax.broadcasted_iota(jnp.int32, (256, ROWS), 0) + self.block * 256
        row = lax.broadcasted_iota(jnp.int32, (256, ROWS), 1) % 128 + self.first_row
        visible = (key <= row) & (key >= doc_ref[self.segment])
        return jnp.where(visible, scores, NEGATIVE)


def run_turns(ctx, first, start, stop, step):
    def body(t, carry):
        turn = Turn(ctx, t, first)
        pl.when(turn.hidden)(lambda: step(turn, True))
        pl.when(jnp.logical_not(turn.hidden))(lambda: step(turn, False))
        return carry

    lax.fori_loop(start, stop, body, 0)


def attend_step(turn, hidden, kv_ref, q_ref, doc_ref, m_ref, l_ref, acc_ref):
    core, b, a = slot_of(turn.block)
    segment = turn.segment
    kv = kv_ref[core, b, a, 0]
    scores = turn.scores(mm(kv[:, :HD], q_ref[segment]), doc_ref, hidden)
    old = m_ref[segment]
    new = jnp.maximum(old, jnp.max(scores, 0, keepdims=True))
    probs = jnp.exp(scores - new)
    keep = jnp.exp(old - new)
    m_ref[segment] = new
    l_ref[segment] = l_ref[segment] * keep + jnp.sum(probs, 0, keepdims=True)
    acc_ref[segment] = acc_ref[segment] * keep + mm(kv[:, HD:].T, probs.astype(BF16))


def attend_back_step(turn, hidden, kv_ref, q_ref, doc_ref, do_ref, lse_ref, delta_ref, dq_ref, dkv_ref):
    core, b, a = slot_of(turn.block)
    segment = turn.segment
    kv = kv_ref[core, b, a, 0]
    keys, values = kv[:, :HD], kv[:, HD:]
    q, do = q_ref[segment], do_ref[segment]
    scores = turn.scores(mm(keys, q), doc_ref, hidden)
    probs = jnp.exp(scores - lse_ref[segment])
    dscores = (probs * (mm(values, do) - delta_ref[segment])).astype(BF16)
    dq_ref[segment] += mm(keys.T, dscores)
    dkv_ref[core, b, a, 0] += jnp.concatenate([mm_nt(dscores, q), mm_nt(probs.astype(BF16), do)], 1)


D, DPAD, FF_HERE, GROUP, GROUP_Q = 896, 1024, 2432, 576, 448
QKV_W, ATTN_W, FFN_W = 640, 1152, 3 * 2432
GAIN_ONE, GAIN_TWO = 576, 577
EPS_VALUE = 1e-06
THETA = 1000000.0
VMEM_BYTES = 62 << 20
CHUNK = 256


def slot_columns():
    index = np.arange(64)
    seq, y, z, core = index // 32, (index // 8) % 4, (index // 2) % 4, index % 2
    a, b = np.where(core == 0, y, z), np.where(core == 0, z, y)
    slot = ((core * 4 + b) * 4 + a) * 2 + seq
    columns = np.full((64, 16), -1)
    columns[slot, :14] = index[:, None] * 14 + np.arange(14)
    return columns.reshape(-1)


def mm_tn(left, right):
    return lax.dot_general(left, right, (((0,), (0,)), ((), ())), preferred_element_type=F32)


def rope_tables(positions):
    exponents = jnp.arange(HD // 2, dtype=F32) * (2.0 / HD)
    freqs = THETA ** (-exponents)
    angles = freqs[:, None] * positions.astype(F32)[None, :]
    angles = jnp.concatenate([angles, angles], 0)
    return jnp.cos(angles), jnp.sin(angles)


def rotate(values, cosine, sine):
    turned = jnp.concatenate([-values[32:], values[:32]], 0)
    return values * cosine + turned * sine


def rotate_back(grads, cosine, sine):
    sined = grads * sine
    return grads * cosine + jnp.concatenate([sined[32:], -sined[:32]], 0)


def inv_rms(values):
    return lax.rsqrt(jnp.sum(values * values, 0, keepdims=True) * (1.0 / D) + EPS_VALUE)


def norm_back(values, inverse, scaled):
    mean = jnp.sum(scaled * values, 0, keepdims=True) * (1.0 / D)
    return inverse * scaled - values * inverse**3 * mean


def head(index):
    return pl.ds(index * HD, HD)


def lanes(index):
    return pl.ds(index * 128, 128)


def flat(ref, start, width):
    return ref[:, :, :, :, :, pl.ds(start, width)].reshape(DPAD, width)


def unflat(value):
    return value.reshape(2, 4, 4, 2, 16, value.shape[-1])


def shape(dims, dtype):
    return jax.ShapeDtypeStruct(dims, dtype)


def forward_kernel(
    attn_row,
    ffn_row,
    x_in,
    ct_in,
    select,
    cosine,
    sine,
    doc,
    attn_full,
    ffn_full,
    x_out,
    ct_out,
    ct_tokens,
    normed_out,
    q_both,
    kv_full,
    attended,
    lse,
    att,
    middle,
    q_send,
    kv_mine,
    att_send,
    att_far,
    branch_send,
    branch_far,
    m_ref,
    l_ref,
    acc_ref,
    pair_send,
    pair_recv,
    *sems,
):
    p = Place()
    attn = Gather(p, attn_row, attn_full, *sems[0:3])
    ffn = Gather(p, ffn_row, ffn_full, *sems[3:6])
    keys = Gather(p, kv_mine, kv_full, *sems[6:9])
    greet(attn.peers() + [p.mirror, p.other_tp])
    attn.begin()
    ffn.begin()
    x = mm_nt(select[...], x_in[...])
    x_out[...] = x
    attn.first()
    ct_out[...] = mm_nt(select[...], ct_in[...]).astype(BF16)
    attn.second()
    ffn.first()
    ct_tokens[...] = mm_nt(ct_in[...], select[...]).astype(BF16)
    attn.third()
    attn.fourth()
    ffn.second()
    attn.fifth()
    attn.finish()
    ffn.third()

    gain = flat(attn_full, 512, 128)[:, GAIN_ONE - 512 : GAIN_ONE - 511].astype(F32)
    row = lax.broadcasted_iota(jnp.int32, (DPAD, 256), 0)
    x = x_out[...]
    normed = jnp.where(row % 16 == 14, 1.0, x * inv_rms(x) * gain)
    normed_out[...] = normed.astype(BF16)
    mixed = mm(normed.T.astype(BF16), flat(attn_full, 0, QKV_W)).T
    for h in range(7):
        query = rotate(mixed[64 * h : 64 * h + 64], cosine[...], sine[...]).astype(BF16).astype(F32) * 0.125
        q_both[0, :, lanes(h)] = query[:, :128].astype(BF16)
        q_send[:, lanes(h)] = query[:, 128:].astype(BF16)
    q_copy = remote(q_send, q_both.at[1], pair_send, pair_recv, 0, p.mirror)
    q_copy.start()
    key = rotate(mixed[GROUP_Q : GROUP_Q + HD], cosine[...], sine[...])
    kv_mine[...] = jnp.concatenate([key, mixed[GROUP_Q + HD : GROUP]], 0).T.astype(BF16)
    for stage in ("begin", "first", "second", "third", "fourth", "fifth", "finish"):
        getattr(keys, stage)()
    m_ref[...] = jnp.full(m_ref.shape, NEGATIVE, F32)
    l_ref[...] = jnp.zeros(l_ref.shape, F32)
    acc_ref[...] = jnp.zeros(acc_ref.shape, F32)
    q_copy.wait()
    ffn.fourth()

    def step(turn, hidden):
        attend_step(turn, hidden, kv_full, q_both, doc, m_ref, l_ref, acc_ref)

    run_turns(p.ctx, 1, 0, 16, step)
    ffn.fifth()
    run_turns(p.ctx, 1, 16, TURNS, step)
    attended[...] = acc_ref[...] / l_ref[...]
    att_send[...] = attended[1].astype(BF16)
    att_copy = remote(att_send, att_far, pair_send, pair_recv, 1, p.mirror)
    att_copy.start()
    lse[...] = m_ref[...] + jnp.log(l_ref[...])
    att[pl.ds(GROUP_Q, 64), :] = jnp.zeros((64, 256), BF16)
    for h in range(7):
        att[head(h), lanes(0)] = attended[0, :, lanes(h)].astype(BF16)
    att_copy.wait()
    for h in range(7):
        att[head(h), lanes(1)] = att_far[:, lanes(h)]
    branch_send[...] = mm(flat(attn_full, QKV_W, 512), att[...]).astype(BF16)
    branch_copy = remote(branch_send, branch_far, pair_send, pair_recv, 2, p.other_tp)
    branch_copy.start()
    ffn.finish()
    branch_copy.wait()
    middle[...] = x_out[...] + (branch_send[...].astype(F32) + branch_far[...].astype(F32))


def forward(attn_row, ffn_row, x, ct, select, cosine, sine, doc):
    dma = pltpu.SemaphoreType.DMA
    gather_sems = [dma((GATHER_SEMS,)), dma((GATHER_SEMS,)), dma]
    in_vmem, in_hbm = pl.BlockSpec(memory_space=VMEM), pl.BlockSpec(memory_space=ANY)
    return pl.pallas_call(
        forward_kernel,
        out_shape=[
            shape((2, 4, 4, 2, 16, ATTN_W), BF16),
            shape((2, 4, 4, 2, 16, FFN_W), BF16),
            shape((DPAD, 256), F32),
            shape((DPAD, 256), BF16),
            shape((256, DPAD), BF16),
            shape((DPAD, 256), BF16),
            shape((2, HD, ROWS), BF16),
            shape((2, 4, 4, 1, 256, 128), BF16),
            shape((2, HD, ROWS), F32),
            shape((2, 1, ROWS), F32),
            shape((512, 256), BF16),
            shape((DPAD, 256), F32),
        ],
        in_specs=[in_vmem, in_hbm] + [in_vmem] * 6,
        out_specs=[in_vmem, in_hbm] + [in_vmem] * 10,
        scratch_shapes=[
            VMEM((HD, ROWS), BF16),
            VMEM((256, 128), BF16),
            VMEM((HD, ROWS), BF16),
            VMEM((HD, ROWS), BF16),
            VMEM((DPAD, 256), BF16),
            VMEM((DPAD, 256), BF16),
            VMEM((2, 1, ROWS), F32),
            VMEM((2, 1, ROWS), F32),
            VMEM((2, HD, ROWS), F32),
            dma((3,)),
            dma((3,)),
        ]
        + gather_sems * 3,
        compiler_params=pltpu.CompilerParams(collective_id=0, has_side_effects=True, vmem_limit_bytes=VMEM_BYTES),
    )(attn_row, ffn_row, x, ct, select, cosine, sine, doc)


def ffn_chunk(weights, slot, width, normed, tokens, ct, ct_tokens, part, start, out_sum, grad_sum):
    w_gate, w_up, w_down = (weights[slot, k, :, pl.ds(0, width)] for k in range(3))
    gate, up = mm(tokens[...], w_gate), mm(tokens[...], w_up)
    grad_hidden = mm(ct_tokens[...], w_down)
    sigmoid = jax.nn.sigmoid(gate)
    silu = gate * sigmoid
    hidden = (silu * up).astype(BF16)
    grad_up = (grad_hidden * silu).astype(BF16)
    grad_gate = (grad_hidden * up * sigmoid * (1.0 + gate * (1.0 - sigmoid))).astype(BF16)
    grad_sum[...] += mm_nt(w_gate, grad_gate) + mm_nt(w_up, grad_up)
    out_sum[...] += mm_nt(w_down, hidden)
    for k, (left, right) in enumerate(((normed, grad_gate), (normed, grad_up), (ct, hidden))):
        part[:, :, :, :, :, pl.ds(k * FF_HERE + start, width)] = unflat(mm(left[...], right).astype(BF16))


def backward_kernel(
    attn_full,
    ffn_full,
    x_kept,
    ct,
    ct_tokens,
    normed_kept,
    q_both,
    kv_full,
    attended,
    lse,
    att,
    middle,
    cosine,
    sine,
    doc,
    output,
    grad_inputs,
    attn_mine,
    ffn_mine,
    weights,
    normed_ffn,
    tokens,
    out_sum,
    grad_sum,
    out_far,
    grad_far,
    do_both,
    delta,
    dq,
    dq_send,
    dq_far,
    dkv,
    kv_part,
    kv_mine,
    grad_mixed,
    ffn_part,
    attn_part,
    gains_far,
    grad_free,
    weight_sems,
    kept_sems,
    pair_send,
    pair_recv,
    *scratch,
):
    p = Place()
    out_send, grad_send, do_send = output, grad_inputs, dq_send
    ffn = Scatter(p, ffn_part, scratch[0:6])
    keys = Scatter(p, kv_part, scratch[6:12])
    attn = Scatter(p, attn_part, scratch[12:18])

    def load(index, slot, width):
        start = index * CHUNK
        copies = []
        for k in range(3):
            place = pl.ds(pl.multiple_of(k * FF_HERE + start, 128), width)
            copies.append(
                pltpu.make_async_copy(
                    ffn_full.at[:, place], weights.at[slot, k, :, pl.ds(0, width)], weight_sems.at[slot, k]
                )
            )
        return copies

    for copy in load(0, 0, CHUNK):
        copy.start()
    greet(ffn.peers() + [p.mirror, p.other_tp])
    gain_two = flat(attn_full, 512, 128)[:, GAIN_TWO - 512 : GAIN_TWO - 511].astype(F32)
    mid = middle[...]
    inverse = inv_rms(mid)
    scaled = mid * inverse * gain_two
    normed_ffn[...] = scaled.astype(BF16)
    tokens[...] = scaled.T.astype(BF16)
    out_sum[...] = jnp.zeros(out_sum.shape, F32)
    grad_sum[...] = jnp.zeros(grad_sum.shape, F32)
    chunks, tail = FF_HERE // CHUNK, FF_HERE % CHUNK

    def chunk_body(index, carry):
        slot = index % 2
        for copy in load(index, slot, CHUNK):
            copy.wait()

        @pl.when(index < chunks - 1)
        def _():
            for copy in load(index + 1, 1 - slot, CHUNK):
                copy.start()

        @pl.when(index == chunks - 1)
        def _():
            for copy in load(chunks, chunks % 2, tail):
                copy.start()

        start = pl.multiple_of(index * CHUNK, 128)
        ffn_chunk(weights, slot, CHUNK, normed_ffn, tokens, ct, ct_tokens, ffn_part, start, out_sum, grad_sum)
        return carry

    lax.fori_loop(0, chunks, chunk_body, 0)
    for copy in load(chunks, chunks % 2, tail):
        copy.wait()
    ffn_chunk(
        weights, chunks % 2, tail, normed_ffn, tokens, ct, ct_tokens, ffn_part, chunks * CHUNK, out_sum, grad_sum
    )
    grad_send[...] = grad_sum[...].astype(BF16)
    grad_copy = remote(grad_send, grad_far, pair_send, pair_recv, 0, p.other_tp)
    grad_copy.start()
    ffn.begin()
    out_send[...] = out_sum[...].astype(BF16)
    out_copy = remote(out_send, out_far, pair_send, pair_recv, 1, p.other_tp)
    out_copy.start()
    x, normed, grad_middle = out_sum, normed_ffn, grad_sum
    kept = [
        pltpu.make_async_copy(x_kept, x, kept_sems.at[0]),
        pltpu.make_async_copy(normed_kept, normed, kept_sems.at[1]),
    ]
    for copy in kept:
        copy.start()
    dq[...] = jnp.zeros(dq.shape, F32)
    dkv[...] = jnp.zeros(dkv.shape, F32)
    grad_copy.wait()
    mid = middle[...]
    inverse = inv_rms(mid)
    grad_normed = grad_send[...].astype(F32) + grad_far[...].astype(F32)
    pl.semaphore_signal(grad_free, inc=1, device_id=p.other_tp, device_id_type=MESH_ID)
    gain_two_grad = jnp.sum(grad_normed * mid * inverse, 1, keepdims=True)
    grad_mid = ct[...].astype(F32) + norm_back(mid, inverse, grad_normed * gain_two)
    grad_middle[...] = grad_mid
    w_out = flat(attn_full, QKV_W, 512)
    grad_att = mm(grad_mid.T.astype(BF16), w_out).T
    for h in range(7):
        do_both[0, :, lanes(h)] = grad_att[64 * h : 64 * h + 64, :128].astype(BF16)
        do_send[:, lanes(h)] = grad_att[64 * h : 64 * h + 64, 128:].astype(BF16)
    do_copy = remote(do_send, do_both.at[1], pair_send, pair_recv, 2, p.mirror)
    do_copy.start()
    ffn.first()
    do_copy.wait()
    delta[...] = jnp.sum(do_both[...].astype(F32) * attended[...], 1, keepdims=True)

    def step(turn, hidden):
        attend_back_step(turn, hidden, kv_full, q_both, doc, do_both, lse, delta, dq, dkv)

    run_turns(p.ctx, 0, 0, 10, step)
    ffn.second()
    run_turns(p.ctx, 0, 10, TURNS, step)
    dq_send[...] = dq[1].astype(BF16)
    dq_copy = remote(dq_send, dq_far, pair_send, pair_recv, 3, p.mirror)
    dq_copy.start()
    kv_part[...] = dkv[...].astype(BF16)
    keys.begin()
    ffn.third()
    keys.first()
    out_copy.wait()
    output[...] = (middle[...] + (out_send[...].astype(F32) + out_far[...].astype(F32))).astype(BF16)
    keys.second()
    attn_part[:, :, :, :, :, pl.ds(QKV_W, 512)] = unflat(mm_nt(grad_middle[...].astype(BF16), att[...]).astype(BF16))
    keys.third()
    ffn.fourth()
    keys.fourth()
    keys.fifth()
    keys.finish(kv_mine)
    ffn.fifth()
    dq_copy.wait()
    grad_mixed[pl.ds(GROUP, QKV_W - GROUP), :] = jnp.zeros((QKV_W - GROUP, 256), BF16)
    for h in range(7):
        far = dq_far[:, lanes(h)].astype(F32)
        near = dq[0, :, lanes(h)]
        grad_query = jnp.concatenate([near, far], 1) * 0.125
        grad_mixed[head(h), :] = rotate_back(grad_query, cosine[...], sine[...]).astype(BF16)
    grad_kv = kv_mine[...].T
    grad_mixed[head(7), :] = rotate_back(grad_kv[:HD], cosine[...], sine[...]).astype(BF16)
    grad_mixed[head(8), :] = grad_kv[HD:].astype(BF16)
    w_qkv = flat(attn_full, 0, QKV_W)
    grad_normed = mm(w_qkv, grad_mixed[...])
    grad_send[...] = grad_normed.astype(BF16)
    pl.semaphore_wait(grad_free, 1)
    grad_copy = remote(grad_send, grad_far, pair_send, pair_recv, 4, p.other_tp)
    grad_copy.start()
    for copy in kept:
        copy.wait()
    value = x[...]
    inverse = inv_rms(value)
    gain_one_grad = jnp.sum(grad_normed * value * inverse, 1, keepdims=True)
    grad_qkv = mm_nt(normed[...], grad_mixed[...])
    lane = lax.broadcasted_iota(jnp.int32, grad_qkv.shape, 1)
    grad_qkv = jnp.where(lane == GAIN_ONE, gain_one_grad, jnp.where(lane == GAIN_TWO, gain_two_grad, grad_qkv))
    attn_part[:, :, :, :, :, pl.ds(0, QKV_W)] = unflat(grad_qkv.astype(BF16))
    attn.begin()
    ffn.finish(ffn_mine)
    attn.first()
    attn.second()
    grad_copy.wait()
    gain_one = flat(attn_full, 512, 128)[:, GAIN_ONE - 512 : GAIN_ONE - 511].astype(F32)
    scaled = (grad_send[...].astype(F32) + grad_far[...].astype(F32)) * gain_one
    grad_inputs[...] = (grad_middle[...] + norm_back(value, inverse, scaled)).astype(BF16)
    attn.third()
    attn.fourth()
    attn.fifth()
    attn.finish(attn_mine)
    gains_copy = remote(attn_mine.at[:, pl.ds(512, 128)], gains_far, pair_send, pair_recv, 5, p.other_tp)
    gains_copy.start()
    gains_copy.wait()
    mine = attn_mine[:, pl.ds(512, 128)]
    lane = lax.broadcasted_iota(jnp.int32, (16, 128), 1) + 512
    attn_mine[:, pl.ds(512, 128)] = mine + jnp.where(lane == GAIN_ONE, gains_far[...], 0.0)


def backward(*arrays):
    dma = pltpu.SemaphoreType.DMA
    in_vmem, in_hbm = pl.BlockSpec(memory_space=VMEM), pl.BlockSpec(memory_space=ANY)
    wide, tall, low = (DPAD, 256), (256, DPAD), (2, HD, ROWS)
    return pl.pallas_call(
        backward_kernel,
        out_shape=[shape(wide, BF16), shape(wide, BF16), shape((16, ATTN_W), F32), shape((16, FFN_W), F32)],
        in_specs=[in_vmem, in_hbm, in_hbm, in_vmem, in_vmem, in_hbm] + [in_vmem] * 9,
        out_specs=[in_vmem] * 4,
        scratch_shapes=[
            VMEM((2, 3, DPAD, CHUNK), BF16),
            VMEM(wide, BF16),
            VMEM(tall, BF16),
            VMEM(wide, F32),
            VMEM(wide, F32),
            VMEM(wide, BF16),
            VMEM(wide, BF16),
            VMEM(low, BF16),
            VMEM((2, 1, ROWS), F32),
            VMEM(low, F32),
            VMEM((HD, ROWS), BF16),
            VMEM((HD, ROWS), BF16),
            VMEM((2, 4, 4, 1, 256, 128), F32),
            VMEM((2, 4, 4, 1, 256, 128), BF16),
            VMEM((256, 128), F32),
            VMEM((QKV_W, 256), BF16),
            VMEM((2, 4, 4, 2, 16, FFN_W), BF16),
            VMEM((2, 4, 4, 2, 16, ATTN_W), BF16),
            VMEM((16, 128), F32),
            pltpu.SemaphoreType.REGULAR,
            dma((2, 3)),
            dma((2,)),
            dma((6,)),
            dma((6,)),
        ]
        + Scatter.scratch(2, 16, FFN_W)
        + Scatter.scratch(1, 256, 128)
        + Scatter.scratch(2, 16, ATTN_W),
        compiler_params=pltpu.CompilerParams(collective_id=1, has_side_effects=True, vmem_limit_bytes=VMEM_BYTES),
    )(*arrays)


def shards(
    inputs,
    positions,
    query_key_value_weight,
    query_key_value_bias,
    gain_attn,
    output_weight,
    gate_weight,
    up_weight,
    down_weight,
    gain_ffn,
    cotangent,
):
    me = lax.axis_index("seq") * 32 + lax.axis_index("ctx")
    select = jnp.asarray(slot_columns()[:, None] == np.arange(D)[None, :], BF16)
    bias_row = lax.dynamic_update_slice(jnp.zeros((1, GROUP), BF16), query_key_value_bias, (0, 9 * me))
    attn_row = jnp.concatenate(
        [
            jnp.concatenate([query_key_value_weight[:, 0], bias_row, jnp.zeros((1, GROUP), BF16)], 0),
            jnp.pad(jnp.stack([gain_attn, gain_ffn], 1), ((0, 2), (0, 62))),
            jnp.pad(output_weight[0].T, ((0, 2), (0, 64))),
        ],
        1,
    )
    ffn_row = jnp.pad(jnp.concatenate([gate_weight, up_weight, down_weight.T], 1), ((0, 2), (0, 0)))
    cosine, sine = rope_tables(positions[0])
    row = lax.axis_index("ctx") * 256 + jnp.arange(128, dtype=jnp.int32)
    doc = jnp.stack([jnp.tile((row - positions[0, :128])[None], (1, 7)), jnp.full((1, ROWS), 128, jnp.int32)])
    attn_full, ffn_full, *kept = forward(
        attn_row, ffn_row, inputs[0], cotangent[0], select, cosine, sine, doc
    )
    output, grad_inputs, attn, ffn = backward(
        attn_full, ffn_full.reshape(DPAD, FFN_W), *kept, cosine, sine, doc
    )
    return (
        mm_tn(output, select).astype(BF16)[None],
        mm_tn(grad_inputs, select).astype(BF16)[None],
        attn[:14, None, :GROUP],
        lax.dynamic_slice(attn, (14, 8 * me), (1, 8)),
        lax.dynamic_slice(attn, (14, 512 + me), (1, 1)),
        attn[:14, GAIN_ONE],
        attn[:14, QKV_W : QKV_W + GROUP_Q].T[None],
        ffn[:14, :FF_HERE],
        ffn[:14, FF_HERE : 2 * FF_HERE],
        ffn[:14, 2 * FF_HERE :].T,
        attn[:14, GAIN_TWO],
    )


def solution(mesh):
    both = ("seq", "ctx")
    return jax.shard_map(
        shards,
        mesh=mesh,
        in_specs=(
            P("seq", "ctx", None),
            P("seq", "ctx"),
            P(both, "tp", None),
            P("tp", both),
            P(both),
            P("tp", None, both),
            P(both, "tp"),
            P(both, "tp"),
            P("tp", both),
            P(both),
            P("seq", "ctx", None),
        ),
        out_specs=(
            P("seq", "ctx", None),
            P("seq", "ctx", None),
            P(both, "tp", None),
            P("tp", both),
            P("tp", both),
            P(both),
            P("tp", None, both),
            P(both, "tp"),
            P(both, "tp"),
            P("tp", both),
            P(both),
        ),
        check_vma=False,
    )
```

```python
import jax
import jax.numpy as jnp
import numpy as np
from jax import lax
from jax.experimental import pallas as pl
from jax.experimental.pallas import tpu as pltpu
from jax.sharding import PartitionSpec as P

MESH_ID = pl.DeviceIdType.MESH
ANY = pl.ANY
VMEM = pltpu.VMEM


class Place:
    def __init__(self):
        self.seq = lax.axis_index("seq")
        ctx = lax.axis_index("ctx")
        self.ctx = ctx
        self.tp = lax.axis_index("tp")
        self.core = ctx % 2
        core = self.core
        y, z = ctx // 8, (ctx // 2) % 4
        self.a = y * (1 - core) + z * core
        self.b = z * (1 - core) + y * core
        self.stride_a = 8 - 6 * core
        self.stride_b = 2 + 6 * core
        self.a_next = self.peer(1, 0)
        self.a_prev = self.peer(3, 0)
        self.b_next = self.peer(0, 1)
        self.b_prev = self.peer(0, 3)
        self.other_core = {"ctx": ctx + 1 - 2 * core}
        self.other_seq = {"seq": 1 - self.seq}
        self.mirror = {"ctx": 31 - ctx}
        self.other_tp = {"tp": 1 - self.tp}
        self.mirror_tp = {"ctx": 31 - ctx, "tp": 1 - self.tp}

    def peer(self, da, db):
        a, b = (self.a + da) % 4, (self.b + db) % 4
        return {"ctx": a * self.stride_a + b * self.stride_b + self.core}


def greet(peers):
    barrier = pltpu.get_barrier_semaphore()
    for peer in peers:
        pl.semaphore_signal(barrier, inc=1, device_id=peer, device_id_type=MESH_ID)
    pl.semaphore_wait(barrier, len(peers))


def remote(src, dst, send, recv, index, peer):
    return pltpu.make_async_remote_copy(
        src_ref=src,
        dst_ref=dst,
        send_sem=send.at[index],
        recv_sem=recv.at[index],
        device_id=peer,
        device_id_type=MESH_ID,
    )


GATHER_SEMS = 15


class Gather:
    def __init__(self, place, own, full, send, recv, local):
        self.p, self.own, self.full = place, own, full
        self.send, self.recv, self.local = send, recv, local
        self.pair = full.shape[3] == 2
        self.started = []

    def go(self, src, dst, index, peer):
        copy = remote(src, dst, self.send, self.recv, index, peer)
        copy.start()
        self.started.append(copy)

    def got(self, ref, index):
        remote(ref, ref, self.send, self.recv, index, self.p.a_next).wait_recv()

    def half(self, b, a, which):
        ref = self.full.at[self.p.core, b, a]
        if self.pair:
            return ref.at[which]
        rows = self.full.shape[4] // 2
        return ref.at[0, pl.ds(which * rows, rows)]

    def begin(self):
        p = self.p
        slot = self.full.at[p.core, p.b, p.a, p.seq if self.pair else 0]
        self.mine = pltpu.make_async_copy(self.own, slot, self.local)
        self.mine.start()
        if self.pair:
            self.go(self.own, slot, 0, p.other_seq)

    def first(self):
        p = self.p
        self.mine.wait()
        if self.pair:
            self.got(self.full.at[p.core, p.b, p.a, 1 - p.seq], 0)
        block = self.full.at[p.core, p.b, p.a]
        self.go(block, block, 1, p.a_next)
        self.go(block, block, 2, p.a_prev)

    def second(self):
        p = self.p
        down, up = (p.a + 3) % 4, (p.a + 1) % 4
        self.got(self.full.at[p.core, p.b, down], 1)
        half = self.half(p.b, down, 0)
        self.go(half, half, 3, p.a_next)
        self.got(self.full.at[p.core, p.b, up], 2)
        half = self.half(p.b, up, 1)
        self.go(half, half, 4, p.a_prev)

    def third_near(self):
        p = self.p
        far = (p.a + 2) % 4
        self.got(self.half(p.b, far, 0), 3)
        self.got(self.half(p.b, far, 1), 4)
        row = self.full.at[p.core, p.b]
        self.go(row.at[pl.ds(0, 2)], row.at[pl.ds(0, 2)], 5, p.b_next)
        self.go(row.at[pl.ds(2, 2)], row.at[pl.ds(2, 2)], 6, p.b_prev)
        self.go(row, row, 9, p.other_core)

    def third_rest(self):
        p = self.p
        row = self.full.at[p.core, p.b]
        self.go(row.at[pl.ds(2, 2)], row.at[pl.ds(2, 2)], 13, p.b_next)
        self.go(row.at[pl.ds(0, 2)], row.at[pl.ds(0, 2)], 14, p.b_prev)

    def third(self):
        self.third_near()
        self.third_rest()

    def fourth_near(self):
        p = self.p
        half = self.full.at[p.core, (p.b + 3) % 4, pl.ds(0, 2)]
        self.got(half, 5)
        self.go(half, half, 7, p.b_next)
        half = self.full.at[p.core, (p.b + 1) % 4, pl.ds(2, 2)]
        self.got(half, 6)
        self.go(half, half, 8, p.b_prev)

    def fourth_rest(self):
        p = self.p
        down, up = (p.b + 3) % 4, (p.b + 1) % 4
        self.got(self.full.at[p.core, down, pl.ds(2, 2)], 13)
        row = self.full.at[p.core, down]
        self.go(row, row, 10, p.other_core)
        self.got(self.full.at[p.core, up, pl.ds(0, 2)], 14)
        row = self.full.at[p.core, up]
        self.go(row, row, 11, p.other_core)

    def fourth(self):
        self.fourth_near()
        self.fourth_rest()

    def fifth(self):
        p = self.p
        far = (p.b + 2) % 4
        self.got(self.full.at[p.core, far, pl.ds(0, 2)], 7)
        self.got(self.full.at[p.core, far, pl.ds(2, 2)], 8)
        block = self.full.at[p.core, far]
        self.go(block, block, 12, p.other_core)

    def finish(self):
        for step in (0, 3, 1, 2):
            self.from_core(step)
        self.sent()

    def from_core(self, step):
        p = self.p
        self.got(self.full.at[1 - p.core, (p.a + step) % 4], {0: 9, 3: 10, 1: 11, 2: 12}[step])

    def sent(self):
        for copy in self.started:
            copy.wait_send()

    def peers(self):
        p = self.p
        found = [p.a_next, p.a_prev, p.b_next, p.b_prev, p.other_core]
        return found + ([p.other_seq] if self.pair else [])


def add_into(target, extra, count):
    def body(k, carry):
        total = target[k].astype(jnp.float32) + extra[k].astype(jnp.float32)
        target[k] = total.astype(target.dtype)
        return carry

    lax.fori_loop(0, count, body, 0)


SCATTER_SEMS = 13


class Scatter:
    @staticmethod
    def scratch(seqs, rows, width):
        bf16 = jnp.bfloat16
        return [
            VMEM((4, 4, seqs, rows, width), bf16),
            VMEM((2, 2, seqs, rows, width), bf16),
            VMEM((1, rows, width), bf16),
            pltpu.SemaphoreType.DMA((SCATTER_SEMS,)),
            pltpu.SemaphoreType.DMA((SCATTER_SEMS,)),
            pltpu.SemaphoreType.REGULAR,
        ]

    def __init__(self, place, part, scratch):
        self.p, self.part = place, part
        self.sums, self.far_b, self.across, self.send, self.recv, self.free = scratch
        self.seqs, self.rows = part.shape[3], part.shape[4]
        spare = part.at[1 - place.core]
        self.near_b = [spare.at[side] for side in range(2)]
        self.near_a = [spare.at[2, side] for side in range(2)]
        self.far_a = [spare.at[2, 2 + side, pl.ds(0, 1)] for side in range(2)]
        if self.seqs == 1:
            self.far_a = [ref.at[:, pl.ds(0, self.rows // 2)] for ref in self.far_a]
        self.started = []

    go = Gather.go
    got = Gather.got

    def half(self, b, a, which):
        ref = self.sums.at[b, a]
        if self.seqs == 2:
            return ref.at[pl.ds(which, 1)]
        rows = self.rows // 2
        return ref.at[:, pl.ds(which * rows, rows)]

    def to_core(self, step):
        p = self.p
        slot = (p.a + step) % 4
        self.go(self.part.at[1 - p.core, slot], self.sums.at[slot], step, p.other_core)

    def begin(self):
        for step in (2, 1, 3, 0):
            self.to_core(step)

    def add_core(self, step):
        p = self.p
        slot = (p.b + step) % 4
        self.got(self.sums.at[slot], step)
        for a in range(4):
            add_into(self.sums.at[slot, a], self.part.at[p.core, slot, a], self.seqs)

    def first(self):
        p = self.p
        self.add_core(2)
        far = (p.b + 2) % 4
        self.go(self.sums.at[far, pl.ds(0, 2)], self.far_b.at[0], 4, p.b_next)
        self.go(self.sums.at[far, pl.ds(2, 2)], self.far_b.at[1], 5, p.b_prev)

    def second(self):
        p = self.p
        up, down = (p.b + 1) % 4, (p.b + 3) % 4
        for copy in self.started[:4]:
            copy.wait_send()
        self.started = self.started[4:]
        ring = (p.a_next, p.a_prev, p.b_next, p.b_prev)
        for peer in ring:
            pl.semaphore_signal(self.free, inc=1, device_id=peer, device_id_type=MESH_ID)
        self.add_core(1)
        self.add_core(3)
        pl.semaphore_wait(self.free, len(ring))
        self.got(self.far_b.at[0], 4)
        for a in range(2):
            add_into(self.sums.at[up, a], self.far_b.at[0, a], self.seqs)
        self.go(self.sums.at[up], self.near_b[0], 6, p.b_next)
        self.got(self.far_b.at[1], 5)
        for a in range(2):
            add_into(self.sums.at[down, a + 2], self.far_b.at[1, a], self.seqs)
        self.go(self.sums.at[down], self.near_b[1], 7, p.b_prev)

    def third(self):
        p = self.p
        self.add_core(0)
        for side in range(2):
            self.got(self.near_b[side], 6 + side)
            for a in range(4):
                add_into(self.sums.at[p.b, a], self.near_b[side].at[a], self.seqs)
        far = (p.a + 2) % 4
        self.go(self.half(p.b, far, 0), self.far_a[0], 8, p.a_next)
        self.go(self.half(p.b, far, 1), self.far_a[1], 9, p.a_prev)

    def fourth(self):
        p = self.p
        up, down = (p.a + 1) % 4, (p.a + 3) % 4
        self.got(self.far_a[0], 8)
        add_into(self.half(p.b, up, 0), self.far_a[0], 1)
        self.go(self.sums.at[p.b, up], self.near_a[0], 10, p.a_next)
        self.got(self.far_a[1], 9)
        add_into(self.half(p.b, down, 1), self.far_a[1], 1)
        self.go(self.sums.at[p.b, down], self.near_a[1], 11, p.a_prev)

    def fifth(self):
        p = self.p
        for side in range(2):
            self.got(self.near_a[side], 10 + side)
            add_into(self.sums.at[p.b, p.a], self.near_a[side], self.seqs)
        if self.seqs == 2:
            self.go(self.sums.at[p.b, p.a, pl.ds(1 - p.seq, 1)], self.across, 12, p.other_seq)

    def finish(self, out):
        p = self.p
        if self.seqs == 2:
            self.got(self.across, 12)
            out[...] = self.sums[p.b, p.a, p.seq].astype(jnp.float32) + self.across[0].astype(jnp.float32)
        else:
            out[...] = self.sums[p.b, p.a, 0].astype(jnp.float32)
        for copy in self.started:
            copy.wait_send()

    def peers(self):
        p = self.p
        found = [p.a_next, p.a_prev, p.b_next, p.b_prev, p.other_core]
        return found + ([p.other_seq] if self.seqs == 2 else [])


NEGATIVE = -1e30
HD = 64
ROWS = 896
TURNS = 33
F32, BF16 = jnp.float32, jnp.bfloat16


def mm(left, right):
    return jnp.dot(left, right, preferred_element_type=F32)


def mm_nt(left, right):
    return lax.dot_general(left, right, (((1,), (1,)), ((), ())), preferred_element_type=F32)


def block_of(core, b, a):
    y = a * (1 - core) + b * core
    z = b * (1 - core) + a * core
    return y * 8 + z * 2 + core


class Turn:
    def __init__(self, ctx, segment, slot):
        self.segment, self.slot = segment, slot
        self.block = block_of(*slot)
        count = (ctx + 1) * (1 - segment) + (32 - ctx) * segment
        self.first_row = (count - 1) * 256 + 128 * segment
        self.needed = self.block < count
        self.hidden = (self.block == 0) | (self.block == count - 1)

    def scores(self, scores, doc_ref, hidden):
        if not hidden:
            return scores
        key = lax.broadcasted_iota(jnp.int32, (256, ROWS), 0) + self.block * 256
        row = lax.broadcasted_iota(jnp.int32, (256, ROWS), 1) % 128 + self.first_row
        visible = (key <= row) & (key >= doc_ref[self.segment])
        return jnp.where(visible, scores, NEGATIVE)


def run_row(ctx, core, b, step):
    def body(n, carry):
        turn = Turn(ctx, n // 4, (core, b, n % 4))
        pl.when(turn.needed & turn.hidden)(lambda: step(turn, True))
        pl.when(turn.needed & jnp.logical_not(turn.hidden))(lambda: step(turn, False))
        return carry

    lax.fori_loop(0, 8, body, 0)


def attend_step(turn, hidden, kv_ref, q_ref, doc_ref, m_ref, l_ref, acc_ref):
    core, b, a = turn.slot
    segment = turn.segment
    kv = kv_ref[core, b, a, 0]
    scores = turn.scores(mm(kv[:, :HD], q_ref[segment]), doc_ref, hidden)
    old = m_ref[segment]
    new = jnp.maximum(old, jnp.max(scores, 0, keepdims=True))
    probs = jnp.exp(scores - new)
    keep = jnp.exp(old - new)
    m_ref[segment] = new
    l_ref[segment] = l_ref[segment] * keep + jnp.sum(probs, 0, keepdims=True)
    acc_ref[segment] = acc_ref[segment] * keep + mm(kv[:, HD:].T, probs.astype(BF16))


def attend_back_step(turn, hidden, kv_ref, q_ref, doc_ref, do_ref, lse_ref, delta_ref, dq_ref, dkv_ref):
    core, b, a = turn.slot
    segment = turn.segment
    kv = kv_ref[core, b, a, 0]
    keys, values = kv[:, :HD], kv[:, HD:]
    q, do = q_ref[segment], do_ref[segment]
    scores = turn.scores(mm(keys, q), doc_ref, hidden)
    probs = jnp.exp(scores - lse_ref[segment])
    dscores = (probs * (mm(values, do) - delta_ref[segment])).astype(BF16)
    dq_ref[segment] += mm(keys.T, dscores)
    dkv_ref[core, b, a, 0] += jnp.concatenate([mm_nt(dscores, q), mm_nt(probs.astype(BF16), do)], 1)


D, DPAD, FF_HERE, GROUP, GROUP_Q = 896, 1024, 2432, 576, 448
QKV_W, OUT_W, FFN_W = 640, 512, 3 * 2432
ATTN_W = QKV_W + OUT_W
GAIN_ONE, GAIN_TWO = 576, 577
EPS_VALUE = 1e-06
THETA = 1000000.0
VMEM_BYTES = 62 << 20
CHUNK = 256


def slot_columns():
    index = np.arange(64)
    seq, y, z, core = index // 32, (index // 8) % 4, (index // 2) % 4, index % 2
    a, b = np.where(core == 0, y, z), np.where(core == 0, z, y)
    slot = ((core * 4 + b) * 4 + a) * 2 + seq
    columns = np.full((64, 16), -1)
    columns[slot, :14] = index[:, None] * 14 + np.arange(14)
    return columns.reshape(-1)


def mm_tn(left, right):
    return lax.dot_general(left, right, (((0,), (0,)), ((), ())), preferred_element_type=F32)


def rope_tables(positions):
    exponents = jnp.arange(HD // 2, dtype=F32) * (2.0 / HD)
    freqs = THETA ** (-exponents)
    angles = freqs[:, None] * positions.astype(F32)[None, :]
    angles = jnp.concatenate([angles, angles], 0)
    return jnp.cos(angles), jnp.sin(angles)


def rotate(values, cosine, sine):
    turned = jnp.concatenate([-values[32:], values[:32]], 0)
    return values * cosine + turned * sine


def rotate_back(grads, cosine, sine):
    sined = grads * sine
    return grads * cosine + jnp.concatenate([sined[32:], -sined[:32]], 0)


def inv_rms(values):
    return lax.rsqrt(jnp.sum(values * values, 0, keepdims=True) * (1.0 / D) + EPS_VALUE)


def norm_back(values, inverse, scaled):
    mean = jnp.sum(scaled * values, 0, keepdims=True) * (1.0 / D)
    return inverse * scaled - values * inverse**3 * mean


def head(index):
    return pl.ds(index * HD, HD)


def lanes(index):
    return pl.ds(index * 128, 128)


def flat(ref, start, width):
    if not isinstance(start, int):
        start = pl.multiple_of(start, 128)
    return ref[:, :, :, :, :, pl.ds(start, width)].reshape(DPAD, width)


def unflat(value):
    return value.reshape(2, 4, 4, 2, 16, value.shape[-1])


def shape(dims, dtype):
    return jax.ShapeDtypeStruct(dims, dtype)


def forward_kernel(
    attn_row,
    out_row,
    ffn_row,
    x_in,
    ct_in,
    select,
    cosine,
    sine,
    doc,
    attn_full,
    ffn_full,
    w_out,
    x_out,
    ct_out,
    ct_tokens,
    normed_out,
    q_both,
    kv_full,
    attended,
    lse,
    att,
    middle,
    outs_mine,
    outs_full,
    q_send,
    kv_mine,
    att_send,
    att_far,
    m_ref,
    l_ref,
    acc_ref,
    pair_send,
    pair_recv,
    *sems,
):
    p = Place()
    attn = Gather(p, attn_row, attn_full, *sems[0:3])
    ffn = Gather(p, ffn_row, ffn_full, *sems[3:6])
    keys = Gather(p, kv_mine, kv_full, *sems[6:9])
    outs = Gather(p, outs_mine, outs_full, *sems[9:12])
    greet(attn.peers() + [p.mirror, p.other_tp, p.mirror_tp])
    attn.begin()
    own_out = pl.ds(pl.multiple_of(p.tp * OUT_W, 128), OUT_W)
    out_copy = remote(out_row, outs_mine.at[:, own_out], pair_send, pair_recv, 0, p.other_tp)
    out_copy.start()
    ffn.begin()
    outs_mine[:, own_out] = out_row[...]
    x = mm_nt(select[...], x_in[...])
    x_out[...] = x
    attn.first()
    ct_out[...] = mm_nt(select[...], ct_in[...]).astype(BF16)
    attn.second()
    ct_tokens[...] = mm_nt(ct_in[...], select[...]).astype(BF16)
    attn.third()
    ffn.first()
    m_ref[...] = jnp.full(m_ref.shape, NEGATIVE, F32)
    l_ref[...] = jnp.zeros(l_ref.shape, F32)
    acc_ref[...] = jnp.zeros(acc_ref.shape, F32)
    attn.fourth()
    attn.fifth()
    ffn.second()
    out_copy.wait()
    attn.finish()
    outs.begin()

    gain = flat(attn_full, 512, 128)[:, GAIN_ONE - 512 : GAIN_ONE - 511].astype(F32)
    row = lax.broadcasted_iota(jnp.int32, (DPAD, 256), 0)
    x = x_out[...]
    normed = jnp.where(row % 16 == 14, 1.0, x * inv_rms(x) * gain)
    normed_out[...] = normed.astype(BF16)
    outs.first()
    mixed = mm(normed.T.astype(BF16), flat(attn_full, 0, QKV_W)).T
    outs.second()
    key = rotate(mixed[GROUP_Q : GROUP_Q + HD], cosine[...], sine[...])
    kv_mine[...] = jnp.concatenate([key, mixed[GROUP_Q + HD : GROUP]], 0).T.astype(BF16)
    keys.begin()
    keys.first()
    for h in range(7):
        query = rotate(mixed[64 * h : 64 * h + 64], cosine[...], sine[...]).astype(BF16).astype(F32) * 0.125
        q_both[0, :, lanes(h)] = query[:, :128].astype(BF16)
        q_send[:, lanes(h)] = query[:, 128:].astype(BF16)
    q_copy = remote(q_send, q_both.at[1], pair_send, pair_recv, 1, p.mirror)
    q_copy.start()
    keys.second()
    ffn.third_near()
    outs.third()
    keys.third()
    q_copy.wait()

    def step(turn, hidden):
        attend_step(turn, hidden, kv_full, q_both, doc, m_ref, l_ref, acc_ref)

    run_row(p.ctx, p.core, p.b, step)
    outs.fourth()
    keys.fourth()
    run_row(p.ctx, p.core, (p.b + 3) % 4, step)
    outs.fifth()
    keys.fifth()
    ffn.third_rest()
    run_row(p.ctx, p.core, (p.b + 1) % 4, step)
    run_row(p.ctx, p.core, (p.b + 2) % 4, step)
    ffn.fourth_near()
    for ahead in (0, 3, 1, 2):
        keys.from_core(ahead)
        run_row(p.ctx, 1 - p.core, (p.a + ahead) % 4, step)
    keys.sent()
    attended[...] = acc_ref[...] / l_ref[...]
    att_send[...] = attended[...].astype(BF16)
    att_copies = [
        remote(att_send.at[1], att_far.at[0], pair_send, pair_recv, 2, p.mirror),
        remote(att_send.at[0], att_far.at[1], pair_send, pair_recv, 3, p.other_tp),
        remote(att_send.at[1], att_far.at[2], pair_send, pair_recv, 4, p.mirror_tp),
    ]
    for copy in att_copies:
        copy.start()
    lse[...] = m_ref[...] + jnp.log(l_ref[...])
    outs.finish()
    ffn.fourth_rest()
    w_out[...] = flat(outs_full, p.tp * OUT_W, OUT_W)
    att[:, pl.ds(GROUP_Q, 64), :] = jnp.zeros((2, 64, 256), BF16)
    for h in range(7):
        att[p.tp, head(h), lanes(0)] = att_send[0, :, lanes(h)]
    for copy in att_copies:
        copy.wait()
    for h in range(7):
        att[p.tp, head(h), lanes(1)] = att_far[0, :, lanes(h)]
        att[1 - p.tp, head(h), lanes(0)] = att_far[1, :, lanes(h)]
        att[1 - p.tp, head(h), lanes(1)] = att_far[2, :, lanes(h)]
    middle[...] = x_out[...] + mm(flat(outs_full, 0, 2 * OUT_W), att[...].reshape(2 * OUT_W, 256))
    ffn.fifth()
    ffn.finish()


def forward(*arrays):
    dma = pltpu.SemaphoreType.DMA
    gather_sems = [dma((GATHER_SEMS,)), dma((GATHER_SEMS,)), dma]
    in_vmem, in_hbm = pl.BlockSpec(memory_space=VMEM), pl.BlockSpec(memory_space=ANY)
    return pl.pallas_call(
        forward_kernel,
        out_shape=[
            shape((2, 4, 4, 2, 16, QKV_W), BF16),
            shape((2, 4, 4, 2, 16, FFN_W), BF16),
            shape((DPAD, OUT_W), BF16),
            shape((DPAD, 256), F32),
            shape((DPAD, 256), BF16),
            shape((256, DPAD), BF16),
            shape((DPAD, 256), BF16),
            shape((2, HD, ROWS), BF16),
            shape((2, 4, 4, 1, 256, 128), BF16),
            shape((2, HD, ROWS), F32),
            shape((2, 1, ROWS), F32),
            shape((2, OUT_W, 256), BF16),
            shape((DPAD, 256), F32),
        ],
        in_specs=[in_vmem, in_vmem, in_hbm] + [in_vmem] * 6,
        out_specs=[in_vmem, in_hbm] + [in_vmem] * 11,
        scratch_shapes=[
            VMEM((16, 2 * OUT_W), BF16),
            VMEM((2, 4, 4, 2, 16, 2 * OUT_W), BF16),
            VMEM((HD, ROWS), BF16),
            VMEM((256, 128), BF16),
            VMEM((2, HD, ROWS), BF16),
            VMEM((3, HD, ROWS), BF16),
            VMEM((2, 1, ROWS), F32),
            VMEM((2, 1, ROWS), F32),
            VMEM((2, HD, ROWS), F32),
            dma((5,)),
            dma((5,)),
        ]
        + gather_sems * 4,
        compiler_params=pltpu.CompilerParams(collective_id=0, has_side_effects=True, vmem_limit_bytes=VMEM_BYTES),
    )(*arrays)


def tile_of(index):
    return index // 16, (index // 4) % 4, index % 4, 0


def ffn_chunk(weights, slot, width, tile, tokens, ct_tokens, gate_kept, up_kept, hidden_kept, out_sum, grad_sum):
    w_gate, w_up, w_down = (weights[slot, k, :, pl.ds(0, width)] for k in range(3))
    gate, up = mm(tokens[...], w_gate), mm(tokens[...], w_up)
    grad_hidden = mm(ct_tokens[...], w_down)
    sigmoid = jax.nn.sigmoid(gate)
    silu = gate * sigmoid
    hidden = (silu * up).astype(BF16)
    grad_up = (grad_hidden * silu).astype(BF16)
    grad_gate = (grad_hidden * up * sigmoid * (1.0 + gate * (1.0 - sigmoid))).astype(BF16)
    grad_sum[...] += mm_nt(w_gate, grad_gate) + mm_nt(w_up, grad_up)
    out_sum[...] += mm_nt(w_down, hidden)
    for k in range(width // 128):
        part = slice(128 * k, 128 * k + 128)
        gate_kept[tile_of(tile + k)] = grad_gate[:, part]
        up_kept[tile_of(tile + k)] = grad_up[:, part].astype(F32)
        hidden_kept[tile + k] = hidden[:, part]


def ffn_weight_grads(tile, tiles, normed, ct, gate_kept, up_kept, hidden_kept, part):
    places = [tile_of(tile + k) for k in range(tiles)]
    pairs = (
        (normed, [gate_kept[place] for place in places]),
        (normed, [up_kept[place].astype(BF16) for place in places]),
        (ct, [hidden_kept[tile + k] for k in range(tiles)]),
    )
    for k, (left, right) in enumerate(pairs):
        start = k * FF_HERE + tile * 128
        if not isinstance(start, int):
            start = pl.multiple_of(start, 128)
        product = mm(left[...], jnp.concatenate(right, 1) if tiles > 1 else right[0])
        part[:, :, :, :, :, pl.ds(start, tiles * 128)] = unflat(product.astype(BF16))


def backward_kernel(
    attn_full,
    ffn_full,
    w_out,
    x_kept,
    ct,
    ct_tokens,
    normed_kept,
    q_both,
    kv_full,
    attended,
    lse,
    att,
    middle,
    cosine,
    sine,
    doc,
    output,
    grad_inputs,
    attn_mine,
    ffn_mine,
    weights,
    hidden_kept,
    normed_ffn,
    tokens,
    out_sum,
    grad_sum,
    out_far,
    grad_far,
    do_both,
    delta,
    dq,
    dq_send,
    dq_far,
    dkv,
    kv_part,
    kv_mine,
    grad_mixed,
    ffn_part,
    attn_part,
    gains_far,
    grad_free,
    weight_sems,
    kept_sems,
    pair_send,
    pair_recv,
    *scratch,
):
    p = Place()
    out_send, grad_send, do_send = output, grad_inputs, dq_send
    ffn = Scatter(p, ffn_part, scratch[0:6])
    keys = Scatter(p, kv_part, scratch[6:12])
    attn = Scatter(p, attn_part, scratch[12:18])

    def load(index, slot, width):
        start = index * CHUNK
        copies = []
        for k in range(3):
            place = pl.ds(pl.multiple_of(k * FF_HERE + start, 128), width)
            copies.append(
                pltpu.make_async_copy(
                    ffn_full.at[:, place], weights.at[slot, k, :, pl.ds(0, width)], weight_sems.at[slot, k]
                )
            )
        return copies

    for copy in load(0, 0, CHUNK):
        copy.start()
    greet(ffn.peers() + [p.mirror, p.other_tp])
    ffn_kept = (kv_part, dkv, hidden_kept)
    gain_two = flat(attn_full, 512, 128)[:, GAIN_TWO - 512 : GAIN_TWO - 511].astype(F32)
    mid = middle[...]
    inverse = inv_rms(mid)
    scaled = mid * inverse * gain_two
    normed_ffn[...] = scaled.astype(BF16)
    tokens[...] = scaled.T.astype(BF16)
    out_sum[...] = jnp.zeros(out_sum.shape, F32)
    grad_sum[...] = jnp.zeros(grad_sum.shape, F32)
    chunks, tail, tiles = FF_HERE // CHUNK, FF_HERE % CHUNK, CHUNK // 128

    def chunk_body(index, carry):
        slot = index % 2
        for copy in load(index, slot, CHUNK):
            copy.wait()

        @pl.when(index < chunks - 1)
        def _():
            for copy in load(index + 1, 1 - slot, CHUNK):
                copy.start()

        @pl.when(index == chunks - 1)
        def _():
            for copy in load(chunks, chunks % 2, tail):
                copy.start()

        ffn_chunk(weights, slot, CHUNK, index * tiles, tokens, ct_tokens, *ffn_kept, out_sum, grad_sum)
        return carry

    lax.fori_loop(0, chunks, chunk_body, 0)
    for copy in load(chunks, chunks % 2, tail):
        copy.wait()
    ffn_chunk(weights, chunks % 2, tail, chunks * tiles, tokens, ct_tokens, *ffn_kept, out_sum, grad_sum)
    grad_send[...] = grad_sum[...].astype(BF16)
    grad_copy = remote(grad_send, grad_far, pair_send, pair_recv, 0, p.other_tp)
    grad_copy.start()

    def grads_body(index, carry):
        ffn_weight_grads(index * tiles, tiles, normed_ffn, ct, *ffn_kept, ffn_part)
        return carry

    lax.fori_loop(0, chunks, grads_body, 0)
    ffn_weight_grads(chunks * tiles, tail // 128, normed_ffn, ct, *ffn_kept, ffn_part)
    ffn.begin()
    out_send[...] = out_sum[...].astype(BF16)
    x, normed, grad_middle = out_sum, normed_ffn, grad_sum
    kept = [
        pltpu.make_async_copy(x_kept, x, kept_sems.at[0]),
        pltpu.make_async_copy(normed_kept, normed, kept_sems.at[1]),
    ]
    for copy in kept:
        copy.start()
    dq[...] = jnp.zeros(dq.shape, F32)
    dkv[...] = jnp.zeros(dkv.shape, F32)
    grad_copy.wait()
    out_copy = remote(out_send, out_far, pair_send, pair_recv, 1, p.other_tp)
    out_copy.start()
    mid = middle[...]
    inverse = inv_rms(mid)
    grad_normed = grad_send[...].astype(F32) + grad_far[...].astype(F32)
    pl.semaphore_signal(grad_free, inc=1, device_id=p.other_tp, device_id_type=MESH_ID)
    gain_two_grad = jnp.sum(grad_normed * mid * inverse, 1, keepdims=True)
    grad_mid = ct[...].astype(F32) + norm_back(mid, inverse, grad_normed * gain_two)
    grad_middle[...] = grad_mid
    grad_att = mm(grad_mid.T.astype(BF16), w_out[...]).T
    for h in range(7):
        do_both[0, :, lanes(h)] = grad_att[64 * h : 64 * h + 64, :128].astype(BF16)
        do_send[:, lanes(h)] = grad_att[64 * h : 64 * h + 64, 128:].astype(BF16)
    do_copy = remote(do_send, do_both.at[1], pair_send, pair_recv, 2, p.mirror)
    do_copy.start()
    ffn.first()
    do_copy.wait()
    delta[...] = jnp.sum(do_both[...].astype(F32) * attended[...], 1, keepdims=True)

    def step(turn, hidden):
        attend_back_step(turn, hidden, kv_full, q_both, doc, do_both, lse, delta, dq, dkv)

    def far_row(ahead):
        slot = (p.a + ahead) % 4
        run_row(p.ctx, 1 - p.core, slot, step)
        kv_part[1 - p.core, slot] = dkv[1 - p.core, slot].astype(BF16)
        keys.to_core(ahead)

    def own_row(ahead):
        slot = (p.b + ahead) % 4
        run_row(p.ctx, p.core, slot, step)
        kv_part[p.core, slot] = dkv[p.core, slot].astype(BF16)

    far_row(2)
    far_row(1)
    ffn.second()
    far_row(3)
    far_row(0)
    own_row(2)
    keys.first()
    own_row(1)
    own_row(3)
    keys.second()
    own_row(0)
    ffn.third()
    dq_send[...] = dq[1].astype(BF16)
    dq_copy = remote(dq_send, dq_far, pair_send, pair_recv, 3, p.mirror)
    dq_copy.start()
    out_copy.wait()
    output[...] = (middle[...] + (out_send[...].astype(F32) + out_far[...].astype(F32))).astype(BF16)
    keys.third()
    attn_part[:, :, :, :, :, pl.ds(QKV_W, OUT_W)] = unflat(
        mm_nt(grad_middle[...].astype(BF16), att[p.tp]).astype(BF16)
    )
    ffn.fourth()
    keys.fourth()
    keys.fifth()
    keys.finish(kv_mine)
    ffn.fifth()
    dq_copy.wait()
    grad_mixed[pl.ds(GROUP, QKV_W - GROUP), :] = jnp.zeros((QKV_W - GROUP, 256), BF16)
    for h in range(7):
        far = dq_far[:, lanes(h)].astype(F32)
        near = dq[0, :, lanes(h)]
        grad_query = jnp.concatenate([near, far], 1) * 0.125
        grad_mixed[head(h), :] = rotate_back(grad_query, cosine[...], sine[...]).astype(BF16)
    grad_kv = kv_mine[...].T
    grad_mixed[head(7), :] = rotate_back(grad_kv[:HD], cosine[...], sine[...]).astype(BF16)
    grad_mixed[head(8), :] = grad_kv[HD:].astype(BF16)
    w_qkv = flat(attn_full, 0, QKV_W)
    grad_normed = mm(w_qkv, grad_mixed[...])
    grad_send[...] = grad_normed.astype(BF16)
    pl.semaphore_wait(grad_free, 1)
    grad_copy = remote(grad_send, grad_far, pair_send, pair_recv, 4, p.other_tp)
    grad_copy.start()
    for copy in kept:
        copy.wait()
    value = x[...]
    inverse = inv_rms(value)
    gain_one_grad = jnp.sum(grad_normed * value * inverse, 1, keepdims=True)
    grad_qkv = mm_nt(normed[...], grad_mixed[...])
    lane = lax.broadcasted_iota(jnp.int32, grad_qkv.shape, 1)
    grad_qkv = jnp.where(lane == GAIN_ONE, gain_one_grad, jnp.where(lane == GAIN_TWO, gain_two_grad, grad_qkv))
    attn_part[:, :, :, :, :, pl.ds(0, QKV_W)] = unflat(grad_qkv.astype(BF16))
    attn.begin()
    ffn.finish(ffn_mine)
    attn.first()
    attn.second()
    grad_copy.wait()
    gain_one = flat(attn_full, 512, 128)[:, GAIN_ONE - 512 : GAIN_ONE - 511].astype(F32)
    scaled = (grad_send[...].astype(F32) + grad_far[...].astype(F32)) * gain_one
    grad_inputs[...] = (grad_middle[...] + norm_back(value, inverse, scaled)).astype(BF16)
    attn.third()
    attn.fourth()
    attn.fifth()
    attn.finish(attn_mine)
    gains_copy = remote(attn_mine.at[:, pl.ds(512, 128)], gains_far, pair_send, pair_recv, 5, p.other_tp)
    gains_copy.start()
    gains_copy.wait()
    mine = attn_mine[:, pl.ds(512, 128)]
    lane = lax.broadcasted_iota(jnp.int32, (16, 128), 1) + 512
    attn_mine[:, pl.ds(512, 128)] = mine + jnp.where(lane == GAIN_ONE, gains_far[...], 0.0)


def backward(*arrays):
    dma = pltpu.SemaphoreType.DMA
    in_vmem, in_hbm = pl.BlockSpec(memory_space=VMEM), pl.BlockSpec(memory_space=ANY)
    wide, tall, low = (DPAD, 256), (256, DPAD), (2, HD, ROWS)
    return pl.pallas_call(
        backward_kernel,
        out_shape=[shape(wide, BF16), shape(wide, BF16), shape((16, ATTN_W), F32), shape((16, FFN_W), F32)],
        in_specs=[in_vmem, in_hbm, in_vmem, in_hbm, in_vmem, in_vmem, in_hbm] + [in_vmem] * 9,
        out_specs=[in_vmem] * 4,
        scratch_shapes=[
            VMEM((2, 3, DPAD, CHUNK), BF16),
            VMEM((FF_HERE // 128, 256, 128), BF16),
            VMEM(wide, BF16),
            VMEM(tall, BF16),
            VMEM(wide, F32),
            VMEM(wide, F32),
            VMEM(wide, BF16),
            VMEM(wide, BF16),
            VMEM(low, BF16),
            VMEM((2, 1, ROWS), F32),
            VMEM(low, F32),
            VMEM((HD, ROWS), BF16),
            VMEM((HD, ROWS), BF16),
            VMEM((2, 4, 4, 1, 256, 128), F32),
            VMEM((2, 4, 4, 1, 256, 128), BF16),
            VMEM((256, 128), F32),
            VMEM((QKV_W, 256), BF16),
            VMEM((2, 4, 4, 2, 16, FFN_W), BF16),
            VMEM((2, 4, 4, 2, 16, ATTN_W), BF16),
            VMEM((16, 128), F32),
            pltpu.SemaphoreType.REGULAR,
            dma((2, 3)),
            dma((2,)),
            dma((6,)),
            dma((6,)),
        ]
        + Scatter.scratch(2, 16, FFN_W)
        + Scatter.scratch(1, 256, 128)
        + Scatter.scratch(2, 16, ATTN_W),
        compiler_params=pltpu.CompilerParams(collective_id=1, has_side_effects=True, vmem_limit_bytes=VMEM_BYTES),
    )(*arrays)


def shards(
    inputs,
    positions,
    query_key_value_weight,
    query_key_value_bias,
    gain_attn,
    output_weight,
    gate_weight,
    up_weight,
    down_weight,
    gain_ffn,
    cotangent,
):
    me = lax.axis_index("seq") * 32 + lax.axis_index("ctx")
    select = jnp.asarray(slot_columns()[:, None] == np.arange(D)[None, :], BF16)
    bias_row = lax.dynamic_update_slice(jnp.zeros((1, GROUP), BF16), query_key_value_bias, (0, 9 * me))
    attn_row = jnp.concatenate(
        [
            jnp.concatenate([query_key_value_weight[:, 0], bias_row, jnp.zeros((1, GROUP), BF16)], 0),
            jnp.pad(jnp.stack([gain_attn, gain_ffn], 1), ((0, 2), (0, 62))),
        ],
        1,
    )
    out_row = jnp.pad(output_weight[0].T, ((0, 2), (0, 64)))
    ffn_row = jnp.pad(jnp.concatenate([gate_weight, up_weight, down_weight.T], 1), ((0, 2), (0, 0)))
    cosine, sine = rope_tables(positions[0])
    row = lax.axis_index("ctx") * 256 + jnp.arange(128, dtype=jnp.int32)
    doc = jnp.stack([jnp.tile((row - positions[0, :128])[None], (1, 7)), jnp.full((1, ROWS), 128, jnp.int32)])
    attn_full, ffn_full, *kept = forward(
        attn_row, out_row, ffn_row, inputs[0], cotangent[0], select, cosine, sine, doc
    )
    output, grad_inputs, attn, ffn = backward(
        attn_full, ffn_full.reshape(DPAD, FFN_W), *kept, cosine, sine, doc
    )
    return (
        mm_tn(output, select).astype(BF16)[None],
        mm_tn(grad_inputs, select).astype(BF16)[None],
        attn[:14, None, :GROUP],
        lax.dynamic_slice(attn, (14, 8 * me), (1, 8)),
        lax.dynamic_slice(attn, (14, 512 + me), (1, 1)),
        attn[:14, GAIN_ONE],
        attn[:14, QKV_W : QKV_W + GROUP_Q].T[None],
        ffn[:14, :FF_HERE],
        ffn[:14, FF_HERE : 2 * FF_HERE],
        ffn[:14, 2 * FF_HERE :].T,
        attn[:14, GAIN_TWO],
    )


def solution(mesh):
    both = ("seq", "ctx")
    return jax.shard_map(
        shards,
        mesh=mesh,
        in_specs=(
            P("seq", "ctx", None),
            P("seq", "ctx"),
            P(both, "tp", None),
            P("tp", both),
            P(both),
            P("tp", None, both),
            P(both, "tp"),
            P(both, "tp"),
            P("tp", both),
            P(both),
            P("seq", "ctx", None),
        ),
        out_specs=(
            P("seq", "ctx", None),
            P("seq", "ctx", None),
            P(both, "tp", None),
            P("tp", both),
            P("tp", both),
            P(both),
            P("tp", None, both),
            P(both, "tp"),
            P(both, "tp"),
            P("tp", both),
            P(both),
        ),
        check_vma=False,
    )
```

```python
import jax
import jax.numpy as jnp
import numpy as np
from jax import lax
from jax.experimental import pallas as pl
from jax.experimental.pallas import tpu as pltpu
from jax.sharding import PartitionSpec as P

MESH_ID = pl.DeviceIdType.MESH
ANY = pl.ANY
VMEM = pltpu.VMEM


class Place:
    def __init__(self):
        self.seq = lax.axis_index("seq")
        ctx = lax.axis_index("ctx")
        self.ctx = ctx
        self.tp = lax.axis_index("tp")
        self.core = ctx % 2
        core = self.core
        y, z = ctx // 8, (ctx // 2) % 4
        self.a = y * (1 - core) + z * core
        self.b = z * (1 - core) + y * core
        self.stride_a = 8 - 6 * core
        self.stride_b = 2 + 6 * core
        self.a_next = self.peer(1, 0)
        self.a_prev = self.peer(3, 0)
        self.b_next = self.peer(0, 1)
        self.b_prev = self.peer(0, 3)
        self.other_core = {"ctx": ctx + 1 - 2 * core}
        self.other_seq = {"seq": 1 - self.seq}
        self.mirror = {"ctx": 31 - ctx}
        self.other_tp = {"tp": 1 - self.tp}
        self.mirror_tp = {"ctx": 31 - ctx, "tp": 1 - self.tp}

    def peer(self, da, db):
        a, b = (self.a + da) % 4, (self.b + db) % 4
        return {"ctx": a * self.stride_a + b * self.stride_b + self.core}


def greet(peers):
    barrier = pltpu.get_barrier_semaphore()
    for peer in peers:
        pl.semaphore_signal(barrier, inc=1, device_id=peer, device_id_type=MESH_ID)
    pl.semaphore_wait(barrier, len(peers))


def remote(src, dst, send, recv, index, peer):
    return pltpu.make_async_remote_copy(
        src_ref=src,
        dst_ref=dst,
        send_sem=send.at[index],
        recv_sem=recv.at[index],
        device_id=peer,
        device_id_type=MESH_ID,
    )


GATHER_SEMS = 15


class Gather:
    def __init__(self, place, own, full, send, recv, local):
        self.p, self.own, self.full = place, own, full
        self.send, self.recv, self.local = send, recv, local
        self.pair = full.shape[3] == 2
        self.started = []

    def go(self, src, dst, index, peer):
        copy = remote(src, dst, self.send, self.recv, index, peer)
        copy.start()
        self.started.append(copy)

    def got(self, ref, index):
        remote(ref, ref, self.send, self.recv, index, self.p.a_next).wait_recv()

    def half(self, b, a, which):
        ref = self.full.at[self.p.core, b, a]
        if self.pair:
            return ref.at[which]
        rows = self.full.shape[4] // 2
        return ref.at[0, pl.ds(which * rows, rows)]

    def begin(self):
        p = self.p
        slot = self.full.at[p.core, p.b, p.a, p.seq if self.pair else 0]
        self.mine = pltpu.make_async_copy(self.own, slot, self.local)
        self.mine.start()
        if self.pair:
            self.go(self.own, slot, 0, p.other_seq)

    def first(self):
        p = self.p
        self.mine.wait()
        if self.pair:
            self.got(self.full.at[p.core, p.b, p.a, 1 - p.seq], 0)
        block = self.full.at[p.core, p.b, p.a]
        self.go(block, block, 1, p.a_next)
        self.go(block, block, 2, p.a_prev)

    def second(self):
        p = self.p
        down, up = (p.a + 3) % 4, (p.a + 1) % 4
        self.got(self.full.at[p.core, p.b, down], 1)
        half = self.half(p.b, down, 0)
        self.go(half, half, 3, p.a_next)
        self.got(self.full.at[p.core, p.b, up], 2)
        half = self.half(p.b, up, 1)
        self.go(half, half, 4, p.a_prev)

    def third_near(self):
        p = self.p
        far = (p.a + 2) % 4
        self.got(self.half(p.b, far, 0), 3)
        self.got(self.half(p.b, far, 1), 4)
        row = self.full.at[p.core, p.b]
        self.go(row.at[pl.ds(0, 2)], row.at[pl.ds(0, 2)], 5, p.b_next)
        self.go(row.at[pl.ds(2, 2)], row.at[pl.ds(2, 2)], 6, p.b_prev)
        self.go(row, row, 9, p.other_core)

    def third_rest(self):
        p = self.p
        row = self.full.at[p.core, p.b]
        self.go(row.at[pl.ds(2, 2)], row.at[pl.ds(2, 2)], 13, p.b_next)
        self.go(row.at[pl.ds(0, 2)], row.at[pl.ds(0, 2)], 14, p.b_prev)

    def third(self):
        self.third_near()
        self.third_rest()

    def fourth_near(self):
        p = self.p
        half = self.full.at[p.core, (p.b + 3) % 4, pl.ds(0, 2)]
        self.got(half, 5)
        self.go(half, half, 7, p.b_next)
        half = self.full.at[p.core, (p.b + 1) % 4, pl.ds(2, 2)]
        self.got(half, 6)
        self.go(half, half, 8, p.b_prev)

    def fourth_rest(self):
        p = self.p
        down, up = (p.b + 3) % 4, (p.b + 1) % 4
        self.got(self.full.at[p.core, down, pl.ds(2, 2)], 13)
        row = self.full.at[p.core, down]
        self.go(row, row, 10, p.other_core)
        self.got(self.full.at[p.core, up, pl.ds(0, 2)], 14)
        row = self.full.at[p.core, up]
        self.go(row, row, 11, p.other_core)

    def fourth(self):
        self.fourth_near()
        self.fourth_rest()

    def fifth(self):
        p = self.p
        far = (p.b + 2) % 4
        self.got(self.full.at[p.core, far, pl.ds(0, 2)], 7)
        self.got(self.full.at[p.core, far, pl.ds(2, 2)], 8)
        block = self.full.at[p.core, far]
        self.go(block, block, 12, p.other_core)

    def finish(self):
        for step in (0, 3, 1, 2):
            self.from_core(step)
        self.sent()

    def from_core(self, step):
        p = self.p
        self.got(self.full.at[1 - p.core, (p.a + step) % 4], {0: 9, 3: 10, 1: 11, 2: 12}[step])

    def sent(self):
        for copy in self.started:
            copy.wait_send()

    def peers(self):
        p = self.p
        found = [p.a_next, p.a_prev, p.b_next, p.b_prev, p.other_core]
        return found + ([p.other_seq] if self.pair else [])


def add_into(target, extra, count):
    def body(k, carry):
        total = target[k].astype(jnp.float32) + extra[k].astype(jnp.float32)
        target[k] = total.astype(target.dtype)
        return carry

    lax.fori_loop(0, count, body, 0)


SCATTER_SEMS = 13


class Scatter:
    @staticmethod
    def scratch(seqs, rows, width):
        bf16 = jnp.bfloat16
        return [
            VMEM((4, 4, seqs, rows, width), bf16),
            VMEM((2, 2, seqs, rows, width), bf16),
            VMEM((1, rows, width), bf16),
            pltpu.SemaphoreType.DMA((SCATTER_SEMS,)),
            pltpu.SemaphoreType.DMA((SCATTER_SEMS,)),
            pltpu.SemaphoreType.REGULAR,
        ]

    def __init__(self, place, part, scratch):
        self.p, self.part = place, part
        self.sums, self.far_b, self.across, self.send, self.recv, self.free = scratch
        self.seqs, self.rows = part.shape[3], part.shape[4]
        spare = part.at[1 - place.core]
        self.near_b = [spare.at[side] for side in range(2)]
        self.near_a = [spare.at[2, side] for side in range(2)]
        self.far_a = [spare.at[2, 2 + side, pl.ds(0, 1)] for side in range(2)]
        if self.seqs == 1:
            self.far_a = [ref.at[:, pl.ds(0, self.rows // 2)] for ref in self.far_a]
        self.started = []

    go = Gather.go
    got = Gather.got

    def half(self, b, a, which):
        ref = self.sums.at[b, a]
        if self.seqs == 2:
            return ref.at[pl.ds(which, 1)]
        rows = self.rows // 2
        return ref.at[:, pl.ds(which * rows, rows)]

    def to_core(self, step):
        p = self.p
        slot = (p.a + step) % 4
        self.go(self.part.at[1 - p.core, slot], self.sums.at[slot], step, p.other_core)

    def begin(self):
        for step in (2, 1, 3, 0):
            self.to_core(step)

    def add_core(self, step):
        p = self.p
        slot = (p.b + step) % 4
        self.got(self.sums.at[slot], step)
        for a in range(4):
            add_into(self.sums.at[slot, a], self.part.at[p.core, slot, a], self.seqs)

    def first(self):
        p = self.p
        self.add_core(2)
        far = (p.b + 2) % 4
        self.go(self.sums.at[far, pl.ds(0, 2)], self.far_b.at[0], 4, p.b_next)
        self.go(self.sums.at[far, pl.ds(2, 2)], self.far_b.at[1], 5, p.b_prev)

    def second(self):
        p = self.p
        up, down = (p.b + 1) % 4, (p.b + 3) % 4
        for copy in self.started[:4]:
            copy.wait_send()
        self.started = self.started[4:]
        ring = (p.a_next, p.a_prev, p.b_next, p.b_prev)
        for peer in ring:
            pl.semaphore_signal(self.free, inc=1, device_id=peer, device_id_type=MESH_ID)
        self.add_core(1)
        self.add_core(3)
        pl.semaphore_wait(self.free, len(ring))
        self.got(self.far_b.at[0], 4)
        for a in range(2):
            add_into(self.sums.at[up, a], self.far_b.at[0, a], self.seqs)
        self.go(self.sums.at[up], self.near_b[0], 6, p.b_next)
        self.got(self.far_b.at[1], 5)
        for a in range(2):
            add_into(self.sums.at[down, a + 2], self.far_b.at[1, a], self.seqs)
        self.go(self.sums.at[down], self.near_b[1], 7, p.b_prev)

    def third(self):
        p = self.p
        self.add_core(0)
        for side in range(2):
            self.got(self.near_b[side], 6 + side)
            for a in range(4):
                add_into(self.sums.at[p.b, a], self.near_b[side].at[a], self.seqs)
        far = (p.a + 2) % 4
        self.go(self.half(p.b, far, 0), self.far_a[0], 8, p.a_next)
        self.go(self.half(p.b, far, 1), self.far_a[1], 9, p.a_prev)

    def fourth(self):
        p = self.p
        up, down = (p.a + 1) % 4, (p.a + 3) % 4
        self.got(self.far_a[0], 8)
        add_into(self.half(p.b, up, 0), self.far_a[0], 1)
        self.go(self.sums.at[p.b, up], self.near_a[0], 10, p.a_next)
        self.got(self.far_a[1], 9)
        add_into(self.half(p.b, down, 1), self.far_a[1], 1)
        self.go(self.sums.at[p.b, down], self.near_a[1], 11, p.a_prev)

    def fifth(self):
        p = self.p
        for side in range(2):
            self.got(self.near_a[side], 10 + side)
            add_into(self.sums.at[p.b, p.a], self.near_a[side], self.seqs)
        if self.seqs == 2:
            self.go(self.sums.at[p.b, p.a, pl.ds(1 - p.seq, 1)], self.across, 12, p.other_seq)

    def finish(self, out):
        p = self.p
        if self.seqs == 2:
            self.got(self.across, 12)
            out[...] = self.sums[p.b, p.a, p.seq].astype(jnp.float32) + self.across[0].astype(jnp.float32)
        else:
            out[...] = self.sums[p.b, p.a, 0].astype(jnp.float32)
        for copy in self.started:
            copy.wait_send()

    def peers(self):
        p = self.p
        found = [p.a_next, p.a_prev, p.b_next, p.b_prev, p.other_core]
        return found + ([p.other_seq] if self.seqs == 2 else [])


NEGATIVE = -1e30
HD = 64
ROWS = 896
TURNS = 33
F32, BF16 = jnp.float32, jnp.bfloat16


def mm(left, right):
    return jnp.dot(left, right, preferred_element_type=F32)


def mm_nt(left, right):
    return lax.dot_general(left, right, (((1,), (1,)), ((), ())), preferred_element_type=F32)


def block_of(core, b, a):
    y = a * (1 - core) + b * core
    z = b * (1 - core) + a * core
    return y * 8 + z * 2 + core


class Turn:
    def __init__(self, ctx, segment, slot):
        self.segment, self.slot = segment, slot
        self.block = block_of(*slot)
        count = (ctx + 1) * (1 - segment) + (32 - ctx) * segment
        self.first_row = (count - 1) * 256 + 128 * segment
        self.needed = self.block < count
        self.hidden = (self.block == 0) | (self.block == count - 1)

    def scores(self, scores, doc_ref, hidden, part=slice(0, ROWS)):
        if not hidden:
            return scores
        key = lax.broadcasted_iota(jnp.int32, scores.shape, 0) + self.block * 256
        row = (lax.broadcasted_iota(jnp.int32, scores.shape, 1) + part.start) % 128 + self.first_row
        visible = (key <= row) & (key >= doc_ref[self.segment, :, part])
        return jnp.where(visible, scores, NEGATIVE)


def run_row(ctx, core, b, step):
    def body(n, carry):
        turn = Turn(ctx, n // 4, (core, b, n % 4))
        pl.when(turn.needed & turn.hidden)(lambda: step(turn, True))
        pl.when(turn.needed & jnp.logical_not(turn.hidden))(lambda: step(turn, False))
        return carry

    lax.fori_loop(0, 8, body, 0)


def attend_step(turn, hidden, kv_ref, q_ref, doc_ref, m_ref, l_ref, acc_ref):
    core, b, a = turn.slot
    segment = turn.segment
    kv = kv_ref[core, b, a, 0]
    keys, values_t = kv[:, :HD], kv[:, HD:].T
    q, old_max, old_sum, old_acc = q_ref[segment], m_ref[segment], l_ref[segment], acc_ref[segment]
    parts = [slice(start, min(start + 256, ROWS)) for start in range(0, ROWS, 256)]
    products = [turn.scores(mm(keys, q[:, part]), doc_ref, hidden, part) for part in parts]
    results = []
    for part, scores in zip(parts, products):
        old = old_max[:, part]
        new = jnp.maximum(old, jnp.max(scores, 0, keepdims=True))
        probs = jnp.exp(scores - new)
        keep = jnp.exp(old - new)
        total = old_sum[:, part] * keep + jnp.sum(probs, 0, keepdims=True)
        results.append((new, total, old_acc[:, part] * keep + mm(values_t, probs.astype(BF16))))
    for part, (new, total, acc) in zip(parts, results):
        m_ref[segment, :, part] = new
        l_ref[segment, :, part] = total
        acc_ref[segment, :, part] = acc


def attend_back_step(turn, hidden, kv_ref, q_ref, doc_ref, do_ref, lse_ref, delta_ref, dq_ref, dkv_ref):
    core, b, a = turn.slot
    segment = turn.segment
    kv = kv_ref[core, b, a, 0]
    keys, values = kv[:, :HD], kv[:, HD:]
    q, do = q_ref[segment], do_ref[segment]
    scores = turn.scores(mm(keys, q), doc_ref, hidden)
    probs = jnp.exp(scores - lse_ref[segment])
    dscores = (probs * (mm(values, do) - delta_ref[segment])).astype(BF16)
    dq_ref[segment] += mm(keys.T, dscores)
    dkv_ref[core, b, a, 0] += jnp.concatenate([mm_nt(dscores, q), mm_nt(probs.astype(BF16), do)], 1)


D, DPAD, FF_HERE, GROUP, GROUP_Q = 896, 1024, 2432, 576, 448
QKV_W, OUT_W, FFN_W = 640, 512, 3 * 2432
ATTN_W = QKV_W + OUT_W
GAIN_ONE, GAIN_TWO = 576, 577
EPS_VALUE = 1e-06
THETA = 1000000.0
VMEM_BYTES = 62 << 20
CHUNK = 256
DEPTH = 3


def slot_columns():
    index = np.arange(64)
    seq, y, z, core = index // 32, (index // 8) % 4, (index // 2) % 4, index % 2
    a, b = np.where(core == 0, y, z), np.where(core == 0, z, y)
    slot = ((core * 4 + b) * 4 + a) * 2 + seq
    columns = np.full((64, 16), -1)
    columns[slot, :14] = index[:, None] * 14 + np.arange(14)
    return columns.reshape(-1)


def rope_tables(positions):
    exponents = jnp.arange(HD // 2, dtype=F32) * (2.0 / HD)
    freqs = THETA ** (-exponents)
    angles = freqs[:, None] * positions.astype(F32)[None, :]
    angles = jnp.concatenate([angles, angles], 0)
    return jnp.cos(angles), jnp.sin(angles)


def rotate(values, cosine, sine):
    turned = jnp.concatenate([-values[32:], values[:32]], 0)
    return values * cosine + turned * sine


def rotate_back(grads, cosine, sine):
    sined = grads * sine
    return grads * cosine + jnp.concatenate([sined[32:], -sined[:32]], 0)


def inv_rms(values):
    return lax.rsqrt(jnp.sum(values * values, 0, keepdims=True) * (1.0 / D) + EPS_VALUE)


def norm_back(values, inverse, scaled):
    mean = jnp.sum(scaled * values, 0, keepdims=True) * (1.0 / D)
    return inverse * scaled - values * inverse**3 * mean


def head(index):
    return pl.ds(index * HD, HD)


def lanes(index):
    return pl.ds(index * 128, 128)


def flat(ref, start, width):
    if not isinstance(start, int):
        start = pl.multiple_of(start, 128)
    return ref[:, :, :, :, :, pl.ds(start, width)].reshape(DPAD, width)


def unflat(value):
    return value.reshape(2, 4, 4, 2, 16, value.shape[-1])


def shape(dims, dtype):
    return jax.ShapeDtypeStruct(dims, dtype)


def forward_kernel(
    attn_row,
    out_row,
    ffn_row,
    x_in,
    ct_in,
    select,
    cosine,
    sine,
    doc,
    attn_out,
    ffn_full,
    w_out,
    x_kept,
    ct_kept,
    tokens_kept,
    normed_kept,
    q_kept,
    kv_kept,
    attended,
    lse,
    att,
    middle,
    attn_full,
    x_out,
    ct_out,
    ct_tokens,
    normed_out,
    q_both,
    kv_full,
    keep_sems,
    outs_mine,
    outs_full,
    q_send,
    kv_mine,
    att_send,
    att_far,
    m_ref,
    l_ref,
    acc_ref,
    pair_send,
    pair_recv,
    *sems,
):
    p = Place()
    kept = []

    def keep(ref, out):
        copy = pltpu.make_async_copy(ref, out, keep_sems.at[len(kept)])
        copy.start()
        kept.append(copy)

    attn = Gather(p, attn_row, attn_full, *sems[0:3])
    ffn = Gather(p, ffn_row, ffn_full, *sems[3:6])
    keys = Gather(p, kv_mine, kv_full, *sems[6:9])
    outs = Gather(p, outs_mine, outs_full, *sems[9:12])
    greet(attn.peers() + [p.mirror, p.other_tp, p.mirror_tp])
    attn.begin()
    own_out = pl.ds(pl.multiple_of(p.tp * OUT_W, 128), OUT_W)
    out_copy = remote(out_row, outs_mine.at[:, own_out], pair_send, pair_recv, 0, p.other_tp)
    out_copy.start()
    ffn.begin()
    outs_mine[:, own_out] = out_row[...]
    x = mm_nt(select[...], x_in[...])
    x_out[...] = x
    keep(x_out, x_kept)
    attn.first()
    ct_out[...] = mm_nt(select[...], ct_in[...]).astype(BF16)
    keep(ct_out, ct_kept)
    attn.second()
    ct_tokens[...] = mm_nt(ct_in[...], select[...]).astype(BF16)
    keep(ct_tokens, tokens_kept)
    attn.third()
    ffn.first()
    m_ref[...] = jnp.full(m_ref.shape, NEGATIVE, F32)
    l_ref[...] = jnp.zeros(l_ref.shape, F32)
    acc_ref[...] = jnp.zeros(acc_ref.shape, F32)
    attn.fourth()
    attn.fifth()
    ffn.second()
    out_copy.wait()
    attn.finish()
    outs.begin()
    keep(attn_full, attn_out)

    gain = flat(attn_full, 512, 128)[:, GAIN_ONE - 512 : GAIN_ONE - 511].astype(F32)
    row = lax.broadcasted_iota(jnp.int32, (DPAD, 256), 0)
    x = x_out[...]
    normed = jnp.where(row % 16 == 14, 1.0, x * inv_rms(x) * gain)
    normed_out[...] = normed.astype(BF16)
    keep(normed_out, normed_kept)
    outs.first()
    mixed = mm(normed.T.astype(BF16), flat(attn_full, 0, QKV_W)).T
    outs.second()
    key = rotate(mixed[GROUP_Q : GROUP_Q + HD], cosine[...], sine[...])
    kv_mine[...] = jnp.concatenate([key, mixed[GROUP_Q + HD : GROUP]], 0).T.astype(BF16)
    keys.begin()
    keys.first()
    for h in range(7):
        query = rotate(mixed[64 * h : 64 * h + 64], cosine[...], sine[...]).astype(BF16).astype(F32) * 0.125
        q_both[0, :, lanes(h)] = query[:, :128].astype(BF16)
        q_send[:, lanes(h)] = query[:, 128:].astype(BF16)
    q_copy = remote(q_send, q_both.at[1], pair_send, pair_recv, 1, p.mirror)
    q_copy.start()
    keys.second()
    outs.third()
    keys.third()
    q_copy.wait()
    keep(q_both, q_kept)

    def step(turn, hidden):
        attend_step(turn, hidden, kv_full, q_both, doc, m_ref, l_ref, acc_ref)

    run_row(p.ctx, p.core, p.b, step)
    outs.fourth()
    keys.fourth()
    run_row(p.ctx, p.core, (p.b + 3) % 4, step)
    outs.fifth()
    keys.fifth()
    ffn.third_near()
    ffn.third_rest()
    run_row(p.ctx, p.core, (p.b + 1) % 4, step)
    run_row(p.ctx, p.core, (p.b + 2) % 4, step)
    for ahead in (0, 3, 1, 2):
        keys.from_core(ahead)
        if ahead == 1:
            ffn.fourth_near()
        run_row(p.ctx, 1 - p.core, (p.a + ahead) % 4, step)
    keys.sent()
    keep(kv_full, kv_kept)
    attended[...] = acc_ref[...] / l_ref[...]
    att_send[...] = attended[...].astype(BF16)
    att_copies = [
        remote(att_send.at[1], att_far.at[0], pair_send, pair_recv, 2, p.mirror),
        remote(att_send.at[0], att_far.at[1], pair_send, pair_recv, 3, p.other_tp),
        remote(att_send.at[1], att_far.at[2], pair_send, pair_recv, 4, p.mirror_tp),
    ]
    for copy in att_copies:
        copy.start()
    lse[...] = m_ref[...] + jnp.log(l_ref[...])
    outs.finish()
    ffn.fourth_rest()
    w_out[...] = flat(outs_full, p.tp * OUT_W, OUT_W)
    att[:, pl.ds(GROUP_Q, 64), :] = jnp.zeros((2, 64, 256), BF16)
    for h in range(7):
        att[p.tp, head(h), lanes(0)] = att_send[0, :, lanes(h)]
    for copy in att_copies:
        copy.wait()
    for h in range(7):
        att[p.tp, head(h), lanes(1)] = att_far[0, :, lanes(h)]
        att[1 - p.tp, head(h), lanes(0)] = att_far[1, :, lanes(h)]
        att[1 - p.tp, head(h), lanes(1)] = att_far[2, :, lanes(h)]
    middle[...] = x_out[...] + mm(flat(outs_full, 0, 2 * OUT_W), att[...].reshape(2 * OUT_W, 256))
    ffn.fifth()
    ffn.finish()
    for copy in kept:
        copy.wait()


def forward(*arrays):
    dma = pltpu.SemaphoreType.DMA
    gather_sems = [dma((GATHER_SEMS,)), dma((GATHER_SEMS,)), dma]
    in_vmem, in_hbm = pl.BlockSpec(memory_space=VMEM), pl.BlockSpec(memory_space=ANY)
    return pl.pallas_call(
        forward_kernel,
        out_shape=[
            shape((2, 4, 4, 2, 16, QKV_W), BF16),
            shape((2, 4, 4, 2, 16, FFN_W), BF16),
            shape((DPAD, OUT_W), BF16),
            shape((DPAD, 256), F32),
            shape((DPAD, 256), BF16),
            shape((256, DPAD), BF16),
            shape((DPAD, 256), BF16),
            shape((2, HD, ROWS), BF16),
            shape((2, 4, 4, 1, 256, 128), BF16),
            shape((2, HD, ROWS), F32),
            shape((2, 1, ROWS), F32),
            shape((2, OUT_W, 256), BF16),
            shape((DPAD, 256), F32),
        ],
        in_specs=[in_vmem, in_vmem, in_hbm] + [in_vmem] * 6,
        out_specs=[in_hbm, in_hbm, in_vmem] + [in_hbm] * 6 + [in_vmem] * 4,
        scratch_shapes=[
            VMEM((2, 4, 4, 2, 16, QKV_W), BF16),
            VMEM((DPAD, 256), F32),
            VMEM((DPAD, 256), BF16),
            VMEM((256, DPAD), BF16),
            VMEM((DPAD, 256), BF16),
            VMEM((2, HD, ROWS), BF16),
            VMEM((2, 4, 4, 1, 256, 128), BF16),
            dma((7,)),
            VMEM((16, 2 * OUT_W), BF16),
            VMEM((2, 4, 4, 2, 16, 2 * OUT_W), BF16),
            VMEM((HD, ROWS), BF16),
            VMEM((256, 128), BF16),
            VMEM((2, HD, ROWS), BF16),
            VMEM((3, HD, ROWS), BF16),
            VMEM((2, 1, ROWS), F32),
            VMEM((2, 1, ROWS), F32),
            VMEM((2, HD, ROWS), F32),
            dma((5,)),
            dma((5,)),
        ]
        + gather_sems * 4,
        compiler_params=pltpu.CompilerParams(collective_id=0, has_side_effects=True, vmem_limit_bytes=VMEM_BYTES),
    )(*arrays)


def tile_of(index):
    return index // 16, (index // 4) % 4, index % 4, 0


def ffn_chunk(weights, slot, width, tile, tokens, ct_tokens, gate_kept, up_kept, hidden_kept, out_sum, grad_sum):
    w_gate, w_up, w_down = (weights[slot, k, :, pl.ds(0, width)] for k in range(3))
    gate, up = mm(tokens[...], w_gate), mm(tokens[...], w_up)
    grad_hidden = mm(ct_tokens[...], w_down)
    sigmoid = jax.nn.sigmoid(gate)
    silu = gate * sigmoid
    hidden = (silu * up).astype(BF16)
    grad_up = (grad_hidden * silu).astype(BF16)
    grad_gate = (grad_hidden * up * sigmoid * (1.0 + gate * (1.0 - sigmoid))).astype(BF16)
    grad_sum[...] += mm_nt(w_gate, grad_gate) + mm_nt(w_up, grad_up)
    out_sum[...] += mm_nt(w_down, hidden)
    for k in range(width // 128):
        part = slice(128 * k, 128 * k + 128)
        gate_kept[tile_of(tile + k)] = grad_gate[:, part]
        up_kept[tile_of(tile + k)] = grad_up[:, part].astype(F32)
        hidden_kept[tile + k] = hidden[:, part]


def ffn_weight_grads(tile, tiles, normed, ct, gate_kept, up_kept, hidden_kept, part):
    places = [tile_of(tile + k) for k in range(tiles)]
    pairs = (
        (normed, [gate_kept[place] for place in places]),
        (normed, [up_kept[place].astype(BF16) for place in places]),
        (ct, [hidden_kept[tile + k] for k in range(tiles)]),
    )
    for k, (left, right) in enumerate(pairs):
        start = k * FF_HERE + tile * 128
        if not isinstance(start, int):
            start = pl.multiple_of(start, 128)
        product = mm(left[...], jnp.concatenate(right, 1) if tiles > 1 else right[0])
        part[:, :, :, :, :, pl.ds(start, tiles * 128)] = unflat(product.astype(BF16))


def backward_kernel(
    attn_kept,
    ffn_full,
    w_out_kept,
    x_kept,
    ct_kept,
    ct_tokens,
    normed_kept,
    q_kept,
    kv_kept,
    attended_kept,
    lse,
    att_kept,
    middle,
    cosine,
    sine,
    doc,
    select,
    output,
    grad_inputs,
    attn_mine,
    ffn_mine,
    attn_full,
    w_out,
    ct,
    q_both,
    kv_full,
    attended,
    att,
    late_sems,
    weights,
    hidden_kept,
    normed_ffn,
    tokens,
    out_sum,
    grad_sum,
    out_far,
    grad_far,
    do_both,
    delta,
    dq,
    dq_send,
    dq_far,
    dkv,
    kv_part,
    kv_mine,
    grad_mixed,
    ffn_part,
    attn_part,
    gains_far,
    grad_free,
    weight_sems,
    kept_sems,
    pair_send,
    pair_recv,
    *scratch,
):
    p = Place()
    out_send, grad_send, do_send = weights.at[2, 0], weights.at[2, 1], dq_send
    ffn = Scatter(p, ffn_part, scratch[0:6])
    keys = Scatter(p, kv_part, scratch[6:12])
    attn = Scatter(p, attn_part, scratch[12:18])

    def load(index, slot, width):
        start = index * CHUNK
        copies = []
        for k in range(3):
            place = pl.ds(pl.multiple_of(k * FF_HERE + start, 128), width)
            copies.append(
                pltpu.make_async_copy(
                    ffn_full.at[:, place], weights.at[slot, k, :, pl.ds(0, width)], weight_sems.at[slot, k]
                )
            )
        return copies

    pairs = (
        (attn_kept, attn_full),
        (ct_kept, ct),
        (w_out_kept, w_out),
        (q_kept, q_both),
        (kv_kept, kv_full),
        (attended_kept, attended),
        (att_kept, att),
    )
    late = [pltpu.make_async_copy(src, dst, late_sems.at[k]) for k, (src, dst) in enumerate(pairs)]
    late[0].start()
    for index in range(DEPTH - 1):
        for copy in load(index, index, CHUNK):
            copy.start()
    for copy in late[1:]:
        copy.start()
    greet(ffn.peers() + [p.mirror, p.other_tp])
    ffn_kept = (kv_part, dkv, hidden_kept)
    late[0].wait()
    gain_two = flat(attn_full, 512, 128)[:, GAIN_TWO - 512 : GAIN_TWO - 511].astype(F32)
    mid = middle[...]
    inverse = inv_rms(mid)
    scaled = mid * inverse * gain_two
    normed_ffn[...] = scaled.astype(BF16)
    tokens[...] = scaled.T.astype(BF16)
    out_sum[...] = jnp.zeros(out_sum.shape, F32)
    grad_sum[...] = jnp.zeros(grad_sum.shape, F32)
    chunks, tail, tiles = FF_HERE // CHUNK, FF_HERE % CHUNK, CHUNK // 128

    def chunk_body(index, carry):
        slot, ahead = index % DEPTH, index + DEPTH - 1
        for copy in load(index, slot, CHUNK):
            copy.wait()

        @pl.when(ahead < chunks)
        def _():
            for copy in load(ahead, ahead % DEPTH, CHUNK):
                copy.start()

        @pl.when(ahead == chunks)
        def _():
            for copy in load(chunks, chunks % DEPTH, tail):
                copy.start()

        ffn_chunk(weights, slot, CHUNK, index * tiles, tokens, ct_tokens, *ffn_kept, out_sum, grad_sum)
        return carry

    lax.fori_loop(0, chunks, chunk_body, 0)
    for copy in load(chunks, chunks % DEPTH, tail):
        copy.wait()
    ffn_chunk(weights, chunks % DEPTH, tail, chunks * tiles, tokens, ct_tokens, *ffn_kept, out_sum, grad_sum)
    grad_send[...] = grad_sum[...].astype(BF16)
    grad_copy = remote(grad_send, grad_far, pair_send, pair_recv, 0, p.other_tp)
    grad_copy.start()

    for copy in late[1:]:
        copy.wait()

    def grads_body(index, carry):
        ffn_weight_grads(index * tiles, tiles, normed_ffn, ct, *ffn_kept, ffn_part)
        return carry

    lax.fori_loop(0, chunks, grads_body, 0)
    ffn_weight_grads(chunks * tiles, tail // 128, normed_ffn, ct, *ffn_kept, ffn_part)
    ffn.begin()
    out_send[...] = out_sum[...].astype(BF16)
    x, normed, grad_middle = out_sum, normed_ffn, grad_sum
    kept = [
        pltpu.make_async_copy(x_kept, x, kept_sems.at[0]),
        pltpu.make_async_copy(normed_kept, normed, kept_sems.at[1]),
    ]
    columns = [pl.ds(start, min(CHUNK, D - start)) for start in range(0, D, CHUNK)]
    picks = [weights.at[k // 3, k % 3, :, pl.ds(0, column.size)] for k, column in enumerate(columns)]
    for k, column in enumerate(columns):
        kept.append(pltpu.make_async_copy(select.at[:, column], picks[k], kept_sems.at[2 + k]))

    def put_features(out, value):
        value = value.T.astype(BF16)
        for column, pick in zip(columns, picks):
            out[:, column] = mm(value, pick[...]).astype(BF16)

    for copy in kept:
        copy.start()
    dq[...] = jnp.zeros(dq.shape, F32)
    dkv[...] = jnp.zeros(dkv.shape, F32)
    grad_copy.wait()
    out_copy = remote(out_send, out_far, pair_send, pair_recv, 1, p.other_tp)
    out_copy.start()
    mid = middle[...]
    inverse = inv_rms(mid)
    grad_normed = grad_send[...].astype(F32) + grad_far[...].astype(F32)
    pl.semaphore_signal(grad_free, inc=1, device_id=p.other_tp, device_id_type=MESH_ID)
    gain_two_grad = jnp.sum(grad_normed * mid * inverse, 1, keepdims=True)
    grad_mid = ct[...].astype(F32) + norm_back(mid, inverse, grad_normed * gain_two)
    grad_middle[...] = grad_mid
    grad_att = mm(grad_mid.T.astype(BF16), w_out[...]).T
    for h in range(7):
        do_both[0, :, lanes(h)] = grad_att[64 * h : 64 * h + 64, :128].astype(BF16)
        do_send[:, lanes(h)] = grad_att[64 * h : 64 * h + 64, 128:].astype(BF16)
    do_copy = remote(do_send, do_both.at[1], pair_send, pair_recv, 2, p.mirror)
    do_copy.start()
    ffn.first()
    do_copy.wait()
    delta[...] = jnp.sum(do_both[...].astype(F32) * attended[...], 1, keepdims=True)

    def step(turn, hidden):
        attend_back_step(turn, hidden, kv_full, q_both, doc, do_both, lse, delta, dq, dkv)

    def far_row(ahead):
        slot = (p.a + ahead) % 4
        run_row(p.ctx, 1 - p.core, slot, step)
        kv_part[1 - p.core, slot] = dkv[1 - p.core, slot].astype(BF16)
        keys.to_core(ahead)

    def own_row(ahead):
        slot = (p.b + ahead) % 4
        run_row(p.ctx, p.core, slot, step)
        kv_part[p.core, slot] = dkv[p.core, slot].astype(BF16)

    far_row(2)
    far_row(1)
    ffn.second()
    far_row(3)
    far_row(0)
    own_row(2)
    keys.first()
    own_row(1)
    own_row(3)
    keys.second()
    own_row(0)
    dq_send[...] = dq[1].astype(BF16)
    dq_copy = remote(dq_send, dq_far, pair_send, pair_recv, 3, p.mirror)
    dq_copy.start()
    out_copy.wait()
    for copy in kept:
        copy.wait()
    put_features(output, middle[...] + (out_send[...].astype(F32) + out_far[...].astype(F32)))
    keys.third()
    ffn.third()
    attn_part[:, :, :, :, :, pl.ds(QKV_W, OUT_W)] = unflat(
        mm_nt(grad_middle[...].astype(BF16), att[p.tp]).astype(BF16)
    )
    keys.fourth()
    keys.fifth()
    ffn.fourth()
    keys.finish(kv_mine)
    dq_copy.wait()
    grad_mixed[pl.ds(GROUP, QKV_W - GROUP), :] = jnp.zeros((QKV_W - GROUP, 256), BF16)
    for h in range(7):
        far = dq_far[:, lanes(h)].astype(F32)
        near = dq[0, :, lanes(h)]
        grad_query = jnp.concatenate([near, far], 1) * 0.125
        grad_mixed[head(h), :] = rotate_back(grad_query, cosine[...], sine[...]).astype(BF16)
    grad_kv = kv_mine[...].T
    grad_mixed[head(7), :] = rotate_back(grad_kv[:HD], cosine[...], sine[...]).astype(BF16)
    grad_mixed[head(8), :] = grad_kv[HD:].astype(BF16)
    w_qkv = flat(attn_full, 0, QKV_W)
    grad_normed = mm(w_qkv, grad_mixed[...])
    grad_send[...] = grad_normed.astype(BF16)
    pl.semaphore_wait(grad_free, 1)
    grad_copy = remote(grad_send, grad_far, pair_send, pair_recv, 4, p.other_tp)
    grad_copy.start()
    value = x[...]
    inverse = inv_rms(value)
    gain_one_grad = jnp.sum(grad_normed * value * inverse, 1, keepdims=True)
    grad_qkv = mm_nt(normed[...], grad_mixed[...])
    lane = lax.broadcasted_iota(jnp.int32, grad_qkv.shape, 1)
    grad_qkv = jnp.where(lane == GAIN_ONE, gain_one_grad, jnp.where(lane == GAIN_TWO, gain_two_grad, grad_qkv))
    attn_part[:, :, :, :, :, pl.ds(0, QKV_W)] = unflat(grad_qkv.astype(BF16))
    attn.begin()
    attn.first()
    ffn.fifth()
    attn.second()
    grad_copy.wait()
    gain_one = flat(attn_full, 512, 128)[:, GAIN_ONE - 512 : GAIN_ONE - 511].astype(F32)
    scaled = (grad_send[...].astype(F32) + grad_far[...].astype(F32)) * gain_one
    put_features(grad_inputs, grad_middle[...] + norm_back(value, inverse, scaled))
    attn.third()
    attn.fourth()
    attn.fifth()
    attn.finish(attn_mine)
    gains_copy = remote(attn_mine.at[:, pl.ds(512, 128)], gains_far, pair_send, pair_recv, 5, p.other_tp)
    gains_copy.start()
    ffn.finish(ffn_mine)
    gains_copy.wait()
    mine = attn_mine[:, pl.ds(512, 128)]
    lane = lax.broadcasted_iota(jnp.int32, (16, 128), 1) + 512
    attn_mine[:, pl.ds(512, 128)] = mine + jnp.where(lane == GAIN_ONE, gains_far[...], 0.0)


def backward(*arrays):
    dma = pltpu.SemaphoreType.DMA
    in_vmem, in_hbm = pl.BlockSpec(memory_space=VMEM), pl.BlockSpec(memory_space=ANY)
    wide, tall, low = (DPAD, 256), (256, DPAD), (2, HD, ROWS)
    return pl.pallas_call(
        backward_kernel,
        out_shape=[shape((256, D), BF16), shape((256, D), BF16), shape((16, ATTN_W), F32), shape((16, FFN_W), F32)],
        in_specs=[in_hbm] * 5 + [in_vmem] + [in_hbm] * 4 + [in_vmem, in_hbm] + [in_vmem] * 4 + [in_hbm],
        out_specs=[in_vmem] * 4,
        scratch_shapes=[
            VMEM((2, 4, 4, 2, 16, QKV_W), BF16),
            VMEM((DPAD, OUT_W), BF16),
            VMEM(wide, BF16),
            VMEM(low, BF16),
            VMEM((2, 4, 4, 1, 256, 128), BF16),
            VMEM(low, F32),
            VMEM((2, OUT_W, 256), BF16),
            dma((7,)),
            VMEM((DEPTH, 3, DPAD, CHUNK), BF16),
            VMEM((FF_HERE // 128, 256, 128), BF16),
            VMEM(wide, BF16),
            VMEM(tall, BF16),
            VMEM(wide, F32),
            VMEM(wide, F32),
            VMEM(wide, BF16),
            VMEM(wide, BF16),
            VMEM(low, BF16),
            VMEM((2, 1, ROWS), F32),
            VMEM(low, F32),
            VMEM((HD, ROWS), BF16),
            VMEM((HD, ROWS), BF16),
            VMEM((2, 4, 4, 1, 256, 128), F32),
            VMEM((2, 4, 4, 1, 256, 128), BF16),
            VMEM((256, 128), F32),
            VMEM((QKV_W, 256), BF16),
            VMEM((2, 4, 4, 2, 16, FFN_W), BF16),
            VMEM((2, 4, 4, 2, 16, ATTN_W), BF16),
            VMEM((16, 128), F32),
            pltpu.SemaphoreType.REGULAR,
            dma((DEPTH, 3)),
            dma((6,)),
            dma((6,)),
            dma((6,)),
        ]
        + Scatter.scratch(2, 16, FFN_W)
        + Scatter.scratch(1, 256, 128)
        + Scatter.scratch(2, 16, ATTN_W),
        compiler_params=pltpu.CompilerParams(collective_id=1, has_side_effects=True, vmem_limit_bytes=VMEM_BYTES),
    )(*arrays)


def shards(
    inputs,
    positions,
    query_key_value_weight,
    query_key_value_bias,
    gain_attn,
    output_weight,
    gate_weight,
    up_weight,
    down_weight,
    gain_ffn,
    cotangent,
):
    me = lax.axis_index("seq") * 32 + lax.axis_index("ctx")
    select = (slot_columns()[:, None] == np.arange(D)[None, :]).astype(BF16)
    attn_row = (
        jnp.pad(query_key_value_weight[:, 0], ((0, 2), (0, QKV_W - GROUP)))
        + jnp.pad(gain_attn[:, None], ((0, 2), (GAIN_ONE, QKV_W - GAIN_ONE - 1)))
        + jnp.pad(gain_ffn[:, None], ((0, 2), (GAIN_TWO, QKV_W - GAIN_TWO - 1)))
    )
    attn_row = lax.dynamic_update_slice(attn_row, query_key_value_bias, (14, 9 * me))
    out_row = jnp.pad(output_weight[0].T, ((0, 2), (0, 64)))
    ffn_row = jnp.pad(jnp.concatenate([gate_weight, up_weight, down_weight.T], 1), ((0, 2), (0, 0)))
    cosine, sine = rope_tables(positions[0])
    row = lax.axis_index("ctx") * 256 + jnp.arange(128, dtype=jnp.int32)
    doc = jnp.stack([jnp.tile((row - positions[0, :128])[None], (1, 7)), jnp.full((1, ROWS), 128, jnp.int32)])
    attn_full, ffn_full, *kept = forward(
        attn_row, out_row, ffn_row, inputs[0], cotangent[0], select, cosine, sine, doc
    )
    output, grad_inputs, attn, ffn = backward(
        attn_full, ffn_full.reshape(DPAD, FFN_W), *kept, cosine, sine, doc, select
    )
    return (
        output[None],
        grad_inputs[None],
        attn[:14, None, :GROUP],
        lax.dynamic_slice(attn, (14, 8 * me), (1, 8)),
        lax.dynamic_slice(attn, (14, 512 + me), (1, 1)),
        attn[:14, GAIN_ONE],
        attn[:14, QKV_W : QKV_W + GROUP_Q].T[None],
        ffn[:14, :FF_HERE],
        ffn[:14, FF_HERE : 2 * FF_HERE],
        ffn[:14, 2 * FF_HERE :].T,
        attn[:14, GAIN_TWO],
    )


def solution(mesh):
    both = ("seq", "ctx")
    return jax.shard_map(
        shards,
        mesh=mesh,
        in_specs=(
            P("seq", "ctx", None),
            P("seq", "ctx"),
            P(both, "tp", None),
            P("tp", both),
            P(both),
            P("tp", None, both),
            P(both, "tp"),
            P(both, "tp"),
            P("tp", both),
            P(both),
            P("seq", "ctx", None),
        ),
        out_specs=(
            P("seq", "ctx", None),
            P("seq", "ctx", None),
            P(both, "tp", None),
            P("tp", both),
            P("tp", both),
            P(both),
            P("tp", None, both),
            P(both, "tp"),
            P(both, "tp"),
            P("tp", both),
            P(both),
        ),
        check_vma=False,
    )
```

```python
import jax
import jax.numpy as jnp
import numpy as np
from jax import lax
from jax.experimental import pallas as pl
from jax.experimental.pallas import tpu as pltpu
from jax.sharding import PartitionSpec as P

MESH_ID = pl.DeviceIdType.MESH
ANY = pl.ANY
VMEM = pltpu.VMEM


class Place:
    def __init__(self):
        self.seq = lax.axis_index("seq")
        ctx = lax.axis_index("ctx")
        self.ctx = ctx
        self.tp = lax.axis_index("tp")
        self.core = ctx % 2
        core = self.core
        y, z = ctx // 8, (ctx // 2) % 4
        self.a = y * (1 - core) + z * core
        self.b = z * (1 - core) + y * core
        self.stride_a = 8 - 6 * core
        self.stride_b = 2 + 6 * core
        self.a_next = self.peer(1, 0)
        self.a_prev = self.peer(3, 0)
        self.b_next = self.peer(0, 1)
        self.b_prev = self.peer(0, 3)
        self.other_core = {"ctx": ctx + 1 - 2 * core}
        self.other_seq = {"seq": 1 - self.seq}
        self.mirror = {"ctx": 31 - ctx}
        self.other_tp = {"tp": 1 - self.tp}
        self.mirror_tp = {"ctx": 31 - ctx, "tp": 1 - self.tp}

    def peer(self, da, db):
        a, b = (self.a + da) % 4, (self.b + db) % 4
        return {"ctx": a * self.stride_a + b * self.stride_b + self.core}


def greet(peers):
    barrier = pltpu.get_barrier_semaphore()
    for peer in peers:
        pl.semaphore_signal(barrier, inc=1, device_id=peer, device_id_type=MESH_ID)
    pl.semaphore_wait(barrier, len(peers))


def remote(src, dst, send, recv, index, peer):
    return pltpu.make_async_remote_copy(
        src_ref=src,
        dst_ref=dst,
        send_sem=send.at[index],
        recv_sem=recv.at[index],
        device_id=peer,
        device_id_type=MESH_ID,
    )


GATHER_SEMS = 15


class Gather:
    def __init__(self, place, own, full, send, recv, local):
        self.p, self.own, self.full = place, own, full
        self.send, self.recv, self.local = send, recv, local
        self.pair = full.shape[3] == 2
        self.started = []

    def go(self, src, dst, index, peer):
        copy = remote(src, dst, self.send, self.recv, index, peer)
        copy.start()
        self.started.append(copy)

    def got(self, ref, index):
        remote(ref, ref, self.send, self.recv, index, self.p.a_next).wait_recv()

    def half(self, b, a, which):
        ref = self.full.at[self.p.core, b, a]
        if self.pair:
            return ref.at[which]
        rows = self.full.shape[4] // 2
        return ref.at[0, pl.ds(which * rows, rows)]

    def begin(self):
        p = self.p
        slot = self.full.at[p.core, p.b, p.a, p.seq if self.pair else 0]
        self.mine = pltpu.make_async_copy(self.own, slot, self.local)
        self.mine.start()
        if self.pair:
            self.go(self.own, slot, 0, p.other_seq)

    def first(self):
        p = self.p
        self.mine.wait()
        if self.pair:
            self.got(self.full.at[p.core, p.b, p.a, 1 - p.seq], 0)
        block = self.full.at[p.core, p.b, p.a]
        self.go(block, block, 1, p.a_next)
        self.go(block, block, 2, p.a_prev)

    def second(self):
        p = self.p
        down, up = (p.a + 3) % 4, (p.a + 1) % 4
        self.got(self.full.at[p.core, p.b, down], 1)
        half = self.half(p.b, down, 0)
        self.go(half, half, 3, p.a_next)
        self.got(self.full.at[p.core, p.b, up], 2)
        half = self.half(p.b, up, 1)
        self.go(half, half, 4, p.a_prev)

    def third_near(self):
        p = self.p
        far = (p.a + 2) % 4
        self.got(self.half(p.b, far, 0), 3)
        self.got(self.half(p.b, far, 1), 4)
        row = self.full.at[p.core, p.b]
        self.go(row.at[pl.ds(0, 2)], row.at[pl.ds(0, 2)], 5, p.b_next)
        self.go(row.at[pl.ds(2, 2)], row.at[pl.ds(2, 2)], 6, p.b_prev)
        self.go(row, row, 9, p.other_core)

    def third_rest(self):
        p = self.p
        row = self.full.at[p.core, p.b]
        self.go(row.at[pl.ds(2, 2)], row.at[pl.ds(2, 2)], 13, p.b_next)
        self.go(row.at[pl.ds(0, 2)], row.at[pl.ds(0, 2)], 14, p.b_prev)

    def third(self):
        self.third_near()
        self.third_rest()

    def fourth_near(self):
        p = self.p
        half = self.full.at[p.core, (p.b + 3) % 4, pl.ds(0, 2)]
        self.got(half, 5)
        self.go(half, half, 7, p.b_next)
        half = self.full.at[p.core, (p.b + 1) % 4, pl.ds(2, 2)]
        self.got(half, 6)
        self.go(half, half, 8, p.b_prev)

    def fourth_rest(self):
        p = self.p
        down, up = (p.b + 3) % 4, (p.b + 1) % 4
        self.got(self.full.at[p.core, down, pl.ds(2, 2)], 13)
        row = self.full.at[p.core, down]
        self.go(row, row, 10, p.other_core)
        self.got(self.full.at[p.core, up, pl.ds(0, 2)], 14)
        row = self.full.at[p.core, up]
        self.go(row, row, 11, p.other_core)

    def fourth(self):
        self.fourth_near()
        self.fourth_rest()

    def fifth(self):
        p = self.p
        far = (p.b + 2) % 4
        self.got(self.full.at[p.core, far, pl.ds(0, 2)], 7)
        self.got(self.full.at[p.core, far, pl.ds(2, 2)], 8)
        block = self.full.at[p.core, far]
        self.go(block, block, 12, p.other_core)

    def finish(self):
        for step in (0, 3, 1, 2):
            self.from_core(step)
        self.sent()

    def from_core(self, step):
        p = self.p
        self.got(self.full.at[1 - p.core, (p.a + step) % 4], {0: 9, 3: 10, 1: 11, 2: 12}[step])

    def sent(self):
        for copy in self.started:
            copy.wait_send()

    def peers(self):
        p = self.p
        found = [p.a_next, p.a_prev, p.b_next, p.b_prev, p.other_core]
        return found + ([p.other_seq] if self.pair else [])


def add_into(target, extra, count):
    def body(k, carry):
        total = target[k].astype(jnp.float32) + extra[k].astype(jnp.float32)
        target[k] = total.astype(target.dtype)
        return carry

    lax.fori_loop(0, count, body, 0)


SCATTER_SEMS = 13


class Scatter:
    @staticmethod
    def scratch(seqs, rows, width):
        bf16 = jnp.bfloat16
        return [
            VMEM((4, 4, seqs, rows, width), bf16),
            VMEM((2, 2, seqs, rows, width), bf16),
            VMEM((1, rows, width), bf16),
            pltpu.SemaphoreType.DMA((SCATTER_SEMS,)),
            pltpu.SemaphoreType.DMA((SCATTER_SEMS,)),
            pltpu.SemaphoreType.REGULAR,
        ]

    def __init__(self, place, part, scratch):
        self.p, self.part = place, part
        self.sums, self.far_b, self.across, self.send, self.recv, self.free = scratch
        self.seqs, self.rows = part.shape[3], part.shape[4]
        spare = part.at[1 - place.core]
        self.near_b = [spare.at[side] for side in range(2)]
        self.near_a = [spare.at[2, side] for side in range(2)]
        self.far_a = [spare.at[2, 2 + side, pl.ds(0, 1)] for side in range(2)]
        if self.seqs == 1:
            self.far_a = [ref.at[:, pl.ds(0, self.rows // 2)] for ref in self.far_a]
        self.started = []

    go = Gather.go
    got = Gather.got

    def half(self, b, a, which):
        ref = self.sums.at[b, a]
        if self.seqs == 2:
            return ref.at[pl.ds(which, 1)]
        rows = self.rows // 2
        return ref.at[:, pl.ds(which * rows, rows)]

    def to_core(self, step):
        p = self.p
        slot = (p.a + step) % 4
        self.go(self.part.at[1 - p.core, slot], self.sums.at[slot], step, p.other_core)

    def begin(self):
        for step in (2, 1, 3, 0):
            self.to_core(step)

    def add_core(self, step):
        p = self.p
        slot = (p.b + step) % 4
        self.got(self.sums.at[slot], step)
        for a in range(4):
            add_into(self.sums.at[slot, a], self.part.at[p.core, slot, a], self.seqs)

    def first(self):
        p = self.p
        self.add_core(2)
        far = (p.b + 2) % 4
        self.go(self.sums.at[far, pl.ds(0, 2)], self.far_b.at[0], 4, p.b_next)
        self.go(self.sums.at[far, pl.ds(2, 2)], self.far_b.at[1], 5, p.b_prev)

    def second(self):
        p = self.p
        up, down = (p.b + 1) % 4, (p.b + 3) % 4
        for copy in self.started[:4]:
            copy.wait_send()
        self.started = self.started[4:]
        ring = (p.a_next, p.a_prev, p.b_next, p.b_prev)
        for peer in ring:
            pl.semaphore_signal(self.free, inc=1, device_id=peer, device_id_type=MESH_ID)
        self.add_core(1)
        self.add_core(3)
        pl.semaphore_wait(self.free, len(ring))
        self.got(self.far_b.at[0], 4)
        for a in range(2):
            add_into(self.sums.at[up, a], self.far_b.at[0, a], self.seqs)
        self.go(self.sums.at[up], self.near_b[0], 6, p.b_next)
        self.got(self.far_b.at[1], 5)
        for a in range(2):
            add_into(self.sums.at[down, a + 2], self.far_b.at[1, a], self.seqs)
        self.go(self.sums.at[down], self.near_b[1], 7, p.b_prev)

    def third(self):
        p = self.p
        self.add_core(0)
        for side in range(2):
            self.got(self.near_b[side], 6 + side)
            for a in range(4):
                add_into(self.sums.at[p.b, a], self.near_b[side].at[a], self.seqs)
        far = (p.a + 2) % 4
        self.go(self.half(p.b, far, 0), self.far_a[0], 8, p.a_next)
        self.go(self.half(p.b, far, 1), self.far_a[1], 9, p.a_prev)

    def fourth(self):
        p = self.p
        up, down = (p.a + 1) % 4, (p.a + 3) % 4
        self.got(self.far_a[0], 8)
        add_into(self.half(p.b, up, 0), self.far_a[0], 1)
        self.go(self.sums.at[p.b, up], self.near_a[0], 10, p.a_next)
        self.got(self.far_a[1], 9)
        add_into(self.half(p.b, down, 1), self.far_a[1], 1)
        self.go(self.sums.at[p.b, down], self.near_a[1], 11, p.a_prev)

    def fifth(self):
        p = self.p
        for side in range(2):
            self.got(self.near_a[side], 10 + side)
            add_into(self.sums.at[p.b, p.a], self.near_a[side], self.seqs)
        if self.seqs == 2:
            self.go(self.sums.at[p.b, p.a, pl.ds(1 - p.seq, 1)], self.across, 12, p.other_seq)

    def finish(self, out):
        p = self.p
        if self.seqs == 2:
            self.got(self.across, 12)
            out[...] = self.sums[p.b, p.a, p.seq].astype(jnp.float32) + self.across[0].astype(jnp.float32)
        else:
            out[...] = self.sums[p.b, p.a, 0].astype(jnp.float32)
        for copy in self.started:
            copy.wait_send()

    def peers(self):
        p = self.p
        found = [p.a_next, p.a_prev, p.b_next, p.b_prev, p.other_core]
        return found + ([p.other_seq] if self.seqs == 2 else [])


NEGATIVE = -1e30
HD = 64
ROWS = 896
TURNS = 33
F32, BF16 = jnp.float32, jnp.bfloat16


def mm(left, right):
    return jnp.dot(left, right, preferred_element_type=F32)


def mm_nt(left, right):
    return lax.dot_general(left, right, (((1,), (1,)), ((), ())), preferred_element_type=F32)


def block_of(core, b, a):
    y = a * (1 - core) + b * core
    z = b * (1 - core) + a * core
    return y * 8 + z * 2 + core


class Turn:
    def __init__(self, ctx, segment, slot):
        self.segment, self.slot = segment, slot
        self.block = block_of(*slot)
        count = (ctx + 1) * (1 - segment) + (32 - ctx) * segment
        self.first_row = (count - 1) * 256 + 128 * segment
        self.needed = self.block < count
        self.hidden = (self.block == 0) | (self.block == count - 1)

    def scores(self, scores, doc_ref, hidden, part=slice(0, ROWS)):
        if not hidden:
            return scores
        key = lax.broadcasted_iota(jnp.int32, scores.shape, 0) + self.block * 256
        row = (lax.broadcasted_iota(jnp.int32, scores.shape, 1) + part.start) % 128 + self.first_row
        visible = (key <= row) & (key >= doc_ref[self.segment, :, part])
        return jnp.where(visible, scores, NEGATIVE)


def run_row(ctx, core, b, step):
    def body(n, carry):
        turn = Turn(ctx, n // 4, (core, b, n % 4))
        pl.when(turn.needed & turn.hidden)(lambda: step(turn, True))
        pl.when(turn.needed & jnp.logical_not(turn.hidden))(lambda: step(turn, False))
        return carry

    lax.fori_loop(0, 8, body, 0)


def attend_step(turn, hidden, kv_ref, q_ref, doc_ref, m_ref, l_ref, acc_ref):
    core, b, a = turn.slot
    segment = turn.segment
    kv = kv_ref[core, b, a, 0]
    keys, values_t = kv[:, :HD], kv[:, HD:].T
    q, old_max, old_sum, old_acc = q_ref[segment], m_ref[segment], l_ref[segment], acc_ref[segment]
    parts = [slice(start, min(start + 256, ROWS)) for start in range(0, ROWS, 256)]
    products = [turn.scores(mm(keys, q[:, part]), doc_ref, hidden, part) for part in parts]
    results = []
    for part, scores in zip(parts, products):
        old = old_max[:, part]
        new = jnp.maximum(old, jnp.max(scores, 0, keepdims=True))
        probs = jnp.exp(scores - new)
        keep = jnp.exp(old - new)
        total = old_sum[:, part] * keep + jnp.sum(probs, 0, keepdims=True)
        results.append((new, total, old_acc[:, part] * keep + mm(values_t, probs.astype(BF16))))
    for part, (new, total, acc) in zip(parts, results):
        m_ref[segment, :, part] = new
        l_ref[segment, :, part] = total
        acc_ref[segment, :, part] = acc


def attend_back_step(turn, hidden, kv_ref, q_ref, doc_ref, do_ref, lse_ref, delta_ref, dq_ref, dkv_ref):
    core, b, a = turn.slot
    segment = turn.segment
    kv = kv_ref[core, b, a, 0]
    keys, values = kv[:, :HD], kv[:, HD:]
    q, do = q_ref[segment], do_ref[segment]
    scores = turn.scores(mm(keys, q), doc_ref, hidden)
    probs = jnp.exp(scores - lse_ref[segment])
    dscores = (probs * (mm(values, do) - delta_ref[segment])).astype(BF16)
    dq_ref[segment] += mm(keys.T, dscores)
    dkv_ref[core, b, a, 0] += jnp.concatenate([mm_nt(dscores, q), mm_nt(probs.astype(BF16), do)], 1)


D, DPAD, FF_HERE, GROUP, GROUP_Q = 896, 1024, 2432, 576, 448
QKV_W, OUT_W, FFN_W = 640, 512, 3 * 2432
ATTN_W = QKV_W + OUT_W
GAIN_ONE, GAIN_TWO = 576, 577
EPS_VALUE = 1e-06
THETA = 1000000.0
VMEM_BYTES = 62 << 20
CHUNK = 256
DEPTH = 3


def slot_columns():
    index = np.arange(64)
    seq, y, z, core = index // 32, (index // 8) % 4, (index // 2) % 4, index % 2
    a, b = np.where(core == 0, y, z), np.where(core == 0, z, y)
    slot = ((core * 4 + b) * 4 + a) * 2 + seq
    columns = np.full((64, 16), -1)
    columns[slot, :14] = index[:, None] * 14 + np.arange(14)
    return columns.reshape(-1)


def rope_tables(positions):
    exponents = jnp.arange(HD // 2, dtype=F32) * (2.0 / HD)
    freqs = THETA ** (-exponents)
    angles = freqs[:, None] * positions.astype(F32)[None, :]
    angles = jnp.concatenate([angles, angles], 0)
    return jnp.cos(angles), jnp.sin(angles)


def rotate(values, cosine, sine):
    turned = jnp.concatenate([-values[32:], values[:32]], 0)
    return values * cosine + turned * sine


def rotate_back(grads, cosine, sine):
    sined = grads * sine
    return grads * cosine + jnp.concatenate([sined[32:], -sined[:32]], 0)


def inv_rms(values):
    return lax.rsqrt(jnp.sum(values * values, 0, keepdims=True) * (1.0 / D) + EPS_VALUE)


def norm_back(values, inverse, scaled):
    mean = jnp.sum(scaled * values, 0, keepdims=True) * (1.0 / D)
    return inverse * scaled - values * inverse**3 * mean


def head(index):
    return pl.ds(index * HD, HD)


def lanes(index):
    return pl.ds(index * 128, 128)


def flat(ref, start, width):
    if not isinstance(start, int):
        start = pl.multiple_of(start, 128)
    return ref[:, :, :, :, :, pl.ds(start, width)].reshape(DPAD, width)


def unflat(value):
    return value.reshape(2, 4, 4, 2, 16, value.shape[-1])


def shape(dims, dtype):
    return jax.ShapeDtypeStruct(dims, dtype)


def fill_doc(doc, positions, p):
    row = lax.broadcasted_iota(jnp.int32, (1, 128), 1) + p.ctx * 256
    doc[0] = jnp.concatenate([row - positions[:, :128]] * 7, 1)
    doc[1] = jnp.full((1, ROWS), 128, jnp.int32)


def forward_kernel(
    attn_row,
    out_row,
    ffn_row,
    x_given,
    ct_given,
    select_given,
    cosine,
    sine,
    positions,
    attn_out,
    ffn_full,
    w_out,
    x_kept,
    ct_kept,
    tokens_kept,
    normed_kept,
    q_kept,
    kv_kept,
    attended,
    lse,
    att,
    middle,
    attn_full,
    x_out,
    ct_out,
    ct_tokens,
    normed_out,
    q_both,
    kv_full,
    keep_sems,
    doc,
    x_in,
    ct_in,
    select,
    given_sems,
    outs_mine,
    outs_full,
    q_send,
    kv_mine,
    att_send,
    att_far,
    m_ref,
    l_ref,
    acc_ref,
    pair_send,
    pair_recv,
    *sems,
):
    p = Place()
    pairs = ((select_given, select), (x_given, x_in), (ct_given, ct_in))
    given = [pltpu.make_async_copy(src, dst, given_sems.at[k]) for k, (src, dst) in enumerate(pairs)]
    for copy in given:
        copy.start()
    kept = []

    def keep(ref, out):
        copy = pltpu.make_async_copy(ref, out, keep_sems.at[len(kept)])
        copy.start()
        kept.append(copy)

    attn = Gather(p, attn_row, attn_full, *sems[0:3])
    ffn = Gather(p, ffn_row, ffn_full, *sems[3:6])
    keys = Gather(p, kv_mine, kv_full, *sems[6:9])
    outs = Gather(p, outs_mine, outs_full, *sems[9:12])
    greet(attn.peers() + [p.mirror, p.other_tp, p.mirror_tp])
    attn.begin()
    own_out = pl.ds(pl.multiple_of(p.tp * OUT_W, 128), OUT_W)
    out_copy = remote(out_row, outs_mine.at[:, own_out], pair_send, pair_recv, 0, p.other_tp)
    out_copy.start()
    ffn.begin()
    outs_mine[:, own_out] = out_row[...]
    fill_doc(doc, positions, p)
    for copy in given:
        copy.wait()
    x = mm_nt(select[...], x_in[...])
    x_out[...] = x
    keep(x_out, x_kept)
    attn.first()
    ct_out[...] = mm_nt(select[...], ct_in[...]).astype(BF16)
    keep(ct_out, ct_kept)
    attn.second()
    ct_tokens[...] = mm_nt(ct_in[...], select[...]).astype(BF16)
    keep(ct_tokens, tokens_kept)
    attn.third()
    ffn.first()
    m_ref[...] = jnp.full(m_ref.shape, NEGATIVE, F32)
    l_ref[...] = jnp.zeros(l_ref.shape, F32)
    acc_ref[...] = jnp.zeros(acc_ref.shape, F32)
    attn.fourth()
    attn.fifth()
    ffn.second()
    out_copy.wait()
    attn.finish()
    outs.begin()
    keep(attn_full, attn_out)

    gain = flat(attn_full, 512, 128)[:, GAIN_ONE - 512 : GAIN_ONE - 511].astype(F32)
    row = lax.broadcasted_iota(jnp.int32, (DPAD, 256), 0)
    x = x_out[...]
    normed = jnp.where(row % 16 == 14, 1.0, x * inv_rms(x) * gain)
    normed_out[...] = normed.astype(BF16)
    keep(normed_out, normed_kept)
    outs.first()
    mixed = mm(normed.T.astype(BF16), flat(attn_full, 0, QKV_W)).T
    outs.second()
    key = rotate(mixed[GROUP_Q : GROUP_Q + HD], cosine[...], sine[...])
    kv_mine[...] = jnp.concatenate([key, mixed[GROUP_Q + HD : GROUP]], 0).T.astype(BF16)
    keys.begin()
    keys.first()
    for h in range(7):
        query = rotate(mixed[64 * h : 64 * h + 64], cosine[...], sine[...]).astype(BF16).astype(F32) * 0.125
        q_both[0, :, lanes(h)] = query[:, :128].astype(BF16)
        q_send[:, lanes(h)] = query[:, 128:].astype(BF16)
    q_copy = remote(q_send, q_both.at[1], pair_send, pair_recv, 1, p.mirror)
    q_copy.start()
    keys.second()
    outs.third()
    keys.third()
    q_copy.wait()
    keep(q_both, q_kept)

    def step(turn, hidden):
        attend_step(turn, hidden, kv_full, q_both, doc, m_ref, l_ref, acc_ref)

    run_row(p.ctx, p.core, p.b, step)
    outs.fourth()
    keys.fourth()
    run_row(p.ctx, p.core, (p.b + 3) % 4, step)
    outs.fifth()
    keys.fifth()
    ffn.third_near()
    ffn.third_rest()
    run_row(p.ctx, p.core, (p.b + 1) % 4, step)
    run_row(p.ctx, p.core, (p.b + 2) % 4, step)
    for ahead in (0, 3, 1, 2):
        keys.from_core(ahead)
        if ahead == 1:
            ffn.fourth_near()
        run_row(p.ctx, 1 - p.core, (p.a + ahead) % 4, step)
    keys.sent()
    keep(kv_full, kv_kept)
    attended[...] = acc_ref[...] / l_ref[...]
    att_send[...] = attended[...].astype(BF16)
    att_copies = [
        remote(att_send.at[1], att_far.at[0], pair_send, pair_recv, 2, p.mirror),
        remote(att_send.at[0], att_far.at[1], pair_send, pair_recv, 3, p.other_tp),
        remote(att_send.at[1], att_far.at[2], pair_send, pair_recv, 4, p.mirror_tp),
    ]
    for copy in att_copies:
        copy.start()
    lse[...] = m_ref[...] + jnp.log(l_ref[...])
    outs.finish()
    ffn.fourth_rest()
    w_out[...] = flat(outs_full, p.tp * OUT_W, OUT_W)
    att[:, pl.ds(GROUP_Q, 64), :] = jnp.zeros((2, 64, 256), BF16)
    for h in range(7):
        att[p.tp, head(h), lanes(0)] = att_send[0, :, lanes(h)]
    for copy in att_copies:
        copy.wait()
    for h in range(7):
        att[p.tp, head(h), lanes(1)] = att_far[0, :, lanes(h)]
        att[1 - p.tp, head(h), lanes(0)] = att_far[1, :, lanes(h)]
        att[1 - p.tp, head(h), lanes(1)] = att_far[2, :, lanes(h)]
    middle[...] = x_out[...] + mm(flat(outs_full, 0, 2 * OUT_W), att[...].reshape(2 * OUT_W, 256))
    ffn.fifth()
    ffn.finish()
    for copy in kept:
        copy.wait()


def forward(*arrays):
    dma = pltpu.SemaphoreType.DMA
    gather_sems = [dma((GATHER_SEMS,)), dma((GATHER_SEMS,)), dma]
    in_vmem, in_hbm = pl.BlockSpec(memory_space=VMEM), pl.BlockSpec(memory_space=ANY)
    return pl.pallas_call(
        forward_kernel,
        out_shape=[
            shape((2, 4, 4, 2, 16, QKV_W), BF16),
            shape((2, 4, 4, 2, 16, FFN_W), BF16),
            shape((DPAD, OUT_W), BF16),
            shape((DPAD, 256), F32),
            shape((DPAD, 256), BF16),
            shape((256, DPAD), BF16),
            shape((DPAD, 256), BF16),
            shape((2, HD, ROWS), BF16),
            shape((2, 4, 4, 1, 256, 128), BF16),
            shape((2, HD, ROWS), F32),
            shape((2, 1, ROWS), F32),
            shape((2, OUT_W, 256), BF16),
            shape((DPAD, 256), F32),
        ],
        in_specs=[in_vmem, in_vmem] + [in_hbm] * 4 + [in_vmem] * 3,
        out_specs=[in_hbm, in_hbm, in_vmem] + [in_hbm] * 6 + [in_vmem] * 4,
        scratch_shapes=[
            VMEM((2, 4, 4, 2, 16, QKV_W), BF16),
            VMEM((DPAD, 256), F32),
            VMEM((DPAD, 256), BF16),
            VMEM((256, DPAD), BF16),
            VMEM((DPAD, 256), BF16),
            VMEM((2, HD, ROWS), BF16),
            VMEM((2, 4, 4, 1, 256, 128), BF16),
            dma((7,)),
            VMEM((2, 1, ROWS), jnp.int32),
            VMEM((256, D), BF16),
            VMEM((256, D), BF16),
            VMEM((DPAD, D), BF16),
            dma((3,)),
            VMEM((16, 2 * OUT_W), BF16),
            VMEM((2, 4, 4, 2, 16, 2 * OUT_W), BF16),
            VMEM((HD, ROWS), BF16),
            VMEM((256, 128), BF16),
            VMEM((2, HD, ROWS), BF16),
            VMEM((3, HD, ROWS), BF16),
            VMEM((2, 1, ROWS), F32),
            VMEM((2, 1, ROWS), F32),
            VMEM((2, HD, ROWS), F32),
            dma((5,)),
            dma((5,)),
        ]
        + gather_sems * 4,
        compiler_params=pltpu.CompilerParams(collective_id=0, has_side_effects=True, vmem_limit_bytes=VMEM_BYTES),
    )(*arrays)


def tile_of(index):
    return index // 16, (index // 4) % 4, index % 4, 0


def ffn_chunk(weights, slot, width, tile, tokens, ct_tokens, gate_kept, up_kept, hidden_kept, out_sum, grad_sum):
    w_gate, w_up, w_down = (weights[slot, k, :, pl.ds(0, width)] for k in range(3))
    gate, up = mm(tokens[...], w_gate), mm(tokens[...], w_up)
    grad_hidden = mm(ct_tokens[...], w_down)
    sigmoid = jax.nn.sigmoid(gate)
    silu = gate * sigmoid
    hidden = (silu * up).astype(BF16)
    grad_up = (grad_hidden * silu).astype(BF16)
    grad_gate = (grad_hidden * up * sigmoid * (1.0 + gate * (1.0 - sigmoid))).astype(BF16)
    grad_sum[...] += mm_nt(w_gate, grad_gate) + mm_nt(w_up, grad_up)
    out_sum[...] += mm_nt(w_down, hidden)
    for k in range(width // 128):
        part = slice(128 * k, 128 * k + 128)
        gate_kept[tile_of(tile + k)] = grad_gate[:, part]
        up_kept[tile_of(tile + k)] = grad_up[:, part].astype(F32)
        hidden_kept[tile + k] = hidden[:, part]


def ffn_weight_grads(tile, tiles, normed, ct, gate_kept, up_kept, hidden_kept, part):
    places = [tile_of(tile + k) for k in range(tiles)]
    pairs = (
        (normed, [gate_kept[place] for place in places]),
        (normed, [up_kept[place].astype(BF16) for place in places]),
        (ct, [hidden_kept[tile + k] for k in range(tiles)]),
    )
    for k, (left, right) in enumerate(pairs):
        start = k * FF_HERE + tile * 128
        if not isinstance(start, int):
            start = pl.multiple_of(start, 128)
        product = mm(left[...], jnp.concatenate(right, 1) if tiles > 1 else right[0])
        part[:, :, :, :, :, pl.ds(start, tiles * 128)] = unflat(product.astype(BF16))


def backward_kernel(
    attn_kept,
    ffn_full,
    w_out_kept,
    x_kept,
    ct_kept,
    ct_tokens,
    normed_kept,
    q_kept,
    kv_kept,
    attended_kept,
    lse,
    att_kept,
    middle,
    cosine,
    sine,
    positions,
    select,
    output,
    grad_inputs,
    attn_mine,
    ffn_mine,
    attn_full,
    w_out,
    ct,
    q_both,
    kv_full,
    attended,
    att,
    late_sems,
    doc,
    weights,
    hidden_kept,
    normed_ffn,
    tokens,
    out_sum,
    grad_sum,
    out_far,
    grad_far,
    do_both,
    delta,
    dq,
    dq_send,
    dq_far,
    dkv,
    kv_part,
    kv_mine,
    grad_mixed,
    ffn_part,
    attn_part,
    gains_far,
    grad_free,
    weight_sems,
    kept_sems,
    pair_send,
    pair_recv,
    *scratch,
):
    p = Place()
    out_send, grad_send, do_send = weights.at[2, 0], weights.at[2, 1], dq_send
    ffn = Scatter(p, ffn_part, scratch[0:6])
    keys = Scatter(p, kv_part, scratch[6:12])
    attn = Scatter(p, attn_part, scratch[12:18])

    def load(index, slot, width):
        start = index * CHUNK
        copies = []
        for k in range(3):
            place = pl.ds(pl.multiple_of(k * FF_HERE + start, 128), width)
            copies.append(
                pltpu.make_async_copy(
                    ffn_full.at[:, place], weights.at[slot, k, :, pl.ds(0, width)], weight_sems.at[slot, k]
                )
            )
        return copies

    pairs = (
        (attn_kept, attn_full),
        (ct_kept, ct),
        (w_out_kept, w_out),
        (q_kept, q_both),
        (kv_kept, kv_full),
        (attended_kept, attended),
        (att_kept, att),
    )
    late = [pltpu.make_async_copy(src, dst, late_sems.at[k]) for k, (src, dst) in enumerate(pairs)]
    late[0].start()
    for index in range(DEPTH - 1):
        for copy in load(index, index, CHUNK):
            copy.start()
    for copy in late[1:]:
        copy.start()
    greet(ffn.peers() + [p.mirror, p.other_tp])
    ffn_kept = (kv_part, dkv, hidden_kept)
    late[0].wait()
    fill_doc(doc, positions, p)
    gain_two = flat(attn_full, 512, 128)[:, GAIN_TWO - 512 : GAIN_TWO - 511].astype(F32)
    mid = middle[...]
    inverse = inv_rms(mid)
    scaled = mid * inverse * gain_two
    normed_ffn[...] = scaled.astype(BF16)
    tokens[...] = scaled.T.astype(BF16)
    out_sum[...] = jnp.zeros(out_sum.shape, F32)
    grad_sum[...] = jnp.zeros(grad_sum.shape, F32)
    chunks, tail, tiles = FF_HERE // CHUNK, FF_HERE % CHUNK, CHUNK // 128

    def chunk_body(index, carry):
        slot, ahead = index % DEPTH, index + DEPTH - 1
        for copy in load(index, slot, CHUNK):
            copy.wait()

        @pl.when(ahead < chunks)
        def _():
            for copy in load(ahead, ahead % DEPTH, CHUNK):
                copy.start()

        @pl.when(ahead == chunks)
        def _():
            for copy in load(chunks, chunks % DEPTH, tail):
                copy.start()

        ffn_chunk(weights, slot, CHUNK, index * tiles, tokens, ct_tokens, *ffn_kept, out_sum, grad_sum)
        return carry

    lax.fori_loop(0, chunks, chunk_body, 0)
    for copy in load(chunks, chunks % DEPTH, tail):
        copy.wait()
    ffn_chunk(weights, chunks % DEPTH, tail, chunks * tiles, tokens, ct_tokens, *ffn_kept, out_sum, grad_sum)
    grad_send[...] = grad_sum[...].astype(BF16)
    grad_copy = remote(grad_send, grad_far, pair_send, pair_recv, 0, p.other_tp)
    grad_copy.start()

    for copy in late[1:]:
        copy.wait()

    def grads_body(index, carry):
        ffn_weight_grads(index * tiles, tiles, normed_ffn, ct, *ffn_kept, ffn_part)
        return carry

    lax.fori_loop(0, chunks, grads_body, 0)
    ffn_weight_grads(chunks * tiles, tail // 128, normed_ffn, ct, *ffn_kept, ffn_part)
    ffn.begin()
    out_send[...] = out_sum[...].astype(BF16)
    x, normed, grad_middle = out_sum, normed_ffn, grad_sum
    kept = [
        pltpu.make_async_copy(x_kept, x, kept_sems.at[0]),
        pltpu.make_async_copy(normed_kept, normed, kept_sems.at[1]),
    ]
    columns = [pl.ds(start, min(CHUNK, D - start)) for start in range(0, D, CHUNK)]
    picks = [weights.at[k // 3, k % 3, :, pl.ds(0, column.size)] for k, column in enumerate(columns)]
    for k, column in enumerate(columns):
        kept.append(pltpu.make_async_copy(select.at[:, column], picks[k], kept_sems.at[2 + k]))

    def put_features(out, value):
        value = value.T.astype(BF16)
        for column, pick in zip(columns, picks):
            out[:, column] = mm(value, pick[...]).astype(BF16)

    for copy in kept:
        copy.start()
    dq[...] = jnp.zeros(dq.shape, F32)
    dkv[...] = jnp.zeros(dkv.shape, F32)
    grad_copy.wait()
    out_copy = remote(out_send, out_far, pair_send, pair_recv, 1, p.other_tp)
    out_copy.start()
    mid = middle[...]
    inverse = inv_rms(mid)
    grad_normed = grad_send[...].astype(F32) + grad_far[...].astype(F32)
    pl.semaphore_signal(grad_free, inc=1, device_id=p.other_tp, device_id_type=MESH_ID)
    gain_two_grad = jnp.sum(grad_normed * mid * inverse, 1, keepdims=True)
    grad_mid = ct[...].astype(F32) + norm_back(mid, inverse, grad_normed * gain_two)
    grad_middle[...] = grad_mid
    grad_att = mm(grad_mid.T.astype(BF16), w_out[...]).T
    for h in range(7):
        do_both[0, :, lanes(h)] = grad_att[64 * h : 64 * h + 64, :128].astype(BF16)
        do_send[:, lanes(h)] = grad_att[64 * h : 64 * h + 64, 128:].astype(BF16)
    do_copy = remote(do_send, do_both.at[1], pair_send, pair_recv, 2, p.mirror)
    do_copy.start()
    ffn.first()
    do_copy.wait()
    delta[...] = jnp.sum(do_both[...].astype(F32) * attended[...], 1, keepdims=True)

    def step(turn, hidden):
        attend_back_step(turn, hidden, kv_full, q_both, doc, do_both, lse, delta, dq, dkv)

    def far_row(ahead):
        slot = (p.a + ahead) % 4
        run_row(p.ctx, 1 - p.core, slot, step)
        kv_part[1 - p.core, slot] = dkv[1 - p.core, slot].astype(BF16)
        keys.to_core(ahead)

    def own_row(ahead):
        slot = (p.b + ahead) % 4
        run_row(p.ctx, p.core, slot, step)
        kv_part[p.core, slot] = dkv[p.core, slot].astype(BF16)

    far_row(2)
    far_row(1)
    ffn.second()
    far_row(3)
    far_row(0)
    own_row(2)
    keys.first()
    own_row(1)
    own_row(3)
    keys.second()
    own_row(0)
    dq_send[...] = dq[1].astype(BF16)
    dq_copy = remote(dq_send, dq_far, pair_send, pair_recv, 3, p.mirror)
    dq_copy.start()
    out_copy.wait()
    for copy in kept:
        copy.wait()
    put_features(output, middle[...] + (out_send[...].astype(F32) + out_far[...].astype(F32)))
    keys.third()
    ffn.third()
    attn_part[:, :, :, :, :, pl.ds(QKV_W, OUT_W)] = unflat(
        mm_nt(grad_middle[...].astype(BF16), att[p.tp]).astype(BF16)
    )
    keys.fourth()
    keys.fifth()
    ffn.fourth()
    keys.finish(kv_mine)
    dq_copy.wait()
    grad_mixed[pl.ds(GROUP, QKV_W - GROUP), :] = jnp.zeros((QKV_W - GROUP, 256), BF16)
    for h in range(7):
        far = dq_far[:, lanes(h)].astype(F32)
        near = dq[0, :, lanes(h)]
        grad_query = jnp.concatenate([near, far], 1) * 0.125
        grad_mixed[head(h), :] = rotate_back(grad_query, cosine[...], sine[...]).astype(BF16)
    grad_kv = kv_mine[...].T
    grad_mixed[head(7), :] = rotate_back(grad_kv[:HD], cosine[...], sine[...]).astype(BF16)
    grad_mixed[head(8), :] = grad_kv[HD:].astype(BF16)
    w_qkv = flat(attn_full, 0, QKV_W)
    grad_normed = mm(w_qkv, grad_mixed[...])
    grad_send[...] = grad_normed.astype(BF16)
    pl.semaphore_wait(grad_free, 1)
    grad_copy = remote(grad_send, grad_far, pair_send, pair_recv, 4, p.other_tp)
    grad_copy.start()
    value = x[...]
    inverse = inv_rms(value)
    gain_one_grad = jnp.sum(grad_normed * value * inverse, 1, keepdims=True)
    grad_qkv = mm_nt(normed[...], grad_mixed[...])
    lane = lax.broadcasted_iota(jnp.int32, grad_qkv.shape, 1)
    grad_qkv = jnp.where(lane == GAIN_ONE, gain_one_grad, jnp.where(lane == GAIN_TWO, gain_two_grad, grad_qkv))
    attn_part[:, :, :, :, :, pl.ds(0, QKV_W)] = unflat(grad_qkv.astype(BF16))
    attn.begin()
    attn.first()
    ffn.fifth()
    attn.second()
    grad_copy.wait()
    gain_one = flat(attn_full, 512, 128)[:, GAIN_ONE - 512 : GAIN_ONE - 511].astype(F32)
    scaled = (grad_send[...].astype(F32) + grad_far[...].astype(F32)) * gain_one
    put_features(grad_inputs, grad_middle[...] + norm_back(value, inverse, scaled))
    attn.third()
    attn.fourth()
    attn.fifth()
    attn.finish(attn_mine)
    gains_copy = remote(attn_mine.at[:, pl.ds(512, 128)], gains_far, pair_send, pair_recv, 5, p.other_tp)
    gains_copy.start()
    ffn.finish(ffn_mine)
    gains_copy.wait()
    mine = attn_mine[:, pl.ds(512, 128)]
    lane = lax.broadcasted_iota(jnp.int32, (16, 128), 1) + 512
    attn_mine[:, pl.ds(512, 128)] = mine + jnp.where(lane == GAIN_ONE, gains_far[...], 0.0)


def backward(*arrays):
    dma = pltpu.SemaphoreType.DMA
    in_vmem, in_hbm = pl.BlockSpec(memory_space=VMEM), pl.BlockSpec(memory_space=ANY)
    wide, tall, low = (DPAD, 256), (256, DPAD), (2, HD, ROWS)
    return pl.pallas_call(
        backward_kernel,
        out_shape=[shape((256, D), BF16), shape((256, D), BF16), shape((16, ATTN_W), F32), shape((16, FFN_W), F32)],
        in_specs=[in_hbm] * 5 + [in_vmem] + [in_hbm] * 4 + [in_vmem, in_hbm] + [in_vmem] * 4 + [in_hbm],
        out_specs=[in_vmem] * 4,
        scratch_shapes=[
            VMEM((2, 4, 4, 2, 16, QKV_W), BF16),
            VMEM((DPAD, OUT_W), BF16),
            VMEM(wide, BF16),
            VMEM(low, BF16),
            VMEM((2, 4, 4, 1, 256, 128), BF16),
            VMEM(low, F32),
            VMEM((2, OUT_W, 256), BF16),
            dma((7,)),
            VMEM((2, 1, ROWS), jnp.int32),
            VMEM((DEPTH, 3, DPAD, CHUNK), BF16),
            VMEM((FF_HERE // 128, 256, 128), BF16),
            VMEM(wide, BF16),
            VMEM(tall, BF16),
            VMEM(wide, F32),
            VMEM(wide, F32),
            VMEM(wide, BF16),
            VMEM(wide, BF16),
            VMEM(low, BF16),
            VMEM((2, 1, ROWS), F32),
            VMEM(low, F32),
            VMEM((HD, ROWS), BF16),
            VMEM((HD, ROWS), BF16),
            VMEM((2, 4, 4, 1, 256, 128), F32),
            VMEM((2, 4, 4, 1, 256, 128), BF16),
            VMEM((256, 128), F32),
            VMEM((QKV_W, 256), BF16),
            VMEM((2, 4, 4, 2, 16, FFN_W), BF16),
            VMEM((2, 4, 4, 2, 16, ATTN_W), BF16),
            VMEM((16, 128), F32),
            pltpu.SemaphoreType.REGULAR,
            dma((DEPTH, 3)),
            dma((6,)),
            dma((6,)),
            dma((6,)),
        ]
        + Scatter.scratch(2, 16, FFN_W)
        + Scatter.scratch(1, 256, 128)
        + Scatter.scratch(2, 16, ATTN_W),
        compiler_params=pltpu.CompilerParams(collective_id=1, has_side_effects=True, vmem_limit_bytes=VMEM_BYTES),
    )(*arrays)


def shards(
    inputs,
    positions,
    query_key_value_weight,
    query_key_value_bias,
    gain_attn,
    output_weight,
    gate_weight,
    up_weight,
    down_weight,
    gain_ffn,
    cotangent,
):
    me = lax.axis_index("seq") * 32 + lax.axis_index("ctx")
    select = (slot_columns()[:, None] == np.arange(D)[None, :]).astype(BF16)
    attn_row = (
        jnp.pad(query_key_value_weight[:, 0], ((0, 2), (0, QKV_W - GROUP)))
        + jnp.pad(gain_attn[:, None], ((0, 2), (GAIN_ONE, QKV_W - GAIN_ONE - 1)))
        + jnp.pad(gain_ffn[:, None], ((0, 2), (GAIN_TWO, QKV_W - GAIN_TWO - 1)))
    )
    attn_row = lax.dynamic_update_slice(attn_row, query_key_value_bias, (14, 9 * me))
    out_row = jnp.pad(output_weight[0].T, ((0, 2), (0, 64)))
    ffn_row = jnp.pad(jnp.concatenate([gate_weight, up_weight, down_weight.T], 1), ((0, 2), (0, 0)))
    cosine, sine = rope_tables(positions[0])
    attn_full, ffn_full, *kept = forward(
        attn_row, out_row, ffn_row, inputs[0], cotangent[0], select, cosine, sine, positions
    )
    output, grad_inputs, attn, ffn = backward(
        attn_full, ffn_full.reshape(DPAD, FFN_W), *kept, cosine, sine, positions, select
    )
    return (
        output[None],
        grad_inputs[None],
        attn[:14, None, :GROUP],
        lax.dynamic_slice(attn, (14, 8 * me), (1, 8)),
        lax.dynamic_slice(attn, (14, 512 + me), (1, 1)),
        attn[:14, GAIN_ONE],
        attn[:14, QKV_W : QKV_W + GROUP_Q].T[None],
        ffn[:14, :FF_HERE],
        ffn[:14, FF_HERE : 2 * FF_HERE],
        ffn[:14, 2 * FF_HERE :].T,
        attn[:14, GAIN_TWO],
    )


def solution(mesh):
    both = ("seq", "ctx")
    return jax.shard_map(
        shards,
        mesh=mesh,
        in_specs=(
            P("seq", "ctx", None),
            P("seq", "ctx"),
            P(both, "tp", None),
            P("tp", both),
            P(both),
            P("tp", None, both),
            P(both, "tp"),
            P(both, "tp"),
            P("tp", both),
            P(both),
            P("seq", "ctx", None),
        ),
        out_specs=(
            P("seq", "ctx", None),
            P("seq", "ctx", None),
            P(both, "tp", None),
            P("tp", both),
            P("tp", both),
            P(both),
            P("tp", None, both),
            P(both, "tp"),
            P(both, "tp"),
            P("tp", both),
            P(both),
        ),
        check_vma=False,
    )
```
